32 devices in a mesh: dp: 4 (over x, core), mp: 8 (over z, y).
Axes of the slice: x: 2, y: 2, z: 4, core: 2. Of those that a mesh axis runs over, the one named last changes fastest.
Arguments:
- fast_in: bfloat16 [8, 64, 196, 128], P('dp', 'mp'), may hold values from -6 to 6
- slow_in: bfloat16 [8, 16, 196, 1024], P('dp', 'mp'), may hold values from -6 to 6
- clip_len: int32 [8, 1], replicated, may hold values from 4 to 16, as said below
- w_fast_a: bfloat16 [3, 128, 32], replicated, may hold values from -0.3125 to 0.3125
- w_fast_b: bfloat16 [9, 32, 32], replicated, may hold values from -0.375 to 0.375
- w_fast_c: bfloat16 [32, 128], replicated, may hold values from -1 to 1
- w_lateral: bfloat16 [5, 128, 256], replicated, may hold values from -0.25 to 0.25
- w_slow_a: bfloat16 [3, 1280, 256], P(None, None, 'mp'), may hold values from -0.09375 to 0.09375
- w_slow_b: bfloat16 [9, 256, 256], P(None, None, 'mp'), may hold values from -0.125 to 0.125
- w_slow_c: bfloat16 [256, 1024], P(None, 'mp'), may hold values from -0.375 to 0.375
- w_short: bfloat16 [1280, 1024], P(None, 'mp'), may hold values from -0.15625 to 0.15625
- norm_fast_a: float32 [2, 32], replicated, may hold values from 0.25 to 1.75
- norm_fast_b: float32 [2, 32], replicated, may hold values from 0.25 to 1.75
- norm_fast_c: float32 [2, 128], replicated, may hold values from 0.25 to 1.75
- norm_slow_a: float32 [2, 256], replicated, may hold values from 0.25 to 1.75
- norm_slow_b: float32 [2, 256], replicated, may hold values from 0.25 to 1.75
- norm_slow_c: float32 [2, 1024], replicated, may hold values from 0.25 to 1.75
- norm_short: float32 [2, 1024], replicated, may hold values from 0.25 to 1.75
- cot_fast: bfloat16 [8, 64, 196, 128], P('dp', 'mp'), may hold values from -6 to 6
- cot_slow: bfloat16 [8, 16, 196, 1024], P('dp', 'mp'), may hold values from -6 to 6
Outputs:
- fast_out: bfloat16 [8, 64, 196, 128], P('dp', 'mp')
- slow_out: bfloat16 [8, 16, 196, 1024], P('dp', 'mp')
- grad_fast_in: bfloat16 [8, 64, 196, 128], P('dp', 'mp')
- grad_slow_in: bfloat16 [8, 16, 196, 1024], P('dp', 'mp')
- grad_w_fast_a: float32 [3, 128, 32], replicated
- grad_w_fast_b: float32 [9, 32, 32], replicated
- grad_w_fast_c: float32 [32, 128], replicated
- grad_w_lateral: float32 [5, 128, 256], replicated
- grad_w_slow_a: float32 [3, 1280, 256], P(None, None, 'mp')
- grad_w_slow_b: float32 [9, 256, 256], P(None, None, 'mp')
- grad_w_slow_c: float32 [256, 1024], P(None, 'mp')
- grad_w_short: float32 [1280, 1024], P(None, 'mp')
- grad_norm_fast_a: float32 [2, 32], replicated
- grad_norm_fast_b: float32 [2, 32], replicated
- grad_norm_fast_c: float32 [2, 128], replicated
- grad_norm_slow_a: float32 [2, 256], replicated
- grad_norm_slow_b: float32 [2, 256], replicated
- grad_norm_slow_c: float32 [2, 1024], replicated
- grad_norm_short: float32 [2, 1024], replicated
The draws below stay inside these ranges and needn't reach their ends.
Inputs may be any that keep to these rules, and one draw needn't show every extreme that they name: `clip_len`: in every aligned block of 2 rows one row has all 16 slow frames valid.
All inputs are finite; a program needn't handle non-finite values.
Results may differ from the reference program's by a relative error of at most 0.019.
Values may be sent and summed in bfloat16 or wider, within the bound.
No kernel may reach another device: no remote copies, remote signals or barrier semaphores. Data moves between devices by JAX's collectives and lax.ppermute only.
A program may use at most 192 MiB of HBM per device.

```python
import jax
import jax.numpy as jnp
from jax import lax

CF = 128
CI = 32
CL = 256
CS = 1024
CM = 256
CO = 1024
H = 14
W = 14
ALPHA = 4
S = 2
PIX = 196
FRAMES = 64
TS = 16
TF = 64
CU = 1280
ROWS = 8
SFRAMES = 16
NC = 1


def draw_clip_len(key, part):
    key = jax.random.fold_in(key, 11)
    lengths = jax.random.randint(jax.random.fold_in(key, 1), (ROWS, NC), 4, TS + 1)
    chosen = jax.random.randint(jax.random.fold_in(key, 2), (ROWS // S, 1), 0, S)
    place = jnp.arange(ROWS).reshape(ROWS // S, S) == chosen
    full_row = place.reshape(ROWS, 1)
    return jnp.where(full_row, TS, lengths).astype(jnp.int32)


def block_scale(key, shape, shards, smallest, largest):
    gain = 1.0
    for dim, shards_of in shards:
        steps = jax.random.uniform(jax.random.fold_in(jax.random.fold_in(key, 6), dim), (shards_of,), jnp.float32, smallest / len(shards), largest / len(shards))
        gain = gain * jnp.repeat(jnp.exp(steps), shape[dim] // shards_of).reshape((-1,) + (1,) * (len(shape) - 1 - dim))
    return gain


def gaussian(own_key, dims, deviation, most, cuts=(), dtype=jnp.bfloat16):
    gain = block_scale(own_key, dims, cuts, -0.22, 0.18) if cuts else 1.0
    array = jax.random.normal(own_key, dims, jnp.float32) * deviation * gain
    return jnp.minimum(jnp.maximum(array, -most), most).astype(dtype)


def setup_inputs(seed: int = 0) -> dict:
    key_list = jax.random.split(jax.random.key(seed), 21)
    return {
        "fast_in": gaussian(key_list[0], (ROWS, FRAMES, PIX, CF), 1.0, 6.0, ((0, 4), (1, 8))),
        "slow_in": gaussian(key_list[1], (ROWS, SFRAMES, PIX, CS), 1.0, 6.0, ((0, 4), (1, 8))),
        "clip_len": draw_clip_len(jax.random.fold_in(key_list[20], 71), 0),
        "w_fast_a": gaussian(key_list[3], (3, CF, CI), (3 * CF) ** -0.5, 0.3125),
        "w_fast_b": gaussian(key_list[4], (9, CI, CI), (9 * CI) ** -0.5, 0.375),
        "w_fast_c": gaussian(key_list[5], (CI, CF), CI ** -0.5, 1.0),
        "w_lateral": gaussian(key_list[6], (5, CF, CL), (5 * CF) ** -0.5, 0.25),
        "w_slow_a": gaussian(key_list[7], (3, CU, CM), (3 * CU) ** -0.5, 0.09375, ((2, 8),)),
        "w_slow_b": gaussian(key_list[8], (9, CM, CM), (9 * CM) ** -0.5, 0.125, ((2, 8),)),
        "w_slow_c": gaussian(key_list[9], (CM, CO), CM ** -0.5, 0.375, ((1, 8),)),
        "w_short": gaussian(key_list[10], (CU, CO), CU ** -0.5, 0.15625, ((1, 8),)),
        "norm_fast_a": jnp.clip(1.0 + 0.15 * jax.random.normal(key_list[11], (2, CI), jnp.float32), 0.25, 1.75),
        "norm_fast_b": jnp.clip(1.0 + 0.15 * jax.random.normal(key_list[12], (2, CI), jnp.float32), 0.25, 1.75),
        "norm_fast_c": jnp.clip(1.0 + 0.15 * jax.random.normal(key_list[13], (2, CF), jnp.float32), 0.25, 1.75),
        "norm_slow_a": jnp.clip(1.0 + 0.15 * jax.random.normal(key_list[14], (2, CM), jnp.float32), 0.25, 1.75),
        "norm_slow_b": jnp.clip(1.0 + 0.15 * jax.random.normal(key_list[15], (2, CM), jnp.float32), 0.25, 1.75),
        "norm_slow_c": jnp.clip(1.0 + 0.15 * jax.random.normal(key_list[16], (2, CO), jnp.float32), 0.25, 1.75),
        "norm_short": jnp.clip(1.0 + 0.15 * jax.random.normal(key_list[17], (2, CO), jnp.float32), 0.25, 1.75),
        "cot_fast": gaussian(key_list[18], (ROWS, FRAMES, PIX, CF), 1.0, 6.0, ((0, 4), (1, 8))),
        "cot_slow": gaussian(key_list[19], (ROWS, SFRAMES, PIX, CO), 1.0, 6.0, ((0, 4), (1, 8))),
    }


NORM_EPSILON = 1e-05

@jax.custom_vjp
def low(v):
    return lax.optimization_barrier(v.astype(jnp.bfloat16)).astype(jnp.float32)

@jax.custom_vjp
def low_back(v):
    return v

def low_keep(v):
    return (low(v), None)

def low_pass(kept, grad):
    return (grad,)

def back_keep(v):
    return (v, None)

def back_low(kept, grad):
    return (low(grad),)
low.defvjp(low_keep, low_pass)
low_back.defvjp(back_keep, back_low)

def clip_conv(inputs, kernel_weights, stride_time, padding):
    return lax.conv_general_dilated(inputs, kernel_weights, (stride_time, 1, 1), padding, dimension_numbers=('NDHWC', 'DHWIO', 'NDHWC'), precision=lax.Precision.HIGHEST)

def into_clips(values, frames_clip):
    return values.reshape(-1, frames_clip, H, W, values.shape[-1])

def from_clips(values, total_rows):
    return values.reshape(total_rows, -1, H * W, values.shape[-1])

def normalize(values, frame_mask, total_count, affine):
    spread_mask = frame_mask[:, :, None, None]
    average = lax.optimization_barrier(jnp.sum(spread_mask * values, axis=(0, 1, 2))) / total_count
    second = lax.optimization_barrier(jnp.sum(spread_mask * values * values, axis=(0, 1, 2))) / total_count - average * average
    standard = (values - average) * lax.rsqrt(second + NORM_EPSILON)
    return affine[0] * standard + affine[1]

def reference(fast_in, slow_in, clip_len, w_fast_a, w_fast_b, w_fast_c, w_lateral, w_slow_a, w_slow_b, w_slow_c, w_short, norm_fast_a, norm_fast_b, norm_fast_c, norm_slow_a, norm_slow_b, norm_slow_c, norm_short, cot_fast, cot_slow):
    total_rows = fast_in.shape[0]
    fast_mask = (jnp.arange(FRAMES)[None, :] % TF < ALPHA * jnp.repeat(clip_len, TF, axis=1)).astype(jnp.float32)
    slow_mask = (jnp.arange(SFRAMES)[None, :] % TS < jnp.repeat(clip_len, TS, axis=1)).astype(jnp.float32)
    fast_count = jnp.sum(clip_len).astype(jnp.float32) * (ALPHA * H * W)
    slow_count = jnp.sum(clip_len).astype(jnp.float32) * (H * W)
    fast_keep = fast_mask[:, :, None, None]
    slow_keep = slow_mask[:, :, None, None]
    time_pad = ((1, 1), (0, 0), (0, 0))
    space_pad = ((0, 0), (1, 1), (1, 1))

    def forward(leaves):
        fast_x, slow_x, weight_fa, weight_fb, weight_fc, weight_lat, weight_sa, weight_sb, weight_sc, weight_sh, affine_fa, affine_fb, affine_fc, affine_sa, affine_sb, affine_sc, affine_sh = leaves
        fast_masked = fast_x * fast_keep
        fast_clips = into_clips(fast_masked, TF)
        fast_first = low_back(from_clips(clip_conv(fast_clips, weight_fa.reshape(3, 1, 1, CF, CI), 1, time_pad), total_rows))
        hidden_a = low(fast_keep * jax.nn.silu(normalize(fast_first, fast_mask, fast_count, affine_fa)))
        fast_second = low_back(from_clips(clip_conv(into_clips(hidden_a, TF), weight_fb.reshape(1, 3, 3, CI, CI), 1, space_pad), total_rows))
        hidden_b = low(fast_keep * jax.nn.silu(normalize(fast_second, fast_mask, fast_count, affine_fb)))
        fast_third = low_back(jnp.dot(hidden_b, weight_fc, precision=lax.Precision.HIGHEST))
        fast_result = fast_keep * jax.nn.silu(normalize(fast_third, fast_mask, fast_count, affine_fc) + fast_masked)
        lateral = low(low_back(from_clips(clip_conv(fast_clips, weight_lat.reshape(5, 1, 1, CF, CL), ALPHA, ((2, 2), (0, 0), (0, 0))), total_rows)))
        joined = slow_keep * jnp.concatenate([slow_x, lateral], -1)
        slow_first = low_back(from_clips(clip_conv(into_clips(joined, TS), weight_sa.reshape(3, 1, 1, CU, CM), 1, time_pad), total_rows))
        hidden_c = low(slow_keep * jax.nn.silu(normalize(slow_first, slow_mask, slow_count, affine_sa)))
        slow_second = low_back(from_clips(clip_conv(into_clips(hidden_c, TS), weight_sb.reshape(1, 3, 3, CM, CM), 1, space_pad), total_rows))
        hidden_d = low(slow_keep * jax.nn.silu(normalize(slow_second, slow_mask, slow_count, affine_sb)))
        slow_third = low_back(jnp.dot(hidden_d, weight_sc, precision=lax.Precision.HIGHEST))
        shortcut = low_back(jnp.dot(joined, weight_sh, precision=lax.Precision.HIGHEST))
        slow_total = normalize(slow_third, slow_mask, slow_count, affine_sc) + normalize(shortcut, slow_mask, slow_count, affine_sh)
        slow_result = slow_keep * jax.nn.silu(slow_total)
        return (fast_result, slow_result)
    leaves = (fast_in.astype(jnp.float32), slow_in.astype(jnp.float32), w_fast_a.astype(jnp.float32), w_fast_b.astype(jnp.float32), w_fast_c.astype(jnp.float32), w_lateral.astype(jnp.float32), w_slow_a.astype(jnp.float32), w_slow_b.astype(jnp.float32), w_slow_c.astype(jnp.float32), w_short.astype(jnp.float32), norm_fast_a, norm_fast_b, norm_fast_c, norm_slow_a, norm_slow_b, norm_slow_c, norm_short)
    results, pullback = jax.vjp(forward, leaves)
    grads = pullback((cot_fast.astype(jnp.float32), cot_slow.astype(jnp.float32)))[0]
    return (results[0].astype(jnp.bfloat16), results[1].astype(jnp.bfloat16), grads[0].astype(jnp.bfloat16), grads[1].astype(jnp.bfloat16), grads[2], grads[3], grads[4], grads[5], grads[6], grads[7], grads[8], grads[9], grads[10], grads[11], grads[12], grads[13], grads[14], grads[15], grads[16])
```

```python
import jax
import jax.numpy as jnp
from jax import lax
from jax.sharding import PartitionSpec as P

H = 14
W = 14
ALPHA = 4


NORM_EPSILON = 1e-05


def padded_2(cells, sides, width):
    for axis, dim in sides:
        count = lax.axis_size(axis)
        ends = count - 1
        head = lax.slice_in_dim(cells, 0, width, axis=dim)
        tail = lax.slice_in_dim(cells, cells.shape[dim] - width, cells.shape[dim], axis=dim)
        cells = jnp.concatenate(
            [
                lax.ppermute(tail, axis, [(i, (i + 1) % count) for i in range(ends)]),
                cells,
                lax.ppermute(head, axis, [((i + 1) % count, i) for i in range(ends)]),
            ],
            axis=dim,
        )
    return cells


def all_sum(parts):
    sizes = [part.size for part in parts]
    flat = jnp.concatenate([part.reshape(-1) for part in parts])
    total = flat.shape[0]
    flat = jnp.pad(flat, (0, -total % 128))
    count = lax.axis_size("dp") * lax.axis_size("mp")
    spread = jnp.broadcast_to(flat[None], (count, flat.shape[0]))
    flat = jnp.sum(lax.all_to_all(spread, ("dp", "mp"), 0, 0, tiled=True), axis=0)
    sums = []
    start = 0
    for part, size in zip(parts, sizes):
        sums.append(flat[start : start + size].reshape(part.shape))
        start += size
    return sums


def all_sum_large(parts):
    sizes = [part.size for part in parts]
    flat = jnp.concatenate([part.reshape(-1) for part in parts])
    total = flat.shape[0]
    count = lax.axis_size("dp") * lax.axis_size("mp")
    flat = jnp.pad(flat, (0, -total % (128 * count))).reshape(count, -1)
    mine = jnp.sum(lax.all_to_all(flat, ("dp", "mp"), 0, 0, tiled=True), axis=0)
    spread = jnp.broadcast_to(mine[None], flat.shape)
    flat = lax.all_to_all(spread, ("dp", "mp"), 0, 0, tiled=True).reshape(-1)
    sums = []
    start = 0
    for part, size in zip(parts, sizes):
        sums.append(flat[start : start + size].reshape(part.shape))
        start += size
    return sums


def silu_slope(values):
    sigmoid_value = jax.nn.sigmoid(values)
    return sigmoid_value * (1.0 + values * (1.0 - sigmoid_value))


def matmul(left_side, right_side):
    return jnp.dot(left_side, right_side, preferred_element_type=jnp.float32)


def outer_sum(left_side, right_side):
    return jnp.einsum("abpc,abpd->cd", left_side, right_side, preferred_element_type=jnp.float32)


def back_product(upstream, weights):
    return jnp.einsum("abpd,cd->abpc", upstream, weights, preferred_element_type=jnp.float32)


def norm_forward(values, frame_mask, total_count, affine):
    masked = frame_mask[:, :, None, None] * values
    totals, squares = all_sum(
        (jnp.sum(masked, axis=(0, 1, 2)), jnp.sum(masked * values, axis=(0, 1, 2)))
    )
    average = totals / total_count
    inverse_std = lax.rsqrt(squares / total_count - average * average + NORM_EPSILON)
    standard = (values - average) * inverse_std
    return (affine[0] * standard + affine[1], standard, inverse_std)


def norm_backward(grad_norm_out, standard, inverse_std, frame_mask, total_count, affine):
    grad_beta, grad_gamma = all_sum(
        (jnp.sum(grad_norm_out, axis=(0, 1, 2)), jnp.sum(grad_norm_out * standard, axis=(0, 1, 2)))
    )
    grad_values = (
        frame_mask[:, :, None, None]
        * (inverse_std * affine[0])
        * (grad_norm_out - (grad_beta + standard * grad_gamma) / total_count)
    )
    return (grad_values, jnp.stack([grad_gamma, grad_beta]))


def spatial_patches(inputs):
    leading, frames_here, pixels, channels = inputs.shape
    padded_grid = jnp.pad(
        inputs.reshape(leading * frames_here, H, W, channels), ((0, 0), (1, 1), (1, 1), (0, 0))
    )
    pieces = [
        padded_grid[:, row_shift : row_shift + H, col_shift : col_shift + W]
        for row_shift in range(3)
        for col_shift in range(3)
    ]
    return jnp.concatenate(pieces, -1).reshape(leading, frames_here, pixels, 9 * channels)


def spatial_fold(upstream):
    leading, frames_here, pixels, widths = upstream.shape
    channels = widths // 9
    pieces = upstream.reshape(leading * frames_here, H, W, 9, channels)
    running = jnp.zeros((leading * frames_here, H + 2, W + 2, channels), jnp.float32)
    for row_shift in range(3):
        for col_shift in range(3):
            running = running + jnp.pad(
                pieces[:, :, :, 3 * row_shift + col_shift],
                ((0, 0), (row_shift, 2 - row_shift), (col_shift, 2 - col_shift), (0, 0)),
            )
    return running[:, 1 : H + 1, 1 : W + 1].reshape(leading, frames_here, pixels, channels)


def frame_stack(padded, frames_here, tap_count):
    return jnp.concatenate(
        [padded[:, offset : offset + frames_here] for offset in range(tap_count)], -1
    )


def frame_fold(upstream, tap_count):
    channels = upstream.shape[-1] // tap_count
    running = jnp.pad(upstream[..., :channels], ((0, 0), (0, tap_count - 1), (0, 0), (0, 0)))
    for offset in range(1, tap_count):
        running = running + jnp.pad(
            upstream[..., offset * channels : (offset + 1) * channels],
            ((0, 0), (offset, tap_count - 1 - offset), (0, 0), (0, 0)),
        )
    return running


def lateral_fold(upstream):
    channels = upstream.shape[-1] // 5
    parts = [upstream[..., offset * channels : (offset + 1) * channels] for offset in range(5)]
    after = ((0, 0), (0, 1), (0, 0), (0, 0))
    before = ((0, 0), (1, 0), (0, 0), (0, 0))
    leading_slot = jnp.pad(parts[0], after) + jnp.pad(parts[4], before)
    stacked = jnp.stack(
        [leading_slot] + [jnp.pad(parts[offset], after) for offset in range(1, 4)], 2
    )
    return stacked.reshape(stacked.shape[0], -1, stacked.shape[3], channels)


def per_device(
    fast_in,
    slow_in,
    clip_len,
    w_fast_a,
    w_fast_b,
    w_fast_c,
    w_lateral,
    w_slow_a,
    w_slow_b,
    w_slow_c,
    w_short,
    norm_fast_a,
    norm_fast_b,
    norm_fast_c,
    norm_slow_a,
    norm_slow_b,
    norm_slow_c,
    norm_short,
    cot_fast,
    cot_slow,
):
    batch_here, fast_frames, pixels, fast_width = fast_in.shape
    slow_frames = slow_in.shape[1]
    slow_width = slow_in.shape[3]
    inner_width = w_fast_a.shape[2]
    lateral_width = w_lateral.shape[2]
    clip_count = clip_len.shape[1]
    slot_fast = fast_frames * lax.axis_size("mp") // clip_count
    slot_slow = slot_fast // ALPHA
    rows_here = lax.dynamic_slice_in_dim(clip_len, lax.axis_index("dp") * batch_here, batch_here, 0)
    fast_start = lax.axis_index("mp") * fast_frames
    clip_here = fast_start // slot_fast
    length_here = jnp.sum(
        jnp.where(jnp.arange(clip_count)[None, :] == clip_here, rows_here, 0), axis=1
    )
    fast_mask = (
        (fast_start % slot_fast + jnp.arange(fast_frames))[None, :] < ALPHA * length_here[:, None]
    ).astype(jnp.float32)
    slow_start = lax.axis_index("mp") * slow_frames
    slow_mask = (
        (slow_start % slot_slow + jnp.arange(slow_frames))[None, :] < length_here[:, None]
    ).astype(jnp.float32)
    fast_count = jnp.sum(clip_len).astype(jnp.float32) * (ALPHA * pixels)
    slow_count = jnp.sum(clip_len).astype(jnp.float32) * pixels
    keep_lower = (fast_start % slot_fast != 0).astype(jnp.float32)
    keep_upper = ((fast_start + fast_frames) % slot_fast != 0).astype(jnp.float32)
    lower_bf = keep_lower.astype(jnp.bfloat16)
    upper_bf = keep_upper.astype(jnp.bfloat16)
    fast_keep = fast_mask[:, :, None, None]
    slow_keep = slow_mask[:, :, None, None]
    fast_masked = fast_in * fast_keep.astype(jnp.bfloat16)
    padded_fast = padded_2(fast_masked, (("mp", 1),), 2)
    padded_fast = jnp.concatenate(
        [padded_fast[:, :2] * lower_bf, padded_fast[:, 2:-2], padded_fast[:, -2:] * upper_bf], 1
    )
    fast_stack = frame_stack(padded_fast[:, 1:-1], fast_frames, 3)
    fast_first = matmul(fast_stack, w_fast_a.reshape(-1, inner_width))
    norm_fa, standard_fa, inverse_fa = norm_forward(fast_first, fast_mask, fast_count, norm_fast_a)
    hidden_a = (fast_keep * jax.nn.silu(norm_fa)).astype(jnp.bfloat16)
    patches_a = spatial_patches(hidden_a)
    fast_second = matmul(patches_a, w_fast_b.reshape(-1, inner_width))
    norm_fb, standard_fb, inverse_fb = norm_forward(fast_second, fast_mask, fast_count, norm_fast_b)
    hidden_b = (fast_keep * jax.nn.silu(norm_fb)).astype(jnp.bfloat16)
    fast_third = matmul(hidden_b, w_fast_c)
    norm_fc, standard_fc, inverse_fc = norm_forward(fast_third, fast_mask, fast_count, norm_fast_c)
    fast_sum = norm_fc + fast_masked.astype(jnp.float32)
    fast_out = (fast_keep * jax.nn.silu(fast_sum)).astype(jnp.bfloat16)
    lateral_stack = jnp.concatenate(
        [padded_fast[:, offset : offset + 4 * slow_frames : 4] for offset in range(5)], -1
    )
    lateral_out = matmul(lateral_stack, w_lateral.reshape(-1, lateral_width)).astype(jnp.bfloat16)
    joined = jnp.concatenate([slow_in, lateral_out], -1) * slow_keep.astype(jnp.bfloat16)
    padded_slow = padded_2(joined, (("mp", 1),), 1)
    padded_slow = jnp.concatenate(
        [padded_slow[:, :1] * lower_bf, padded_slow[:, 1:-1], padded_slow[:, -1:] * upper_bf], 1
    )
    full_a, full_b, full_c, full_short = (
        lax.all_gather(w_slow_a, "mp", axis=2, tiled=True),
        lax.all_gather(w_slow_b, "mp", axis=2, tiled=True),
        lax.all_gather(w_slow_c, "mp", axis=1, tiled=True),
        lax.all_gather(w_short, "mp", axis=1, tiled=True),
    )
    middle_width = full_a.shape[2]
    slow_stack = frame_stack(padded_slow, slow_frames, 3)
    slow_first = matmul(slow_stack, full_a.reshape(-1, middle_width))
    norm_sa, standard_sa, inverse_sa = norm_forward(slow_first, slow_mask, slow_count, norm_slow_a)
    hidden_c = (slow_keep * jax.nn.silu(norm_sa)).astype(jnp.bfloat16)
    patches_c = spatial_patches(hidden_c)
    slow_second = matmul(patches_c, full_b.reshape(-1, middle_width))
    norm_sb, standard_sb, inverse_sb = norm_forward(slow_second, slow_mask, slow_count, norm_slow_b)
    hidden_d = (slow_keep * jax.nn.silu(norm_sb)).astype(jnp.bfloat16)
    slow_third = matmul(hidden_d, full_c)
    shortcut = matmul(joined, full_short)
    norm_sc, standard_sc, inverse_sc = norm_forward(slow_third, slow_mask, slow_count, norm_slow_c)
    norm_sh, standard_sh, inverse_sh = norm_forward(shortcut, slow_mask, slow_count, norm_short)
    slow_sum = norm_sc + norm_sh
    slow_out = (slow_keep * jax.nn.silu(slow_sum)).astype(jnp.bfloat16)
    back_a, back_b, back_c, back_short = (full_a, full_b, full_c, full_short)
    slow_cot = cot_slow.astype(jnp.float32) * slow_keep * silu_slope(slow_sum)
    d_slow_third, grad_norm_slow_c = norm_backward(
        slow_cot, standard_sc, inverse_sc, slow_mask, slow_count, norm_slow_c
    )
    d_shortcut, grad_norm_short = norm_backward(
        slow_cot, standard_sh, inverse_sh, slow_mask, slow_count, norm_short
    )
    d_third_low = d_slow_third.astype(jnp.bfloat16)
    d_short_low = d_shortcut.astype(jnp.bfloat16)
    slow_grad_c = outer_sum(hidden_d, d_third_low)
    slow_grad_short = outer_sum(joined, d_short_low)
    d_hidden_d = back_product(d_third_low, back_c)
    d_slow_second, grad_norm_slow_b = norm_backward(
        d_hidden_d * slow_keep * silu_slope(norm_sb),
        standard_sb,
        inverse_sb,
        slow_mask,
        slow_count,
        norm_slow_b,
    )
    d_second_low = d_slow_second.astype(jnp.bfloat16)
    slow_grad_b = outer_sum(patches_c, d_second_low).reshape(9, middle_width, middle_width)
    d_hidden_c = spatial_fold(back_product(d_second_low, back_b.reshape(-1, middle_width)))
    d_slow_first, grad_norm_slow_a = norm_backward(
        d_hidden_c * slow_keep * silu_slope(norm_sa),
        standard_sa,
        inverse_sa,
        slow_mask,
        slow_count,
        norm_slow_a,
    )
    d_first_low = d_slow_first.astype(jnp.bfloat16)
    slow_grad_a = outer_sum(slow_stack, d_first_low).reshape(3, -1, middle_width)
    d_padded_slow = frame_fold(back_product(d_first_low, back_a.reshape(-1, middle_width)), 3)
    slow_rims = jnp.concatenate(
        [d_padded_slow[:, :1] * keep_lower, d_padded_slow[:, -1:] * keep_upper], 1
    )
    slow_back = padded_2(slow_rims.astype(jnp.bfloat16), (("mp", 1),), 1).astype(slow_rims.dtype)
    slow_edges = jnp.pad(
        slow_back[:, :1], ((0, 0), (0, slow_frames - 1), (0, 0), (0, 0))
    ) + jnp.pad(slow_back[:, -1:], ((0, 0), (slow_frames - 1, 0), (0, 0), (0, 0)))
    d_joined = slow_keep * (
        d_padded_slow[:, 1:-1] + slow_edges + back_product(d_short_low, back_short)
    )
    grad_slow_in = d_joined[..., :slow_width].astype(jnp.bfloat16)
    d_lateral_low = d_joined[..., slow_width:].astype(jnp.bfloat16)
    fast_grad_lateral = outer_sum(lateral_stack, d_lateral_low)
    d_padded_fast = lateral_fold(back_product(d_lateral_low, w_lateral.reshape(-1, lateral_width)))
    fast_cot = cot_fast.astype(jnp.float32) * fast_keep * silu_slope(fast_sum)
    d_fast_third, grad_norm_fast_c = norm_backward(
        fast_cot, standard_fc, inverse_fc, fast_mask, fast_count, norm_fast_c
    )
    d_fthird_low = d_fast_third.astype(jnp.bfloat16)
    fast_grad_c = outer_sum(hidden_b, d_fthird_low)
    d_hidden_b = back_product(d_fthird_low, w_fast_c)
    d_fast_second, grad_norm_fast_b = norm_backward(
        d_hidden_b * fast_keep * silu_slope(norm_fb),
        standard_fb,
        inverse_fb,
        fast_mask,
        fast_count,
        norm_fast_b,
    )
    d_fsecond_low = d_fast_second.astype(jnp.bfloat16)
    fast_grad_b = outer_sum(patches_a, d_fsecond_low)
    d_hidden_a = spatial_fold(back_product(d_fsecond_low, w_fast_b.reshape(-1, inner_width)))
    d_fast_first, grad_norm_fast_a = norm_backward(
        d_hidden_a * fast_keep * silu_slope(norm_fa),
        standard_fa,
        inverse_fa,
        fast_mask,
        fast_count,
        norm_fast_a,
    )
    d_ffirst_low = d_fast_first.astype(jnp.bfloat16)
    fast_grad_a = outer_sum(fast_stack, d_ffirst_low)
    d_inner = frame_fold(back_product(d_ffirst_low, w_fast_a.reshape(-1, inner_width)), 3)
    d_padded_fast = d_padded_fast + jnp.pad(d_inner, ((0, 0), (1, 1), (0, 0), (0, 0)))
    fast_rims = jnp.concatenate(
        [d_padded_fast[:, :2] * keep_lower, d_padded_fast[:, -2:] * keep_upper], 1
    )
    fast_back = padded_2(fast_rims.astype(jnp.bfloat16), (("mp", 1),), 2).astype(fast_rims.dtype)
    fast_edges = jnp.pad(
        fast_back[:, :2], ((0, 0), (0, fast_frames - 2), (0, 0), (0, 0))
    ) + jnp.pad(fast_back[:, -2:], ((0, 0), (fast_frames - 2, 0), (0, 0), (0, 0)))
    grad_fast_in = (fast_keep * (d_padded_fast[:, 2:-2] + fast_edges + fast_cot)).astype(
        jnp.bfloat16
    )
    summed_a, summed_b, summed_c, summed_lateral = all_sum_large(
        (fast_grad_a, fast_grad_b, fast_grad_c, fast_grad_lateral)
    )
    whole = (
        lax.psum(slow_grad_a.astype(jnp.bfloat16), "dp").astype(jnp.float32),
        lax.psum(slow_grad_b.astype(jnp.bfloat16), "dp").astype(jnp.float32),
        lax.psum(slow_grad_c.astype(jnp.bfloat16), "dp").astype(jnp.float32),
        lax.psum(slow_grad_short.astype(jnp.bfloat16), "dp").astype(jnp.float32),
    )
    pieces = (
        lax.psum_scatter(
            whole[0].astype(jnp.bfloat16), "mp", scatter_dimension=2, tiled=True
        ).astype(jnp.float32),
        lax.psum_scatter(
            whole[1].astype(jnp.bfloat16), "mp", scatter_dimension=2, tiled=True
        ).astype(jnp.float32),
        lax.psum_scatter(
            whole[2].astype(jnp.bfloat16), "mp", scatter_dimension=1, tiled=True
        ).astype(jnp.float32),
        lax.psum_scatter(
            whole[3].astype(jnp.bfloat16), "mp", scatter_dimension=1, tiled=True
        ).astype(jnp.float32),
    )
    return (
        fast_out,
        slow_out,
        grad_fast_in,
        grad_slow_in,
        summed_a.reshape(3, fast_width, inner_width),
        summed_b.reshape(9, inner_width, inner_width),
        summed_c,
        summed_lateral.reshape(5, fast_width, lateral_width),
        pieces[0],
        pieces[1],
        pieces[2],
        pieces[3],
        grad_norm_fast_a,
        grad_norm_fast_b,
        grad_norm_fast_c,
        grad_norm_slow_a,
        grad_norm_slow_b,
        grad_norm_slow_c,
        grad_norm_short,
    )


def solution(mesh):
    placed = (
        P("dp", "mp", None, None),
        P("dp", "mp", None, None),
        P(),
        P(),
        P(),
        P(),
        P(),
        P(None, None, "mp"),
        P(None, None, "mp"),
        P(None, "mp"),
        P(None, "mp"),
        P(),
        P(),
        P(),
        P(),
        P(),
        P(),
        P(),
        P("dp", "mp", None, None),
        P("dp", "mp", None, None),
    )
    return jax.shard_map(
        per_device,
        mesh=mesh,
        in_specs=placed,
        out_specs=(
            P("dp", "mp", None, None),
            P("dp", "mp", None, None),
            P("dp", "mp", None, None),
            P("dp", "mp", None, None),
            P(),
            P(),
            P(),
            P(),
            P(None, None, "mp"),
            P(None, None, "mp"),
            P(None, "mp"),
            P(None, "mp"),
            P(),
            P(),
            P(),
            P(),
            P(),
            P(),
            P(),
        ),
        check_vma=False,
    )
```

```python
import functools

import jax
import jax.numpy as jnp
import numpy as np
from jax import lax
from jax.experimental import pallas as pl
from jax.experimental.pallas import tpu as pltpu
from jax.sharding import PartitionSpec as P

H = 14
W = 14
ALPHA = 4
NORM_EPSILON = 1e-05
BF = jnp.bfloat16
F32 = jnp.float32


def xor_permute(values, axis, bits):
    count = lax.axis_size(axis)
    return lax.ppermute(values, axis, [(i, i ^ bits) for i in range(count)])


def shift_permute(values, axis, step):
    count = lax.axis_size(axis)
    return lax.ppermute(
        values, axis, [(i, i + step) for i in range(count) if 0 <= i + step < count]
    )


def sum_everywhere(rows):
    count = lax.axis_size("dp") * lax.axis_size("mp")
    parts = rows.reshape(count, -1, 128)
    pieces = lax.all_to_all(parts, ("dp", "mp"), 0, 0, tiled=True)
    mine = jnp.sum(pieces.astype(F32), axis=0).astype(BF)
    whole = lax.all_to_all(
        jnp.broadcast_to(mine[None], parts.shape), ("dp", "mp"), 0, 0, tiled=True
    )
    return whole.reshape(rows.shape).astype(F32)


def small_mesh():
    return lax.axis_size("dp") == 4 and lax.axis_size("mp") == 8


def pick(values, index, axis):
    return lax.dynamic_index_in_dim(values, index, axis, keepdims=False)


COST_BYTES = 0
SLACK = 3 * 2**20


def cost(microseconds):
    return pl.CostEstimate(
        flops=0, bytes_accessed=1 + int(microseconds * COST_BYTES), transcendentals=0
    )


def place_call(kernel, pieces, outs):
    where = jnp.stack([lax.axis_index("mp"), lax.axis_index("dp") % 2]).astype(jnp.int32)

    def body(where_ref, *refs):
        side, core = lax.rem(where_ref[0], 2), where_ref[1]
        mine = where_ref[0] - side
        for k in range(4):
            owner_side = side if k % 2 == 0 else 1 - side
            half = core if k < 2 else 1 - core
            for far in range(4):
                line = jnp.bitwise_xor(mine, 2 * far)
                kernel(line + owner_side, half, refs[k].at[far], *refs[4:])

    vmem = pl.BlockSpec(memory_space=pltpu.VMEM)
    return pl.pallas_call(
        body,
        out_shape=[jax.ShapeDtypeStruct(shape, BF) for shape in outs],
        in_specs=[pl.BlockSpec(memory_space=pltpu.SMEM)] + [vmem] * 4,
        out_specs=[vmem] * len(outs),
        compiler_params=pltpu.CompilerParams(vmem_limit_bytes=32 * 2**20),
        cost_estimate=cost(2),
    )(where, *pieces)


def line_apart(shard):
    mine = pick(shard, lax.axis_index("dp") % 2, 0)
    return [mine] + [xor_permute(mine, "mp", 2 * step) for step in (1, 2, 3)]


def line_pieces(shard):
    return jnp.stack(line_apart(shard))


def both_sides(near):
    side = xor_permute(near, "mp", 1)
    return near, side, xor_permute(near, "dp", 1), xor_permute(side, "dp", 1)


def place_a(block, half, piece, out):
    part = piece.shape[0] // 3
    width = out.shape[0] // 3
    for tap in range(3):
        start = pl.multiple_of(tap * width + block * (2 * part) + half * part, part)
        out[pl.ds(start, part), :] = piece[tap * part : (tap + 1) * part, :]


def place_bc(block, half, piece, out_f, out_b, out_c):
    width = out_f.shape[0]
    part = width // 16
    for tap in range(9):
        values = piece[tap * part : (tap + 1) * part, :]
        start = pl.multiple_of(block * (2 * part) + half * part, part)
        out_f[pl.ds(start, part), tap * width : (tap + 1) * width] = values
        start = pl.multiple_of((8 - tap) * width + block * (2 * part) + half * part, part)
        out_b[pl.ds(start, part), :] = values
    rest = piece.shape[0] - 9 * part
    columns = pl.ds(pl.multiple_of(block * 128, 128), 128)
    for k in range(2):
        start = pl.multiple_of(half * (2 * rest) + k * rest, rest)
        out_c[pl.ds(start, rest), columns] = piece[9 * part :, k * 128 : (k + 1) * 128]


def place_short(block, half, piece, out):
    part = piece.shape[0]
    columns = pl.ds(pl.multiple_of(block * 128, 128), 128)
    out[pl.ds(pl.multiple_of(half * part, part), part), columns] = piece[...]


def held(values, other):
    return lax.optimization_barrier((values, other))[0]


def start_gather(w_slow_a, w_slow_b, w_slow_c, w_short):
    cu, part = w_slow_a.shape[1:]
    cm = w_slow_b.shape[1]
    wide = w_short.shape[1]
    a_t = jnp.swapaxes(w_slow_a, 1, 2)
    b_t = jnp.swapaxes(w_slow_b, 1, 2)
    if not small_mesh():
        return a_t, b_t, w_slow_c, w_short
    half = part // 2
    a_t = a_t.reshape(3, 2, half, cu).transpose(1, 0, 2, 3).reshape(2, 3 * half, cu)
    b_t = b_t.reshape(9, 2, half, cm).transpose(1, 0, 2, 3).reshape(2, 9 * half, cm)
    c_t = w_slow_c.reshape(2, 2, cm // 4, wide).transpose(0, 2, 1, 3).reshape(2, cm // 4, 2 * wide)
    return line_pieces(a_t), jnp.concatenate([b_t, c_t], 1), w_short.reshape(2, cu // 2, wide)


def gather_a(shard, others):
    if not small_mesh():
        wa = lax.all_gather(shard, "mp", axis=1, tiled=True)
        return wa.reshape(-1, wa.shape[2])
    cm, cu = 16 * (shard.shape[1] // 3), shard.shape[2]
    return place_call(place_a, held(both_sides(shard), others), [(3 * cm, cu)])[0]


def gather_bc(b_part, c_part, pieces):
    if not small_mesh():
        wb = lax.all_gather(b_part, "mp", axis=1, tiled=True)
        wc = lax.all_gather(c_part, "mp", axis=1, tiled=True)
        cm = wb.shape[1]
        return wb.transpose(1, 0, 2).reshape(cm, 9 * cm), wb[::-1].reshape(9 * cm, cm), wc
    cm = b_part.shape[2]
    return place_call(place_bc, pieces, [(cm, 9 * cm), (9 * cm, cm), (cm, 4 * cm)])


def gather_short(shard, pieces):
    if not small_mesh():
        return lax.all_gather(shard, "mp", axis=1, tiled=True)
    return place_call(place_short, pieces, [(2 * shard.shape[1], 8 * shard.shape[2])])[0]


def quick_call(kernel, arrays, outs):
    clips = lax.axis_index("dp")
    where = jnp.stack([lax.axis_index("mp"), clips % 2, clips // 2]).astype(jnp.int32)
    vmem = pl.BlockSpec(memory_space=pltpu.VMEM)
    return pl.pallas_call(
        kernel,
        out_shape=[jax.ShapeDtypeStruct(shape, dtype) for shape, dtype in outs],
        in_specs=[pl.BlockSpec(memory_space=pltpu.SMEM)] + [vmem] * len(arrays),
        out_specs=[vmem] * len(outs),
        compiler_params=pltpu.CompilerParams(vmem_limit_bytes=12 * 2**20),
        cost_estimate=cost(1.5),
    )(where, *arrays)


def plus(*values):
    total = values[0].astype(F32)
    for value in values[1:]:
        total = total + value.astype(F32)
    return total.astype(BF)


def columns_of(index, width):
    return pl.ds(pl.multiple_of(index * width, 128), width)


def groups_of(arrays):
    places, start = [], 0
    for k, array in enumerate(arrays):
        width = array.shape[-1] // 2
        for row in range(0, array.shape[-2], 16):
            places.append((k, row, start, width))
            start += width
    return places, start


def cores_kernel(where_ref, *refs):
    count = (len(refs) - 2) // 2
    keeps, sents, (far_ref, near_ref) = refs[:count], refs[count:-2], refs[-2:]
    x = where_ref[2]
    for k, row, start, width in groups_of(keeps)[0]:
        for columns, out_ref in ((columns_of(x, width), near_ref), (columns_of(1 - x, width), far_ref)):
            total = plus(
                keeps[k][:, row : row + 16, columns], sents[k][:, row : row + 16, columns]
            )
            out_ref[:, :, start : start + width] = total


def cross_cores(sents, keeps):
    outs = [((8, 16, groups_of(keeps)[1]), BF)] * 2
    return quick_call(cores_kernel, [*keeps, *sents], outs)


def swap_cores(send):
    return xor_permute(send, "dp", 1)


def chips_kernel(where_ref, keep_ref, sent_ref, far_ref, near_ref):
    side = lax.rem(where_ref[0], 2)
    for line in range(4):
        near, far = 2 * line + side, 2 * line + 1 - side
        near_ref[line] = plus(keep_ref[near], sent_ref[near])
        far_ref[line] = plus(keep_ref[far], sent_ref[far])


def cross_chips(far, near):
    outs = [((4,) + near.shape[1:], BF)] * 2
    return quick_call(chips_kernel, [near, xor_permute(far, "dp", 2)], outs)


def lines_kernel(where_ref, keep_ref, sent_ref, *out_refs):
    mine = where_ref[0] // 2
    for step, out_ref in enumerate(out_refs):
        place = jnp.bitwise_xor(mine, step)
        out_ref[...] = plus(keep_ref[place], sent_ref[place])


def cross_lines(far, near):
    outs = [(near.shape[1:], BF)] * 4
    return quick_call(lines_kernel, [near, xor_permute(far, "mp", 1)], outs)


def along_kernel(where_ref, *refs):
    refs[-1][...] = plus(*[ref[...] for ref in refs[:-1]])


def along_line(pieces):
    sent = [xor_permute(piece, "mp", 2 * step) for step, piece in enumerate(pieces) if step]
    return quick_call(along_kernel, [pieces[0]] + sent, [(pieces[0].shape, BF)])[0]


def clips_kernel(where_ref, mine_ref, far_ref, other_ref, far_other_ref, *out_refs):
    core, x = where_ref[1], where_ref[2]
    pairs = ((core, x, mine_ref), (core, 1 - x, far_ref), (1 - core, x, other_ref), (1 - core, 1 - x, far_other_ref))
    for k, row, start, width in groups_of(out_refs)[0]:
        for half, side, ref in pairs:
            values = ref[:, start : start + width].astype(F32)
            out_refs[k][half, row : row + 16, columns_of(side, width)] = values


def cross_clips(total, shapes):
    arrays = [total] + [xor_permute(total, "dp", bits) for bits in (2, 1, 3)]
    return quick_call(clips_kernel, arrays, [((2,) + shape, F32) for shape in shapes])


def reduce_whole(blocks):
    whole = lax.psum(blocks.astype(BF), "dp")
    return lax.psum_scatter(whole, "mp", scatter_dimension=0, tiled=True)[0].astype(F32)


def tn(left, right):
    return lax.dot_general(left, right, (((0,), (0,)), ((), ())), preferred_element_type=F32)


def cut_halves(core, whole_ref, send_ref, keep_ref, groups=1):
    blocks, size = keep_ref.shape[0], keep_ref.shape[1] // groups
    for group in range(groups):
        for block in range(blocks):
            start = (group * blocks + block) * 2 * size
            place = slice(group * size, (group + 1) * size)
            send_ref[block, place, :] = whole_ref[pl.ds(pl.multiple_of(start + (1 - core) * size, size), size), :]
            keep_ref[block, place, :] = whole_ref[pl.ds(pl.multiple_of(start + core * size, size), size), :]


def grad_cs_kernel(core_ref, dh_ref, ds_ref, joined_ref, hidden_ref, send_ref, keep_ref, whole_ref):
    wide, cu = dh_ref.shape[1], joined_ref.shape[1]
    for start in range(0, wide, 256):
        part = slice(start, start + 256)
        whole_ref[part, 0:cu] = tn(dh_ref[:, part], joined_ref[...]).astype(BF)
    whole_ref[:, cu:] = tn(ds_ref[...], hidden_ref[...]).astype(BF)
    cut_halves(core_ref[0], whole_ref, send_ref, keep_ref)


def fill_buffer(buffer, values_ref):
    clear_margins(buffer)
    for start in range(0, values_ref.shape[0], ROWS_STEP):
        rows = values_ref[start : start + ROWS_STEP, :].astype(F32)
        buffer[MARGIN + start : MARGIN + start + ROWS_STEP, :] = rows


def grad_b_kernel(
    core_ref, ds_ref, hidden_ref, edge_ref, send_ref, keep_ref, whole_ref, buffer_ref, patches_ref
):
    fill_buffer(buffer_ref, hidden_ref)
    write_patches(buffer_ref, patches_ref, edge_ref)
    whole_ref[...] = tn(ds_ref[...], patches_ref[...]).astype(BF)
    cut_halves(core_ref[0], whole_ref, send_ref, keep_ref)


def grad_b_whole_kernel(
    core_ref, ds_ref, hidden_ref, edge_ref, out_ref, buffer_ref, patches_ref
):
    fill_buffer(buffer_ref, hidden_ref)
    write_patches(buffer_ref, patches_ref, edge_ref)
    out_ref[...] = tn(ds_ref[...], patches_ref[...])


def grad_a_kernel(
    core_ref, one_ref, two_ref, before_ref, after_ref, joined_ref, send_ref, keep_ref, whole_ref
):
    cm = whole_ref.shape[0] // 3
    pairs = ((two_ref, after_ref), (one_ref, two_ref), (before_ref, one_ref))
    for tap, (left_ref, right_ref) in enumerate(pairs):
        total = tn(left_ref[:, :cm], joined_ref[0]) + tn(right_ref[:, :cm], joined_ref[1])
        whole_ref[tap * cm : (tap + 1) * cm, :] = total.astype(BF)
    cut_halves(core_ref[0], whole_ref, send_ref, keep_ref, 3)


def fast_grads_kernel(
    core_ref, stack_ref, one_ref, two_ref, hidden_a_ref, second_ref, hidden_ref, third_ref,
    lateral_ref, dl_ref, edge_ref, out_ref, buffer_ref, patches_ref,
):
    ci, cf = 128 // ALPHA, 128

    def leftward(values, j):
        return pltpu.roll(values, 128 - j * ci, 1) if j else values

    cm = one_ref.shape[1] - 128
    fill_buffer(buffer_ref, hidden_a_ref)
    write_patches(buffer_ref, patches_ref, edge_ref)
    raw = tn(stack_ref[0], one_ref[:, cm:]) + tn(stack_ref[1], two_ref[:, cm:])
    out_ref[0 : 3 * cf, :] = sum(
        leftward(raw[j * cf : (j + 3) * cf, :], j) for j in range(ALPHA)
    ).astype(BF)
    raw = tn(patches_ref[...], second_ref[...])
    for tap in range(9):
        total = sum(
            leftward(raw[tap * 128 + j * ci : tap * 128 + (j + 1) * ci, :], j) for j in range(ALPHA)
        )
        out_ref[3 * cf + tap * ci : 3 * cf + (tap + 1) * ci, :] = total.astype(BF)
    raw = tn(hidden_ref[...], third_ref[...])
    start = 3 * cf + 9 * ci
    out_ref[start : start + ci, :] = sum(
        raw[j * ci : (j + 1) * ci, j * cf : (j + 1) * cf] for j in range(ALPHA)
    ).astype(BF)
    raw = tn(lateral_ref[0], dl_ref[0]) + tn(lateral_ref[1], dl_ref[1])
    start += ci
    size = raw.shape[0]
    out_ref[start : start + size, :] = raw[:, :128].astype(BF)
    out_ref[start + size : start + 2 * size, :] = raw[:, 128:].astype(BF)
    rest = out_ref.shape[0] - start - 2 * size
    out_ref[start + 2 * size :, :] = jnp.zeros((rest, 128), BF)


def first_kernel(
    count_ref, sums_ref, first_ref, gf_ref, gs_ref, vf_ref, vs_ref, afa_ref, asa_ref, mask_ref,
    one_ref, two_ref, total_ref,
):
    fast_count, slow_count = count_ref[0], count_ref[1]
    total = jnp.sum(sums_ref[...], axis=0)
    total_ref[...] = total
    cells, cm = one_ref.shape[0], gs_ref.shape[1]
    fast_beta, fast_gamma, beta, gamma = split(total, (128, 128, 256, 256))
    ft, fq, st, sq = split(first_ref[...], (128, 128, 256, 256))
    mean, inverse = mean_inverse(fold_lanes(ft, ALPHA), fold_lanes(fq, ALPHA), fast_count)
    fast_lines = back_line(
        mean, inverse, afa_ref[0:1, :], fold_lanes(fast_beta, ALPHA), fold_lanes(fast_gamma, ALPHA), fast_count
    )
    slow_lines = back_line(*mean_inverse(st, sq, slow_count), asa_ref[0:1, :], beta, gamma, slow_count)
    for grad_ref, value_ref, columns, (one, two, three) in (
        (gf_ref, vf_ref, slice(cm, cm + 128), fast_lines),
        (gs_ref, vs_ref, slice(0, cm), slow_lines),
    ):
        for frame, out_ref in enumerate((one_ref, two_ref)):
            now = slice(frame * cells, (frame + 1) * cells)
            mask = wide_mask(mask_ref[now, :], grad_ref.shape[1])
            grad = mask * (grad_ref[now, :] * one - two - value_ref[now, :] * three)
            out_ref[:, columns] = grad.astype(BF)


def joined_back_kernel(
    mask_ref, one_ref, two_ref, before_ref, after_ref, dh_ref, wa_ref, ws_ref,
    out_ref, lat_ref, rows_ref,
):
    cells = one_ref.shape[0]
    cm = wa_ref.shape[0] // 3
    cs = out_ref.shape[1]
    for frame, pieces in enumerate(
        ((two_ref, one_ref, before_ref), (after_ref, two_ref, one_ref))
    ):
        mask = mask_ref[frame * cells : (frame + 1) * cells, :]
        taps = jnp.concatenate([piece[:, :cm] for piece in pieces], axis=1)
        for start in range(0, ws_ref.shape[0], 256):
            part = slice(start, start + 256)
            grad = mm(taps, wa_ref[:, part]) + mm_t(dh_ref[frame], ws_ref[part, :])
            grad = grad * wide_mask(mask, 256)
            if start < cs:
                for column in range(start, start + 256, 128):
                    piece = grad[:, column - start : column - start + 128]
                    rows_ref[column // 128, pl.ds(frame, cells, 2), :] = piece
            else:
                lat_ref[frame, :, start - cs : start - cs + 256] = grad.astype(BF)
    for column in range(0, cs, 128):
        out_ref[:, column : column + 128] = rows_ref[column // 128].astype(BF)


def unpack_kernel(mask_ref, in_ref, out_ref, tail_ref, head_ref, rows_ref):
    frames, cells = out_ref.shape[:2]
    step = frames * ALPHA
    rows_ref[...] = in_ref[...].astype(F32)
    for frame in range(frames):
        mask = mask_ref[frame * cells : (frame + 1) * cells, :]
        for j in range(ALPHA):
            values = rows_ref[pl.ds(frame * ALPHA + j, cells, step), :] * mask
            values = values.astype(BF)
            out_ref[frame, :, j * 128 : (j + 1) * 128] = values
            if frame == frames - 1 and j >= 2:
                tail_ref[:, (j - 2) * 128 : (j - 1) * 128] = values
            if frame == 0 and j == 0:
                head_ref[...] = values


def entry_kernel(
    mask_ref, fast_ref, before_ref, after_ref, slow_ref, wa_ref, wl_ref,
    stack_ref, lateral_ref, first_ref, sums_ref, joined_ref,
):
    cells = before_ref.shape[0]
    cs, cf = slow_ref.shape[2], 128
    tots, squares = [], []
    for frame in range(2):
        mask = mask_ref[frame * cells : (frame + 1) * cells, :]
        own = fast_ref[frame]
        past = before_ref[...] if frame == 0 else fast_ref[0][:, 2 * cf :]
        following = fast_ref[1][:, :cf] if frame == 0 else after_ref[...]
        stack_ref[frame, :, 0:cf] = past[:, cf:]
        stack_ref[frame, :, cf : 5 * cf] = own
        stack_ref[frame, :, 5 * cf :] = following
        lateral_ref[frame, :, 0 : 2 * cf] = past
        lateral_ref[frame, :, 2 * cf :] = own[:, : 3 * cf]
        value = mm(stack_ref[frame], wa_ref[...])
        first_ref[frame * cells : (frame + 1) * cells, :] = value
        tots.append(total_row(value * mask))
        squares.append(total_row(value * mask * value))
        lateral = mm(lateral_ref[frame], wl_ref[...]).astype(BF)
        low = mask.astype(BF)
        joined_ref[frame, :, cs:] = lateral * wide_mask(low, 256)
        for start in range(0, cs, 128):
            part = slice(start, start + 128)
            joined_ref[frame, :, part] = slow_ref[frame, :, part] * low
    sums_ref[:, :128] = tots[0] + tots[1]
    sums_ref[:, 128:] = squares[0] + squares[1]


def taps_kernel(core_ref, joined_ref, wa_ref, base_ref, right_ref, left_ref, one_ref, two_ref):
    cells, cm = right_ref.shape
    one_ref[...] = mm_t(joined_ref[0], wa_ref[...])
    two_ref[...] = mm_t(joined_ref[1], wa_ref[...])
    base_ref[:cells, :] = one_ref[:, cm : 2 * cm] + two_ref[:, 2 * cm :]
    base_ref[cells:, :] = two_ref[:, cm : 2 * cm] + one_ref[:, :cm]
    right_ref[...] = two_ref[:, :cm].astype(BF)
    left_ref[...] = one_ref[:, 2 * cm :].astype(BF)


def first_sums_kernel(mask_ref, base_ref, left_ref, right_ref, fast_ref, first_ref, vec_ref):
    cells, cm = left_ref.shape
    tot = square = jnp.zeros((1, cm), F32)
    for frame, halo_ref in enumerate((left_ref, right_ref)):
        now = slice(frame * cells, (frame + 1) * cells)
        value = base_ref[now, :] + halo_ref[...].astype(F32)
        first_ref[now, :] = value
        masked = value * wide_mask(mask_ref[now, :], cm)
        tot = tot + total_row(masked)
        square = square + total_row(masked * value)
    send_all(vec_ref, [fast_ref[...], tot, square])


def sum_kernel(where_ref, sums_ref, vec_ref):
    total = jnp.sum(sums_ref[...], axis=0)
    vec_ref[...] = jnp.broadcast_to(total[None], vec_ref.shape)


def fast_back_kernel(
    mask_ref, one_ref, two_ref, before_ref, after_ref, dl_ref, halo_ref, cot_ref, wl_ref, wa_ref,
    out_ref, rows_ref,
):
    cells = one_ref.shape[0]
    cm = one_ref.shape[1] - 128
    for frame in range(2):
        now = slice(frame * cells, (frame + 1) * cells)
        mask = mask_ref[now, :]
        pieces = (before_ref, one_ref, two_ref) if frame == 0 else (one_ref, two_ref, after_ref)
        taps = jnp.concatenate([piece[:, cm:] for piece in pieces], axis=1)
        lateral = jnp.concatenate([dl_ref[frame], halo_ref[...] if frame else dl_ref[1]], axis=1)
        for j in range(ALPHA):
            part = slice(j * 128, (j + 1) * 128)
            grad = mm(lateral, wl_ref[:, part]) + mm(taps, wa_ref[:, part]) + cot_ref[now, part]
            rows_ref[pl.ds(frame * ALPHA + j, cells, 2 * ALPHA), :] = grad * mask
    out_ref[...] = rows_ref[...].astype(BF)


def dot(left, right, left_dim, right_dim):
    return lax.dot_general(
        left, right, (((left_dim,), (right_dim,)), ((), ())), preferred_element_type=F32
    )


def rows_dot(left, right):
    return lax.dot_general(
        left, right, (((0, 1), (0, 1)), ((), ())), preferred_element_type=F32
    )


def folded(vector, groups):
    return jnp.sum(vector.reshape(groups, -1), axis=0)


def norm_terms(totals, squares, count, groups=1):
    average = totals / count
    inverse = lax.rsqrt(squares / count - average * average + NORM_EPSILON)
    return jnp.tile(average, groups), jnp.tile(inverse, groups)


ROWS_STEP = 112
TAPS = [(dh, dw) for dh in (-1, 0, 1) for dw in (-1, 0, 1)]


def row_chunks(rows, step):
    return [pl.ds(start, step) for start in range(0, rows, step)]


def loop_rows(rows, step, body, init):
    def turn(i, carry):
        return body(pl.ds(pl.multiple_of(i * step, step), step), carry)

    return lax.fori_loop(0, rows // step, turn, init)


def collapse(values):
    return jnp.sum(values.reshape(-1, 8, values.shape[-1]), axis=0)


def gate_of(values):
    return 0.5 * jnp.tanh(0.5 * values) + 0.5


def fold_lanes(vector, groups):
    width = vector.shape[-1] // groups
    total = vector
    for j in range(1, groups):
        total = total + pltpu.roll(vector, j * width, 1)
    return total


def mean_inverse(totals, squares, count):
    average = totals / count
    return average, lax.rsqrt(squares / count - average * average + NORM_EPSILON)


def line(average, inverse, affine):
    scale = affine[0:1] * inverse
    return scale, affine[1:2] - average * scale


def send_all(vec_ref, pieces):
    start = 0
    for piece in pieces:
        width = piece.shape[-1]
        spread = jnp.broadcast_to(piece[None], (vec_ref.shape[0], 1, width))
        vec_ref[:, :, start : start + width] = spread
        start += width


def received(sums_ref, widths):
    total = jnp.sum(sums_ref[...], axis=0)
    return split(total, widths)


def split(total, widths):
    pieces = []
    start = 0
    for width in widths:
        pieces.append(total[:, start : start + width])
        start += width
    return pieces


def total_row(vector):
    return jnp.sum(vector, axis=0, keepdims=True)


MARGIN = 16


def clear_margins(buffer):
    rows = buffer.shape[0]
    zeros = jnp.zeros((MARGIN, buffer.shape[1]), F32)
    buffer[0:MARGIN, :] = zeros
    buffer[rows - MARGIN : rows, :] = zeros


def write_patches(buffer, patches, edges):
    rows, channels = patches.shape[0], buffer.shape[1]
    for start in range(0, rows, ROWS_STEP):
        top, bottom, left, right = (edges[k, start : start + ROWS_STEP, :] for k in range(4))
        for tap, (dh, dw) in enumerate(TAPS):
            mask = None
            if dh:
                mask = top if dh < 0 else bottom
            if dw:
                side = left if dw < 0 else right
                mask = side if mask is None else mask * side
            offset = MARGIN + start + W * dh + dw
            for column in range(0, channels, 128):
                piece = buffer[offset : offset + ROWS_STEP, column : column + 128]
                if mask is not None:
                    piece = piece * mask
                place = tap * channels + column
                patches[start : start + ROWS_STEP, place : place + 128] = piece.astype(BF)


def mm(left, right):
    return jnp.dot(left, right, preferred_element_type=F32)


def mm_t(left, right):
    return lax.dot_general(left, right, (((1,), (1,)), ((), ())), preferred_element_type=F32)


def wide_mask(mask, width):
    return jnp.concatenate([mask] * (width // 128), axis=1) if width > 128 else mask


def conv_kernel(
    count_ref, sums_ref, vf_ref, vs_ref, af_ref, as_ref, mask_ref, edge_ref, wf_ref, ws_ref,
    hf_ref, hs_ref, of_ref, os_ref, total_ref, vec_ref, bf_ref, bs_ref, pf_ref, ps_ref,
):
    fast_count, slow_count = count_ref[0], count_ref[1]
    total = jnp.sum(sums_ref[...], axis=0)
    total_ref[...] = total
    ft, fq, st, sq = split(total, (128, 128, 256, 256))
    lines = []
    for tot, square, count, affine in ((ft, fq, fast_count, af_ref), (st, sq, slow_count, as_ref)):
        if tot.shape[-1] == 128:
            tot, square = fold_lanes(tot, ALPHA), fold_lanes(square, ALPHA)
        lines.append(line(*mean_inverse(tot, square, count), affine[...]))
    rows = vf_ref.shape[0]
    for value_ref, hidden_ref, buffer, (scale, shift) in (
        (vf_ref, hf_ref, bf_ref, lines[0]),
        (vs_ref, hs_ref, bs_ref, lines[1]),
    ):
        width = value_ref.shape[1]
        clear_margins(buffer)
        for start in range(0, rows, ROWS_STEP):
            z = value_ref[start : start + ROWS_STEP, :] * scale + shift
            hidden = z * gate_of(z) * wide_mask(mask_ref[start : start + ROWS_STEP, :], width)
            buffer[MARGIN + start : MARGIN + start + ROWS_STEP, :] = hidden
            hidden_ref[start : start + ROWS_STEP, :] = hidden.astype(BF)
    write_patches(bf_ref, pf_ref, edge_ref)
    write_patches(bs_ref, ps_ref, edge_ref)
    of_ref[...] = mm(pf_ref[...], wf_ref[...])
    os_ref[...] = mm_t(ps_ref[...], ws_ref[...])
    pieces = []
    for out_ref in (of_ref, os_ref):
        width = out_ref.shape[1]

        def body(rows_now, carry):
            value = out_ref[rows_now, :]
            masked = value * wide_mask(mask_ref[rows_now, :], width)
            return carry[0] + collapse(masked), carry[1] + collapse(masked * value)

        zero = jnp.zeros((8, width), F32)
        pieces += [total_row(v) for v in loop_rows(rows, ROWS_STEP, body, (zero, zero))]
    send_all(vec_ref, pieces)


def expand_kernel(
    count_ref, sums_ref, short_ref, vf_ref, vs_ref, af_ref, as_ref, mask_ref, wf_ref, ws_ref,
    hf_ref, hs_ref, yf_ref, ys_ref, total_ref, vec_ref, of_ref, os_ref,
):
    fast_count, slow_count = count_ref[0], count_ref[1]
    total = jnp.sum(sums_ref[...], axis=0)
    total_ref[...] = total
    ft, fq, st, sq = split(total, (128, 128, 256, 256))
    ft, fq = fold_lanes(ft, ALPHA), fold_lanes(fq, ALPHA)
    lines = (
        line(*mean_inverse(ft, fq, fast_count), af_ref[...]),
        line(*mean_inverse(st, sq, slow_count), as_ref[...]),
    )
    rows = vf_ref.shape[0]
    for value_ref, hidden_ref, (scale, shift) in ((vf_ref, hf_ref, lines[0]), (vs_ref, hs_ref, lines[1])):
        width = value_ref.shape[1]

        def body(rows_now, carry):
            z = value_ref[rows_now, :] * scale + shift
            hidden = z * gate_of(z) * wide_mask(mask_ref[rows_now, :], width)
            hidden_ref[rows_now, :] = hidden.astype(BF)
            return carry

        loop_rows(rows, ROWS_STEP, body, 0)
    of_ref[...] = mm(hf_ref[...], wf_ref[...])
    os_ref[...] = mm(hs_ref[...], ws_ref[...])
    pieces = []
    for out_ref, low_ref in ((of_ref, yf_ref), (os_ref, ys_ref)):
        width = out_ref.shape[1]
        tots, squares = [], []
        for column in range(0, width, 512):

            def body(rows_now, carry):
                value = out_ref[rows_now, column : column + 512]
                low_ref[rows_now, column : column + 512] = value.astype(low_ref.dtype)
                value = value.astype(low_ref.dtype).astype(F32)
                masked = value * wide_mask(mask_ref[rows_now, :], 512)
                return carry[0] + collapse(masked), carry[1] + collapse(masked * value)

            zero = jnp.zeros((8, 512), F32)
            one, two = loop_rows(rows, 16, body, (zero, zero))
            tots.append(total_row(one))
            squares.append(total_row(two))
        if width == 512:
            pieces += [sum(v[:, j * 128 : (j + 1) * 128] for j in range(ALPHA)) for v in (tots[0], squares[0])]
        else:
            pieces += [jnp.concatenate(tots, 1), jnp.concatenate(squares, 1)]
    send_all(vec_ref, pieces + [short_ref[...]])


def short_kernel(mask_ref, joined_ref, ws_ref, out_ref, vec_ref):
    rows, wide = out_ref.shape
    for column in range(0, wide, 256):
        part = slice(column, column + 256)
        one = jnp.zeros((8, 256), F32)
        two = one
        for start in range(0, rows, 2 * ROWS_STEP):
            now = slice(start, min(start + 2 * ROWS_STEP, rows))
            value = mm(joined_ref[now, :], ws_ref[:, part])
            out_ref[now, part] = value.astype(BF)
            value = value.astype(BF).astype(F32)
            masked = value * wide_mask(mask_ref[now, :], 256)
            one = one + collapse(masked)
            two = two + collapse(masked * value)
        vec_ref[:, part] = total_row(one)
        vec_ref[:, wide + column : wide + column + 256] = total_row(two)


def output_kernel(
    count_ref, sums_ref, vf_ref, vs_ref, vh_ref, fast_ref, cf_ref, cs_ref,
    af_ref, as_ref, ah_ref, mask_ref,
    yf_ref, ys_ref, gf_ref, gs_ref, total_ref, vec_ref, rows_ref, cots_ref,
):
    fast_count, slow_count = count_ref[0], count_ref[1]
    total = jnp.sum(sums_ref[...], axis=0)
    total_ref[...] = total
    wide = vs_ref.shape[1]
    ft, fq, st, sq, ht, hq = split(total, (128, 128, wide, wide, wide, wide))
    rows = vf_ref.shape[0]
    mean, inverse = mean_inverse(ft, fq, fast_count)
    mean, inverse = (jnp.concatenate([v] * ALPHA, 1) for v in (mean, inverse))
    scale, shift = line(mean, inverse, af_ref[...])

    frames, cells = fast_ref.shape[:2]
    step = frames * ALPHA
    cots_ref[...] = cf_ref[...].astype(F32)
    zero = jnp.zeros((8, 512), F32)
    beta = gamma = jnp.zeros((1, 128), F32)
    for frame in range(frames):
        now = slice(frame * cells, (frame + 1) * cells)
        for j in range(ALPHA):
            part = slice(j * 128, (j + 1) * 128)
            place = pl.ds(frame * ALPHA + j, cells, step)
            mask = mask_ref[now, :]
            value = vf_ref[now, part]
            z = value * scale[:, part] + shift[:, part] + fast_ref[frame, :, part].astype(F32)
            gate = gate_of(z)
            rows_ref[place, :] = mask * z * gate
            grad = cots_ref[place, :] * mask * gate * (1.0 + z * (1.0 - gate))
            gf_ref[now, part] = grad
            beta = beta + total_row(grad)
            gamma = gamma + total_row(grad * value)
    yf_ref[...] = rows_ref[...].astype(BF)
    pieces = [beta, (gamma - mean[:, :128] * beta) * inverse[:, :128]]
    mean_c, inverse_c = mean_inverse(st, sq, slow_count)
    mean_h, inverse_h = mean_inverse(ht, hq, slow_count)
    scale_c, shift_c = line(mean_c, inverse_c, as_ref[...])
    scale_h, shift_h = line(mean_h, inverse_h, ah_ref[...])
    betas, gammas, others = [], [], []
    for column in range(0, wide, 512):
        part = slice(column, column + 512)
        sc, sh, shift_both = scale_c[:, part], scale_h[:, part], shift_c[:, part] + shift_h[:, part]

        def body(rows_now, carry):
            third, short = vs_ref[rows_now, part].astype(F32), vh_ref[rows_now, part].astype(F32)
            mask = wide_mask(mask_ref[rows_now, :], 512)
            z = third * sc + short * sh + shift_both
            gate = gate_of(z)
            ys_ref[rows_now, part] = (mask * z * gate).astype(BF)
            grad = cs_ref[rows_now, part].astype(F32) * mask * gate * (1.0 + z * (1.0 - gate))
            gs_ref[rows_now, part] = grad.astype(BF)
            grad = grad.astype(BF).astype(F32)
            return (
                carry[0] + collapse(grad),
                carry[1] + collapse(grad * third),
                carry[2] + collapse(grad * short),
            )

        beta, gamma, other = (total_row(v) for v in loop_rows(rows, 16, body, (zero, zero, zero)))
        betas.append(beta)
        gammas.append((gamma - mean_c[:, part] * beta) * inverse_c[:, part])
        others.append((other - mean_h[:, part] * beta) * inverse_h[:, part])
    pieces += [jnp.concatenate(v, 1) for v in (betas, gammas, others)]
    send_all(vec_ref, pieces)


def back_line(mean, inverse, scale, beta, gamma, count):
    first = inverse * scale
    third = first * gamma * inverse / count
    return first, first * beta / count - mean * third, third


def narrow_kernel(
    count_ref, sums_ref, third_ref, second_ref,
    gf_ref, gs_ref, vf_ref, vs_ref, vh_ref, uf_ref, us_ref,
    afc_ref, asc_ref, ash_ref, afb_ref, asb_ref, mask_ref, wf_ref, ws_ref,
    df_ref, ds_ref, dh_ref, of_ref, os_ref, total_ref, vec_ref,
):
    fast_count, slow_count = count_ref[0], count_ref[1]
    total = jnp.sum(sums_ref[...], axis=0)
    total_ref[...] = total
    wide = vs_ref.shape[1]
    rows = vf_ref.shape[0]
    fast_beta, fast_gamma, beta, gamma_c, gamma_h = split(total, (128, 128, wide, wide, wide))
    ft, fq, st, sq, ht, hq = split(third_ref[...], (128, 128, wide, wide, wide, wide))
    mean, inverse = mean_inverse(ft, fq, fast_count)
    tiled = [jnp.concatenate([v] * ALPHA, 1) for v in (mean, inverse, fast_beta, fast_gamma)]
    f1, f2, f3 = back_line(tiled[0], tiled[1], afc_ref[0:1, :], tiled[2], tiled[3], fast_count)

    def fast_body(rows_now, carry):
        mask = wide_mask(mask_ref[rows_now, :], 512)
        grad = mask * (gf_ref[rows_now, :].astype(F32) * f1 - f2 - vf_ref[rows_now, :].astype(F32) * f3)
        df_ref[rows_now, :] = grad.astype(BF)
        return carry

    loop_rows(rows, 16, fast_body, 0)
    mean_c, inverse_c = mean_inverse(st, sq, slow_count)
    mean_h, inverse_h = mean_inverse(ht, hq, slow_count)
    lines_c = back_line(mean_c, inverse_c, asc_ref[0:1, :], beta, gamma_c, slow_count)
    lines_h = back_line(mean_h, inverse_h, ash_ref[0:1, :], beta, gamma_h, slow_count)
    for column in range(0, wide, 512):
        part = slice(column, column + 512)
        c1, c2, c3 = (v[:, part] for v in lines_c)
        h1, h2, h3 = (v[:, part] for v in lines_h)

        def body(rows_now, carry):
            mask = wide_mask(mask_ref[rows_now, :], 512)
            grad = gs_ref[rows_now, part].astype(F32)
            third, short = vs_ref[rows_now, part].astype(F32), vh_ref[rows_now, part].astype(F32)
            ds_ref[rows_now, part] = (mask * (grad * c1 - c2 - third * c3)).astype(BF)
            dh_ref[rows_now, part] = (mask * (grad * h1 - h2 - short * h3)).astype(BF)
            return carry

        loop_rows(rows, 16, body, 0)
    of_ref[...] = mm_t(df_ref[...], wf_ref[...])
    os_ref[...] = mm_t(ds_ref[...], ws_ref[...])
    ft, fq, st, sq = split(second_ref[...], (128, 128, 256, 256))
    pieces = slope_sums(
        (of_ref, uf_ref, afb_ref, fold_lanes(ft, ALPHA), fold_lanes(fq, ALPHA), fast_count),
        (os_ref, us_ref, asb_ref, st, sq, slow_count),
        mask_ref,
    )
    send_all(vec_ref, pieces)


def slope_sums(fast_parts, slow_parts, mask_ref):
    pieces = []
    for out_ref, value_ref, affine_ref, tot, square, count in (fast_parts, slow_parts):
        width = out_ref.shape[1]
        mean, inverse = mean_inverse(tot, square, count)
        scale, shift = line(mean, inverse, affine_ref[...])

        def body(rows_now, carry):
            value = value_ref[rows_now, :]
            z = value * scale + shift
            gate = gate_of(z)
            mask = wide_mask(mask_ref[rows_now, :], width)
            grad = out_ref[rows_now, :] * mask * gate * (1.0 + z * (1.0 - gate))
            out_ref[rows_now, :] = grad
            return carry[0] + collapse(grad), carry[1] + collapse(grad * value)

        zero = jnp.zeros((8, width), F32)
        rows = out_ref.shape[0]
        beta, gamma = (total_row(v) for v in loop_rows(rows, ROWS_STEP // 2, body, (zero, zero)))
        pieces += [beta, (gamma - mean * beta) * inverse]
    return pieces


def conv_back_kernel(
    count_ref, sums_ref, second_ref, first_ref,
    gf_ref, gs_ref, uf_ref, us_ref, vf_ref, vs_ref,
    afb_ref, asb_ref, afa_ref, asa_ref, mask_ref, edge_ref, wf_ref, ws_ref,
    df_ref, ds_ref, of_ref, os_ref, total_ref, vec_ref,
    bf_ref, bs_ref, pf_ref, ps_ref,
):
    fast_count, slow_count = count_ref[0], count_ref[1]
    total = jnp.sum(sums_ref[...], axis=0)
    total_ref[...] = total
    rows = gf_ref.shape[0]
    fast_beta, fast_gamma, beta, gamma = split(total, (128, 128, 256, 256))
    ft, fq, st, sq = split(second_ref[...], (128, 128, 256, 256))
    mean, inverse = mean_inverse(fold_lanes(ft, ALPHA), fold_lanes(fq, ALPHA), fast_count)
    fast_lines = back_line(
        mean, inverse, afb_ref[0:1, :], fold_lanes(fast_beta, ALPHA), fold_lanes(fast_gamma, ALPHA), fast_count
    )
    slow_lines = back_line(*mean_inverse(st, sq, slow_count), asb_ref[0:1, :], beta, gamma, slow_count)
    for grad_ref, value_ref, out_ref, buffer, lines in (
        (gf_ref, uf_ref, df_ref, bf_ref, fast_lines),
        (gs_ref, us_ref, ds_ref, bs_ref, slow_lines),
    ):
        width = grad_ref.shape[1]
        one, two, three = lines
        clear_margins(buffer)
        for start in range(0, rows, ROWS_STEP):
            now = slice(start, start + ROWS_STEP)
            grad = grad_ref[now, :] * one - two - value_ref[now, :] * three
            grad = grad * wide_mask(mask_ref[now, :], width)
            out_ref[now, :] = grad.astype(BF)
            buffer[MARGIN + start : MARGIN + start + ROWS_STEP, :] = grad
    write_patches(bf_ref, pf_ref, edge_ref)
    write_patches(bs_ref, ps_ref, edge_ref)
    of_ref[...] = mm(pf_ref[...], wf_ref[...])
    os_ref[...] = mm(ps_ref[...], ws_ref[...])
    ft, fq, st, sq = split(first_ref[...], (128, 128, 256, 256))
    pieces = slope_sums(
        (of_ref, vf_ref, afa_ref, fold_lanes(ft, ALPHA), fold_lanes(fq, ALPHA), fast_count),
        (os_ref, vs_ref, asa_ref, st, sq, slow_count),
        mask_ref,
    )
    send_all(vec_ref, pieces)


def local_call(us, kernel, counts, arrays, outs, scratch=()):
    vmem = pl.BlockSpec(memory_space=pltpu.VMEM)
    shapes = [(a.shape, a.dtype) for a in arrays] + list(outs) + list(scratch)
    need = sum(int(np.prod(shape)) * jnp.dtype(dtype).itemsize for shape, dtype in shapes)
    return pl.pallas_call(
        kernel,
        out_shape=[jax.ShapeDtypeStruct(s, d) for s, d in outs],
        in_specs=[vmem if counts.ndim > 1 else pl.BlockSpec(memory_space=pltpu.SMEM)]
        + [vmem] * len(arrays),
        out_specs=[vmem] * len(outs),
        scratch_shapes=[pltpu.VMEM(s, d) for s, d in scratch],
        compiler_params=pltpu.CompilerParams(vmem_limit_bytes=56 * 2**20),
        cost_estimate=cost(us),
    )(counts, *arrays)


def exchange(vec):
    return lax.all_to_all(vec, ("dp", "mp"), 0, 0, tiled=True)


def spread_columns(matrix, groups, step):
    last = (groups - 1) * step
    return jnp.concatenate(
        [jnp.pad(matrix, ((j * step, last - j * step), (0, 0))) for j in range(groups)], 1
    )


def per_device(
    fast_in,
    slow_in,
    clip_len,
    w_fast_a,
    w_fast_b,
    w_fast_c,
    w_lateral,
    w_slow_a,
    w_slow_b,
    w_slow_c,
    w_short,
    norm_fast_a,
    norm_fast_b,
    norm_fast_c,
    norm_slow_a,
    norm_slow_b,
    norm_slow_c,
    norm_short,
    cot_fast,
    cot_slow,
):
    batch, fast_frames, pixels, cf = fast_in.shape
    frames, cs = slow_in.shape[1], slow_in.shape[3]
    cells = batch * pixels
    ci = w_fast_a.shape[2]
    cl = w_lateral.shape[2]
    co = norm_slow_c.shape[1]
    cm = norm_slow_a.shape[1]
    cu = cs + cl
    mp = lax.axis_size("mp")
    me = lax.axis_index("mp")

    part, wide = w_slow_a.shape[2], w_short.shape[1]
    gather = start_gather(w_slow_a, w_slow_b, w_slow_c, w_short)

    lengths = lax.dynamic_slice_in_dim(clip_len[:, 0], lax.axis_index("dp") * batch, batch, 0)
    place = me * frames + jnp.arange(frames)
    mask = (place[:, None] < lengths[None, :]).astype(F32)
    mask = jnp.repeat(mask, pixels, axis=1)[:, :, None]
    slow_count = jnp.sum(clip_len).astype(F32) * pixels
    fast_count = slow_count * ALPHA

    rows = frames * cells
    flat_mask = jnp.broadcast_to(mask.reshape(rows, 1), (rows, 128))
    spot = np.arange(rows) % pixels
    edges = np.stack([spot >= W, spot < pixels - W, spot % W > 0, spot % W < W - 1])
    edges = jnp.asarray(np.repeat(edges.astype(np.float32)[:, :, None], 128, axis=2))
    counts = jnp.stack([fast_count, slow_count])
    devices = lax.axis_size("dp") * mp

    def flat(values):
        return values.reshape(rows, values.shape[-1])

    def framed(values):
        return values.reshape(frames, cells, values.shape[-1])

    def by_pixel(values):
        return values.transpose(0, 2, 1, 3).reshape(-1, values.shape[-1])

    def by_frame(values, count):
        return values.reshape(batch, pixels, count, values.shape[-1]).transpose(0, 2, 1, 3)

    def call(kernel, arrays, outs, scratch=(), first=None):
        return local_call(1, kernel, counts if first is None else first, arrays, outs, scratch)

    lane = ALPHA * ci
    fw = ALPHA * cf
    small = 2 * lane + 2 * cm
    core = (lax.axis_index("dp") % 2).astype(jnp.int32).reshape(1)
    joined_flat_shape = ((frames, cells, cu), BF)

    fast, tail, head = call(
        unpack_kernel,
        [by_pixel(fast_in)],
        [((frames, cells, fw), BF), ((cells, 2 * cf), BF), ((cells, cf), BF)],
        [((rows * ALPHA, cf), F32)],
        flat_mask,
    )
    before = shift_permute(tail, "mp", 1)
    following = shift_permute(head, "mp", -1)
    big_a = spread_columns(w_fast_a.reshape(3 * cf, ci), ALPHA, cf)
    fast_stack, lateral_stack, fast_first, fast_sums, joined = call(
        entry_kernel,
        [
            fast, before, following, slow_in.transpose(1, 0, 2, 3).reshape(frames, cells, cs),
            big_a, w_lateral.reshape(-1, cl),
        ],
        [
            ((frames, cells, 6 * cf), BF), ((frames, cells, 5 * cf), BF), ((rows, lane), F32),
            ((1, 2 * lane), F32), joined_flat_shape,
        ],
        first=flat_mask,
    )

    affine_fa = jnp.tile(norm_fast_a, (1, ALPHA))
    affine_fb = jnp.tile(norm_fast_b, (1, ALPHA))
    affine_fc = jnp.tile(norm_fast_c, (1, ALPHA))
    big_b = jnp.stack([spread_columns(w_fast_b[tap], ALPHA, ci) for tap in range(9)])
    big_b = big_b.reshape(-1, lane)
    big_c = spread_columns(w_fast_c, ALPHA, ci)
    prepared = (affine_fa, affine_fb, affine_fc, big_b, big_c)

    if small_mesh():
        near_bc = line_pieces(gather[1])
        pieces_a = both_sides(held(gather[0], joined))
        pieces_bc = both_sides(near_bc)
        near_short = line_pieces(gather[2])
        side_short = xor_permute(near_short, "mp", 1)
        wa_t = place_call(place_a, pieces_a, [(3 * cm, cu)])[0]
    else:
        wa_t = gather_a(gather[0], None)
    base, to_right, to_left = call(
        taps_kernel,
        [joined, wa_t],
        [((rows, cm), F32), ((cells, cm), BF), ((cells, cm), BF)],
        [((cells, 3 * cm), F32)] * 2,
        core,
    )
    left = shift_permute(to_right, "mp", 1)
    right = shift_permute(to_left, "mp", -1)
    left, right, prepared = lax.optimization_barrier((left, right, prepared))
    affine_fa, affine_fb, affine_fc, big_b, big_c = prepared
    slow_first, vec = call(
        first_sums_kernel,
        [base, left, right, fast_sums],
        [((rows, cm), F32), ((devices, 1, small), F32)],
        first=flat_mask,
    )
    if small_mesh():
        vec, pieces_bc = lax.optimization_barrier((vec, pieces_bc))
        wb, wb_back, wc = gather_bc(gather[1], None, pieces_bc)
        sums = held(exchange(vec), wb)
    else:
        wb, wb_back, wc = gather_bc(gather[1], gather[2], None)
        sums = exchange(vec)

    hidden_a, hidden_c, fast_second, slow_second, total_1, vec = call(
        conv_kernel,
        [sums, fast_first, slow_first, affine_fa, norm_slow_a, flat_mask, edges, big_b, wb],
        [
            ((rows, lane), BF), ((rows, cm), BF), ((rows, lane), F32), ((rows, cm), F32),
            ((1, small), F32), ((devices, 1, small), F32),
        ],
        [
            ((rows + 2 * MARGIN, lane), F32), ((rows + 2 * MARGIN, cm), F32),
            ((rows, 9 * lane), BF), ((rows, 9 * cm), BF),
        ],
    )

    if small_mesh():
        near_short, side_short = held((near_short, side_short), vec)
        pieces = near_short, side_short, swap_cores(near_short), swap_cores(side_short)
        ws = gather_short(gather[2], pieces)
    else:
        ws = gather_short(gather[3], None)
    shortcut, short_vec = call(
        short_kernel, [flat(joined), ws], [((rows, co), BF), ((1, 2 * co), F32)], first=flat_mask
    )
    sums = held(exchange(vec), short_vec)
    dp = lax.axis_size("dp")
    hidden_b, hidden_d, fast_third, slow_third, total_2, vec = call(
        expand_kernel,
        [sums, short_vec, fast_second, slow_second, affine_fb, norm_slow_b, flat_mask, big_c, wc],
        [
            ((rows, lane), BF), ((rows, cm), BF), ((rows, fw), F32), ((rows, co), BF),
            ((1, small), F32), ((dp, 1, 2 * cf + 4 * co), F32),
        ],
        [((rows, fw), F32), ((rows, co), F32)],
    )
    raw = held((cot_slow, w_fast_b, w_lateral, w_fast_a), vec)
    slow_cots = raw[0].transpose(1, 0, 2, 3).reshape(rows, co)
    big_b_back = jnp.concatenate(
        [spread_columns(raw[1][tap].T, ALPHA, ci) for tap in range(8, -1, -1)]
    )
    wl_t = jnp.swapaxes(raw[2], 1, 2)
    nothing = jnp.zeros_like(wl_t[0])
    big_lateral = jnp.concatenate(
        [
            jnp.concatenate([wl_t[2], wl_t[3], wl_t[4], nothing], 1),
            jnp.concatenate([nothing, nothing, wl_t[0], wl_t[1]], 1),
        ],
        0,
    )
    wfa_t = jnp.swapaxes(raw[3], 1, 2)[::-1].reshape(3 * ci, cf)
    big_back = jnp.pad(spread_columns(wfa_t, ALPHA, ci), ((lane - ci, lane - ci), (0, 0)))
    prepared = (slow_cots, big_b_back, big_lateral, big_back)
    sums = lax.all_to_all(vec, "dp", 0, 0, tiled=True)
    (vec,) = call(sum_kernel, [sums], [((mp, 1, vec.shape[2]), F32)], first=core)
    sums = lax.all_to_all(vec, "mp", 0, 0, tiled=True)
    sums, prepared = lax.optimization_barrier((sums, prepared))
    slow_cots, big_b_back, big_lateral, big_back = prepared

    fast_out, slow_out, fast_cot, slow_cot, total_3, vec = call(
        output_kernel,
        [
            sums, fast_third, slow_third, shortcut, fast, by_pixel(cot_fast), slow_cots,
            affine_fc, norm_slow_c, norm_short, flat_mask,
        ],
        [
            ((rows * ALPHA, cf), BF), ((rows, co), BF), ((rows, fw), F32), ((rows, co), BF),
            ((1, 2 * cf + 4 * co), F32), ((devices, 1, 2 * cf + 3 * co), F32),
        ],
        [((rows * ALPHA, cf), F32)] * 2,
    )
    slow_out = slow_out.reshape(frames, batch, pixels, co).transpose(1, 0, 2, 3)
    sums = held(exchange(vec), slow_out)

    d_fast_third, d_slow_third, d_short, grad_fb, grad_sb, total_4, vec = call(
        narrow_kernel,
        [
            sums, total_3, total_2, fast_cot, slow_cot, fast_third, slow_third, shortcut,
            fast_second, slow_second, affine_fc, norm_slow_c, norm_short, affine_fb, norm_slow_b,
            flat_mask, big_c, wc,
        ],
        [
            ((rows, fw), BF), ((rows, co), BF), ((rows, co), BF), ((rows, lane), F32),
            ((rows, cm), F32), ((1, 2 * cf + 3 * co), F32), ((devices, 1, small), F32),
        ],
    )

    def weight_grad(kernel, arrays, size, length, total, scratch=()):
        halves = ((mp, size, length), BF)
        return call(kernel, arrays, [halves, halves], [((total, length), BF), *scratch], core)

    if small_mesh():
        raw_cs = weight_grad(
            grad_cs_kernel, [d_short, d_slow_third, flat(joined), hidden_d], wide // 2, cu + cm, co
        )
        sums, raw_cs = lax.optimization_barrier((exchange(vec), raw_cs))
        sent_cs = swap_cores(raw_cs[0])
    else:
        raw_cs = jnp.concatenate(
            [rows_dot(framed(d_short), joined), rows_dot(framed(d_slow_third), framed(hidden_d))], -1
        )
        sum_cs = reduce_whole(raw_cs.reshape(mp, 2, wide // 2, cu + cm))
        sums = exchange(vec)

    d_fast_second, d_slow_second, grad_fa, grad_sa, total_5, vec = call(
        conv_back_kernel,
        [
            sums, total_2, total_1, grad_fb, grad_sb, fast_second, slow_second, fast_first,
            slow_first, affine_fb, norm_slow_b, affine_fa, norm_slow_a, flat_mask, edges,
            big_b_back, wb_back,
        ],
        [
            ((rows, lane), BF), ((rows, cm), BF), ((rows, lane), F32), ((rows, cm), F32),
            ((1, small), F32), ((devices, 1, small), F32),
        ],
        [
            ((rows + 2 * MARGIN, lane), F32), ((rows + 2 * MARGIN, cm), F32),
            ((rows, 9 * lane), BF), ((rows, 9 * cm), BF),
        ],
    )
    if small_mesh():
        raw_b = weight_grad(
            grad_b_kernel, [d_slow_second, hidden_c, edges], part // 2, 9 * cm, cm,
            [((rows + 2 * MARGIN, cm), F32), ((rows, 9 * cm), BF)],
        )
        sums, raw_b = lax.optimization_barrier((exchange(vec), raw_b))
        sent_b = swap_cores(raw_b[0])
    else:
        (raw_b,) = call(
            grad_b_whole_kernel,
            [d_slow_second, hidden_c, edges],
            [((cm, 9 * cm), F32)],
            [((rows + 2 * MARGIN, cm), F32), ((rows, 9 * cm), BF)],
            core,
        )
        sum_b = reduce_whole(raw_b.reshape(mp, 2, part // 2, 9 * cm))
        sums = exchange(vec)
    d_first, d_second, total_6 = call(
        first_kernel,
        [sums, total_1, grad_fa, grad_sa, fast_first, slow_first, affine_fa, norm_slow_a, flat_mask],
        [((cells, cm + lane), BF)] * 2 + [((1, small), F32)],
    )
    d_before = shift_permute(d_second, "mp", 1)
    d_after = shift_permute(d_first, "mp", -1)
    d_parts = [d_first, d_second, d_before, d_after]
    if small_mesh():
        chips_csb = cross_cores((sent_cs, sent_b), held((raw_cs[1], raw_b[1]), d_first))
        raw_a = weight_grad(
            grad_a_kernel, held(d_parts, chips_csb) + [joined], 3 * part // 2, cu, 3 * cm
        )
        sent_a = swap_cores(raw_a[0])
        d_parts = held(d_parts, raw_a)
    else:
        three = jnp.stack(
            [
                jnp.concatenate([d_second, d_after]),
                jnp.concatenate([d_first, d_second]),
                jnp.concatenate([d_before, d_first]),
            ]
        )[:, :, :cm]
        raw_a = jnp.einsum("kro,rc->koc", three, flat(joined), preferred_element_type=F32)
        raw_a = raw_a.reshape(3, mp, 2, part // 2, cu).transpose(1, 2, 0, 3, 4)
        sum_a = reduce_whole(raw_a.reshape(mp, 2, 3 * part // 2, cu))
    grad_slow_in, d_lateral = call(
        joined_back_kernel,
        d_parts + [framed(d_short), wa_t, ws],
        [((rows, cs), BF), ((frames, cells, cl), BF)],
        [((cs // 128, rows, 128), F32)],
        flat_mask,
    )
    lateral_after = shift_permute(d_lateral[0], "mp", -1)
    if small_mesh():
        chips_a = cross_cores((sent_a,), held((raw_a[1],), d_lateral))
        d_lateral = held(d_lateral, chips_a)
    (raw_fast,) = call(
        fast_grads_kernel,
        [
            fast_stack, d_first, d_second, hidden_a, d_fast_second, hidden_b, d_fast_third,
            lateral_stack, d_lateral, edges,
        ],
        [((2048, 128), BF)],
        [((rows + 2 * MARGIN, lane), F32), ((rows, 9 * lane), BF)],
        core,
    )
    (grad_fast_in,) = call(
        fast_back_kernel,
        d_parts + [d_lateral, held(lateral_after, raw_fast), fast_cot, big_lateral, big_back],
        [((rows * ALPHA, cf), BF)],
        [((rows * ALPHA, cf), F32)],
        flat_mask,
    )
    grad_slow_in = by_frame(grad_slow_in, frames)
    if small_mesh():
        lines_csb = cross_chips(chips_csb[0], held(chips_csb[1], (grad_fast_in, grad_slow_in)))
        lines_a = cross_chips(chips_a[0], held(chips_a[1], lines_csb))
        line_csb = cross_lines(lines_csb[0], held(lines_csb[1], lines_a))
        line_a = cross_lines(lines_a[0], held(lines_a[1], line_csb))
        total_csb = along_line([held(line_csb[0], line_a), *line_csb[1:]])
        total_a = along_line([held(line_a[0], total_csb), *line_a[1:]])
        sum_cs, sum_b = cross_clips(total_csb, [(wide // 2, cu + cm), (part // 2, 9 * cm)])
        (sum_a,) = cross_clips(total_a, [(3 * part // 2, cu)])
    raw_fast = sum_everywhere(raw_fast)
    row = 3 * cf + 10 * ci
    fast_a = raw_fast[: 3 * cf, :ci].reshape(3, cf, ci)
    fast_b = raw_fast[3 * cf : row - ci, :ci].reshape(9, ci, ci)
    fast_c = raw_fast[row - ci : row]
    grad_lateral = jnp.concatenate(
        [raw_fast[row : row + 5 * cf], raw_fast[row + 5 * cf : row + 10 * cf]], 1
    )
    sum_cs = sum_cs.reshape(wide, cu + cm)
    sum_b = sum_b.reshape(part, 9, cm)
    sum_a = sum_a.reshape(2, 3, part // 2, cu).transpose(1, 0, 2, 3).reshape(3, part, cu)

    def small_norms(total):
        fast_part = jnp.stack([folded(total[0, lane : 2 * lane], ALPHA), folded(total[0, :lane], ALPHA)])
        slow_part = jnp.stack([total[0, 2 * lane + cm :], total[0, 2 * lane : 2 * lane + cm]])
        return fast_part, slow_part

    grad_norm_fast_c = jnp.concatenate([total_4[:, cf : 2 * cf], total_4[:, :cf]])
    betas = total_4[:, 2 * cf : 2 * cf + co]
    grad_norm_slow_c = jnp.concatenate([total_4[:, 2 * cf + co : 2 * cf + 2 * co], betas])
    grad_norm_short = jnp.concatenate([total_4[:, 2 * cf + 2 * co :], betas])
    grad_norm_fast_b, grad_norm_slow_b = small_norms(total_5)
    grad_norm_fast_a, grad_norm_slow_a = small_norms(total_6)

    return (
        by_frame(fast_out, fast_frames),
        slow_out,
        by_frame(grad_fast_in, fast_frames),
        grad_slow_in,
        fast_a,
        fast_b,
        fast_c,
        grad_lateral.reshape(5, cf, cl),
        jnp.swapaxes(sum_a, 1, 2),
        sum_b.transpose(1, 2, 0),
        sum_cs[:, cu:].T,
        sum_cs[:, :cu].T,
        grad_norm_fast_a,
        grad_norm_fast_b,
        grad_norm_fast_c,
        grad_norm_slow_a,
        grad_norm_slow_b,
        grad_norm_slow_c,
        grad_norm_short,
    )


def solution(mesh):
    frames = P("dp", "mp", None, None)
    last = P(None, None, "mp")
    wide = P(None, "mp")
    return jax.shard_map(
        per_device,
        mesh=mesh,
        in_specs=(frames, frames, P(), P(), P(), P(), P(), last, last, wide, wide)
        + (P(),) * 7
        + (frames, frames),
        out_specs=(frames,) * 4 + (P(),) * 4 + (last, last, wide, wide) + (P(),) * 7,
        check_vma=False,
    )
```

```python
import functools

import jax
import jax.numpy as jnp
import numpy as np
from jax import lax
from jax.experimental import pallas as pl
from jax.experimental.pallas import tpu as pltpu
from jax.sharding import PartitionSpec as P

H = 14
W = 14
ALPHA = 4
NORM_EPSILON = 1e-05
BF = jnp.bfloat16
F32 = jnp.float32


def xor_permute(values, axis, bits):
    count = lax.axis_size(axis)
    return lax.ppermute(values, axis, [(i, i ^ bits) for i in range(count)])


def shift_permute(values, axis, step):
    count = lax.axis_size(axis)
    return lax.ppermute(
        values, axis, [(i, i + step) for i in range(count) if 0 <= i + step < count]
    )


def small_mesh():
    return lax.axis_size("dp") == 4 and lax.axis_size("mp") == 8


def pick(values, index, axis):
    return lax.dynamic_index_in_dim(values, index, axis, keepdims=False)


FREE = pl.CostEstimate(flops=0, bytes_accessed=1, transcendentals=0)
VMEM = pl.BlockSpec(memory_space=pltpu.VMEM)
SMEM = pl.BlockSpec(memory_space=pltpu.SMEM)
LARGE = 56 * 2**20
SMALL = 16 * 2**20


class Sync:
    def __init__(self, copies_in, copies_out):
        self.copies_in, self.copies_out = copies_in, copies_out

    def arrive(self, *places):
        for place in places:
            self.copies_in[place].wait()

    def send(self, *places):
        for place in places:
            self.copies_out[place].start()


def local_call(
    kernel, scalars, arrays, outs, scratch=(), limit=LARGE, out_specs=None, late=(), early=()
):
    count, total = len(scalars), len(arrays)
    anywhere = pl.BlockSpec(memory_space=pl.ANY)
    in_specs = [SMEM] * count + [anywhere if k in late else VMEM for k in range(total)]
    out_specs = out_specs or [anywhere if k in early else VMEM for k in range(len(outs))]
    own = [pltpu.VMEM(s, d) for s, d in scratch]
    buffers = [pltpu.VMEM(arrays[k].shape, arrays[k].dtype) for k in late]
    buffers += [pltpu.VMEM(*outs[k]) for k in early]

    def body(*refs):
        refs = list(refs)
        first_out = count + total
        sems = refs.pop()
        spare = refs[len(refs) - len(buffers) :]
        refs = refs[: len(refs) - len(buffers)]
        copies_in, copies_out = {}, {}
        for i, k in enumerate(late):
            copies_in[k] = pltpu.make_async_copy(refs[count + k], spare[i], sems.at[i])
            copies_in[k].start()
            refs[count + k] = spare[i]
        for i, k in enumerate(early, len(late)):
            copies_out[k] = pltpu.make_async_copy(spare[i], refs[first_out + k], sems.at[i])
            refs[first_out + k] = spare[i]
        kernel(*refs, sync=Sync(copies_in, copies_out))
        for copy in copies_out.values():
            copy.wait()

    moved = len(late) + len(early)
    return pl.pallas_call(
        body if moved else kernel,
        out_shape=[jax.ShapeDtypeStruct(s, d) for s, d in outs],
        in_specs=in_specs,
        out_specs=out_specs,
        scratch_shapes=own + buffers + ([pltpu.SemaphoreType.DMA((moved,))] if moved else []),
        compiler_params=pltpu.CompilerParams(vmem_limit_bytes=limit),
        cost_estimate=FREE,
    )(*scalars, *arrays)


def quick_call(kernel, arrays, outs):
    return local_call(kernel, [], arrays, outs, limit=SMALL)


def this_core():
    return lax.rem(lax.axis_index("dp"), 2)


def place_call(kernel, pieces, outs):
    def body(*refs):
        me, core = lax.axis_index("mp"), this_core()
        side = lax.rem(me, 2)
        for k in range(4):
            owner_side = side if k % 2 == 0 else 1 - side
            half = core if k < 2 else 1 - core
            for far in range(4):
                line = jnp.bitwise_xor(me - side, 2 * far)
                kernel(line + owner_side, half, refs[k].at[far], *refs[4:])

    return local_call(body, [], pieces, [(shape, BF) for shape in outs], limit=32 * 2**20)


def stack_kernel(*refs):
    for k, ref in enumerate(refs[:-1]):
        refs[-1][k] = ref[...]


def line_pieces(mine):
    return [mine] + [xor_permute(mine, "mp", 2 * step) for step in (1, 2, 3)]


def stacked(pieces):
    return quick_call(stack_kernel, pieces, [((4,) + pieces[0].shape, BF)])[0]


def both_sides(near):
    side = xor_permute(near, "mp", 1)
    return near, side, xor_permute(near, "dp", 1), xor_permute(side, "dp", 1)


def place_a(block, half, piece, out):
    part = piece.shape[0] // 3
    width = out.shape[0] // 3
    for tap in range(3):
        start = pl.multiple_of(tap * width + block * (2 * part) + half * part, part)
        out[pl.ds(start, part), :] = piece[tap * part : (tap + 1) * part, :]


def place_bc(block, half, piece, out_f, out_b, out_c):
    width = out_f.shape[0]
    part = width // 16
    for tap in range(9):
        values = piece[tap * part : (tap + 1) * part, :]
        start = pl.multiple_of(block * (2 * part) + half * part, part)
        out_f[pl.ds(start, part), tap * width : (tap + 1) * width] = values
        start = pl.multiple_of((8 - tap) * width + block * (2 * part) + half * part, part)
        out_b[pl.ds(start, part), :] = values
    rest = piece.shape[0] - 9 * part
    columns = pl.ds(pl.multiple_of(block * 128, 128), 128)
    for k in range(2):
        start = pl.multiple_of(half * (2 * rest) + k * rest, rest)
        out_c[pl.ds(start, rest), columns] = piece[9 * part :, k * 128 : (k + 1) * 128]


def place_short(block, half, piece, out):
    part = piece.shape[0]
    columns = pl.ds(pl.multiple_of(block * 128, 128), 128)
    out[pl.ds(pl.multiple_of(half * part, part), part), columns] = piece[...]


def held(values, other):
    return lax.optimization_barrier((values, other))[0]


def shards_kernel(a_ref, b_ref, c_ref, s_ref, a_out, bc_out, s_out):
    core = this_core()
    half = a_ref.shape[1] // 2
    mine = pl.ds(pl.multiple_of(core * half, half), half)
    for tap in range(3):
        a_out[tap * half : (tap + 1) * half, :] = a_ref[tap, mine, :]
    for tap in range(9):
        bc_out[tap * half : (tap + 1) * half, :] = b_ref[tap, mine, :]
    rest = c_ref.shape[0] // 4
    for k in range(2):
        rows = pl.ds(pl.multiple_of(core * (2 * rest) + k * rest, rest), rest)
        bc_out[9 * half :, k * 128 : (k + 1) * 128] = c_ref[rows, :]
    size = s_out.shape[0]
    s_out[...] = s_ref[pl.ds(pl.multiple_of(core * size, size), size), :]


def own_halves(a_t, b_t, w_slow_c, w_short):
    half, cu = a_t.shape[1] // 2, a_t.shape[2]
    cm = b_t.shape[2]
    outs = [((3 * half, cu), BF), ((9 * half + cm // 4, cm), BF), ((cu // 2, 128), BF)]
    return quick_call(shards_kernel, [a_t, b_t, w_slow_c, w_short], outs)


def gather_whole(a_t, b_t, w_slow_c, w_short):
    wa = lax.all_gather(a_t, "mp", axis=1, tiled=True)
    wb = lax.all_gather(b_t, "mp", axis=1, tiled=True)
    wc = lax.all_gather(w_slow_c, "mp", axis=1, tiled=True)
    ws = lax.all_gather(w_short, "mp", axis=1, tiled=True)
    cm = wb.shape[1]
    wb_back = wb[::-1].reshape(9 * cm, cm)
    return wa.reshape(-1, wa.shape[2]), wb.transpose(1, 0, 2).reshape(cm, 9 * cm), wb_back, wc, ws


def plus(*values):
    total = values[0].astype(F32)
    for value in values[1:]:
        total = total + value.astype(F32)
    return total.astype(BF)


def columns_of(index, width):
    return pl.ds(pl.multiple_of(index * width, 128), width)


def swap_cores(send):
    return xor_permute(send, "dp", 1)


def row_groups(rows, width):
    return [(row, row // 16 * width) for row in range(0, rows, 16)]


def merge_kernel(*refs):
    count = len(refs) // 2 - 1
    keeps, sents, (far_ref, near_ref) = refs[:count], refs[count:-2], refs[-2:]
    x = lax.axis_index("dp") // 2
    first = 0
    for keep, sent in zip(keeps, sents):
        width = keep.shape[2] // 2
        for row, start in row_groups(keep.shape[1], width):
            place = slice(first + start, first + start + width)
            for index, out_ref in ((x, near_ref), (1 - x, far_ref)):
                columns = columns_of(index, width)
                out_ref[:, :, place] = plus(
                    keep[:, row : row + 16, columns], sent[:, row : row + 16, columns]
                )
        first += keep.shape[1] // 16 * width


def turn_kernel(near_ref, sent_ref, far_y_ref, near_y_ref):
    side = lax.rem(lax.axis_index("mp"), 2)
    for line in range(4):
        for near, out_ref in ((side, near_y_ref), (1 - side, far_y_ref)):
            block = 2 * line + near
            out_ref[line] = plus(near_ref[block], sent_ref[block])


def lines_kernel(near_1, sent_1, near_2, sent_2, *out_refs):
    mine = lax.axis_index("mp") // 2
    width = near_1.shape[2]
    for step, out_ref in enumerate(out_refs):
        place = jnp.bitwise_xor(mine, step)
        out_ref[:, :width] = plus(near_1[place], sent_1[place])
        out_ref[:, width:] = plus(near_2[place], sent_2[place])


def along_kernel(*refs):
    main_ref, fast_ref = refs[-2:]
    width = main_ref.shape[1]
    main_ref[...] = plus(*[ref[:, :width] for ref in refs[:-2]])
    fast = plus(*[ref[:, width:] for ref in refs[:-2]])
    fast_ref[...] = jnp.broadcast_to(fast[None], fast_ref.shape)


def merge(keeps, sents):
    columns = sum(keep.shape[1] // 16 * keep.shape[2] // 2 for keep in keeps)
    return quick_call(merge_kernel, [*keeps, *sents], [((8, 16, columns), BF)] * 2)


def turn(far, near):
    outs = [((4,) + near.shape[1:], BF)] * 2
    return quick_call(turn_kernel, [near, xor_permute(far, "dp", 2)], outs)


def cut_lines(first, second):
    arrays = []
    for far, near in (first, second):
        arrays += [near, xor_permute(far, "mp", 1)]
    columns = first[1].shape[2] + second[1].shape[2]
    return quick_call(lines_kernel, arrays, [((16, columns), BF)] * 4)


def along_line(mine, sent, width):
    outs = [((16, width), BF), ((32, 16, mine.shape[1] - width), BF)]
    return quick_call(along_kernel, [mine, *sent], outs)


def clip_values(refs):
    core, x = this_core(), lax.axis_index("dp") // 2
    places = ((core, x), (core, 1 - x), (1 - core, x), (1 - core, 1 - x))
    return [(half, side, ref) for (half, side), ref in zip(places, refs)]


def clips_kernel(
    mine_ref, far_ref, other_ref, far_other_ref, c_ref, s_ref, b_ref, a_ref, block_ref
):
    cu = s_ref.shape[0]
    wide = block_ref.shape[1] // 2
    half_rows = block_ref.shape[0] // 2
    for half, side, ref in clip_values((mine_ref, far_ref, other_ref, far_other_ref)):
        for group in range(half_rows // 16):
            rows = pl.ds(pl.multiple_of(half * half_rows + group * 16, 16), 16)
            values = ref[:, group * wide : (group + 1) * wide].astype(F32)
            block_ref[rows, columns_of(side, wide)] = values
        start = half_rows // 16 * wide
        count = b_ref.shape[0] * b_ref.shape[2] // 256
        rows = pl.ds(pl.multiple_of(half * 16, 16), 16)
        for k in range(count):
            unit = side * count + k
            columns = pl.ds(pl.multiple_of(lax.rem(unit, 2) * 128, 128), 128)
            values = ref[:, start + k * 128 : start + (k + 1) * 128].astype(F32)
            b_ref[unit // 2, rows, columns] = values
        start += count * 128
        part = a_ref.shape[2] // 2
        for tap in range(3):
            values = ref[:, start + tap * part : start + (tap + 1) * part].astype(F32)
            a_ref[tap, rows, columns_of(side, part)] = values
    for column in range(0, cu, 128):
        s_ref[column : column + 128, :] = block_ref[:, column : column + 128].T
    for column in range(cu, block_ref.shape[1], 128):
        c_ref[column - cu : column - cu + 128, :] = block_ref[:, column : column + 128].T


def cross_clips(total, outs, scratch, other):
    sent = [xor_permute(total, "dp", bits) for bits in (2, 1, 3)]
    arrays = [held(total, other), *sent]
    return local_call(clips_kernel, [], arrays, [(shape, F32) for shape in outs], scratch, SMALL)


def reduce_whole(blocks):
    whole = lax.psum(blocks.astype(BF), "dp")
    return lax.psum_scatter(whole, "mp", scatter_dimension=0, tiled=True)[0].astype(F32)


def tn(left, right):
    return lax.dot_general(left, right, (((0,), (0,)), ((), ())), preferred_element_type=F32)


def cut_halves(core, whole_ref, send_ref, keep_ref, groups=1):
    blocks, size = keep_ref.shape[0], keep_ref.shape[1] // groups
    for group in range(groups):
        for block in range(blocks):
            start = (group * blocks + block) * 2 * size
            place = slice(group * size, (group + 1) * size)
            send_ref[block, place, :] = whole_ref[pl.ds(pl.multiple_of(start + (1 - core) * size, size), size), :]
            keep_ref[block, place, :] = whole_ref[pl.ds(pl.multiple_of(start + core * size, size), size), :]


def grad_cs_kernel(dh_ref, ds_ref, joined_ref, hidden_ref, send_ref, keep_ref, whole_ref):
    wide, cu = dh_ref.shape[1], joined_ref.shape[1]
    for start in range(0, wide, 256):
        part = slice(start, start + 256)
        whole_ref[part, 0:cu] = tn(dh_ref[:, part], joined_ref[...]).astype(BF)
    whole_ref[:, cu:] = tn(ds_ref[...], hidden_ref[...]).astype(BF)
    cut_halves(this_core(), whole_ref, send_ref, keep_ref)


def fill_buffer(buffer, values_ref):
    clear_margins(buffer)
    for start in range(0, values_ref.shape[0], ROWS_STEP):
        rows = values_ref[start : start + ROWS_STEP, :].astype(F32)
        buffer[MARGIN + start : MARGIN + start + ROWS_STEP, :] = rows


def grad_b_kernel(
    ds_ref, hidden_ref, edge_ref, send_ref, keep_ref, whole_ref, buffer_ref, patches_ref
):
    fill_buffer(buffer_ref, hidden_ref)
    write_patches(buffer_ref, patches_ref, edge_ref)
    whole_ref[...] = tn(ds_ref[...], patches_ref[...]).astype(BF)
    cut_halves(this_core(), whole_ref, send_ref, keep_ref)


def grad_b_whole_kernel(
    ds_ref, hidden_ref, edge_ref, out_ref, buffer_ref, patches_ref
):
    fill_buffer(buffer_ref, hidden_ref)
    write_patches(buffer_ref, patches_ref, edge_ref)
    out_ref[...] = tn(ds_ref[...], patches_ref[...])


def grad_a_kernel(
    one_ref, two_ref, before_ref, after_ref, joined_ref, send_ref, keep_ref, whole_ref
):
    cm = whole_ref.shape[0] // 3
    pairs = ((two_ref, after_ref), (one_ref, two_ref), (before_ref, one_ref))
    for tap, (left_ref, right_ref) in enumerate(pairs):
        total = tn(left_ref[:, :cm], joined_ref[0]) + tn(right_ref[...], joined_ref[1])
        whole_ref[tap * cm : (tap + 1) * cm, :] = total.astype(BF)
    cut_halves(this_core(), whole_ref, send_ref, keep_ref, 3)


def leftward(values, j):
    return pltpu.roll(values, 128 - j * (128 // ALPHA), 1) if j else values


def fast_inner_kernel(
    hidden_a_ref, second_ref, hidden_ref, third_ref, edge_ref, out_ref, buffer_ref, patches_ref
):
    ci, cf = 128 // ALPHA, 128
    fill_buffer(buffer_ref, hidden_a_ref)
    write_patches(buffer_ref, patches_ref, edge_ref)
    raw = tn(patches_ref[...], second_ref[...])
    for tap in range(9):
        total = sum(
            leftward(raw[tap * 128 + j * ci : tap * 128 + (j + 1) * ci, :], j) for j in range(ALPHA)
        )
        out_ref[tap * ci : (tap + 1) * ci, :] = total.astype(BF)
    raw = tn(hidden_ref[...], third_ref[...])
    out_ref[9 * ci :, :] = sum(
        raw[j * ci : (j + 1) * ci, j * cf : (j + 1) * cf] for j in range(ALPHA)
    ).astype(BF)


def fast_outer_kernel(
    stack_ref, one_ref, two_ref, lateral_ref, dl_ref, inner_ref, send_ref, keep_ref, whole_ref
):
    cf = 128
    raw = tn(stack_ref[0], one_ref[...]) + tn(stack_ref[1], two_ref[...])
    whole_ref[0 : 3 * cf, :] = sum(
        leftward(raw[j * cf : (j + 3) * cf, :], j) for j in range(ALPHA)
    ).astype(BF)
    start = 3 * cf
    count = inner_ref.shape[0]
    whole_ref[start : start + count, :] = inner_ref[...]
    start += count
    raw = tn(lateral_ref[0], dl_ref[0]) + tn(lateral_ref[1], dl_ref[1])
    size = raw.shape[0]
    whole_ref[start : start + size, :] = raw[:, :128].astype(BF)
    whole_ref[start + size : start + 2 * size, :] = raw[:, 128:].astype(BF)
    start += 2 * size
    whole_ref[start:, :] = jnp.zeros((whole_ref.shape[0] - start, 128), BF)
    core = this_core()
    for half, out_ref in ((core, keep_ref), (1 - core, send_ref)):
        for block in range(8):
            for group in range(8):
                row = half * 1024 + block * 128 + group * 16
                rows = pl.ds(pl.multiple_of(row, 16), 16)
                out_ref[block, :, group * 128 : (group + 1) * 128] = whole_ref[rows, :]


def fast_whole_kernel(stack_ref, one_ref, two_ref, lateral_ref, dl_ref, inner_ref, out_ref):
    cf = 128
    raw = tn(stack_ref[0], one_ref[...]) + tn(stack_ref[1], two_ref[...])
    out_ref[0 : 3 * cf, :] = sum(leftward(raw[j * cf : (j + 3) * cf, :], j) for j in range(ALPHA))
    start = 3 * cf
    out_ref[start : start + inner_ref.shape[0], :] = inner_ref[...].astype(F32)
    start += inner_ref.shape[0]
    raw = tn(lateral_ref[0], dl_ref[0]) + tn(lateral_ref[1], dl_ref[1])
    size = raw.shape[0]
    out_ref[start : start + size, :] = raw[:, :128]
    out_ref[start + size : start + 2 * size, :] = raw[:, 128:]
    start += 2 * size
    out_ref[start:, :] = jnp.zeros((out_ref.shape[0] - start, 128), F32)


def first_kernel(
    count_ref, sums_ref, first_ref, gf_ref, gs_ref, vf_ref, vs_ref, afa_ref, asa_ref, mask_ref,
    f0_ref, f1_ref, s0_ref, s1_ref, right_ref, total_ref, tile_ref,
):
    fast_count, slow_count = count_ref[0], count_ref[1]
    total = jnp.sum(sums_ref[...], axis=0)
    total_ref[...] = total
    cells = f0_ref.shape[0]
    fast_beta, fast_gamma, beta, gamma = split(total, (128, 128, 256, 256))
    ft, fq, st, sq = split(first_ref[...], (128, 128, 256, 256))
    mean, inverse = mean_inverse(fold_lanes(ft, ALPHA), fold_lanes(fq, ALPHA), fast_count)
    fast_lines = back_line(
        mean, inverse, tiled_affine(afa_ref, tile_ref)[0:1], fold_lanes(fast_beta, ALPHA), fold_lanes(fast_gamma, ALPHA), fast_count
    )
    slow_lines = back_line(*mean_inverse(st, sq, slow_count), asa_ref[0:1, :], beta, gamma, slow_count)
    for grad_ref, value_ref, outs, (one, two, three) in (
        (gf_ref, vf_ref, (f0_ref, f1_ref), fast_lines),
        (gs_ref, vs_ref, (s0_ref, s1_ref), slow_lines),
    ):
        for frame, out_ref in enumerate(outs):
            now = slice(frame * cells, (frame + 1) * cells)
            mask = wide_mask(mask_ref[now, :], grad_ref.shape[1])
            grad = mask * (grad_ref[now, :] * one - two - value_ref[now, :] * three)
            out_ref[...] = grad.astype(BF)
            if frame:
                start = 0 if out_ref is s1_ref else s1_ref.shape[1]
                right_ref[:, start : start + out_ref.shape[1]] = grad.astype(BF)


def joined_back_kernel(
    mask_ref, one_ref, two_ref, before_ref, after_ref, dh_ref, wa_ref, ws_ref, out_ref
):
    cells = one_ref.shape[0]
    cs = out_ref.shape[2]
    cm = wa_ref.shape[0] // 3
    for frame, pieces in enumerate(
        ((two_ref, one_ref, before_ref), (after_ref, two_ref, one_ref))
    ):
        mask = mask_ref[frame * cells : (frame + 1) * cells, :]
        taps = jnp.concatenate([piece[:, :cm] for piece in pieces], axis=1)
        for start in range(0, cs, 256):
            part = slice(start, start + 256)
            grad = mm(taps, wa_ref[:, part]) + mm_t(dh_ref[frame], ws_ref[part, :])
            out_ref[:, frame, part] = (grad * wide_mask(mask, 256)).astype(BF)


def lateral_back_kernel(
    mask_ref, one_ref, two_ref, before_ref, after_ref, fast_ref, dh_ref, wa_ref, ws_ref,
    lat_ref, edge_ref, a_ref, s_ref, sems,
):
    cells, cl = one_ref.shape[0], lat_ref.shape[2]
    cm = wa_ref.shape[0] // 3
    cs = ws_ref.shape[0] - cl
    copies = [
        pltpu.make_async_copy(wa_ref.at[:, pl.ds(cs, cl)], a_ref, sems.at[0]),
        pltpu.make_async_copy(ws_ref.at[pl.ds(cs, cl), :], s_ref, sems.at[1]),
    ]
    for copy in copies:
        copy.start()
    for copy in copies:
        copy.wait()
    for frame, pieces in enumerate(
        ((two_ref, one_ref, before_ref), (after_ref, two_ref, one_ref))
    ):
        mask = mask_ref[frame * cells : (frame + 1) * cells, :]
        taps = jnp.concatenate([piece[:, :cm] for piece in pieces], axis=1)
        grad = mm(taps, a_ref[...]) + mm_t(dh_ref[frame], s_ref[...])
        grad = (grad * wide_mask(mask, cl)).astype(BF)
        lat_ref[frame] = grad
        if frame == 0:
            edge_ref[:, :cl] = grad
            edge_ref[:, cl:] = fast_ref[...]


def lateral_back(arrays, outs):
    wa, ws = arrays[-2:]
    cl = outs[0][0][2]
    anywhere = pl.BlockSpec(memory_space=pl.ANY)
    return pl.pallas_call(
        lateral_back_kernel,
        out_shape=[jax.ShapeDtypeStruct(s, d) for s, d in outs],
        in_specs=[VMEM] * (len(arrays) - 2) + [anywhere] * 2,
        out_specs=[VMEM] * len(outs),
        scratch_shapes=[
            pltpu.VMEM((wa.shape[0], cl), BF),
            pltpu.VMEM((cl, ws.shape[1]), BF),
            pltpu.SemaphoreType.DMA((2,)),
        ],
        compiler_params=pltpu.CompilerParams(vmem_limit_bytes=LARGE),
        cost_estimate=FREE,
    )(*arrays)


def unpack_kernel(
    clip_ref, in_ref, mask_ref, out_ref, tail_ref, last_ref, head_ref, count_ref, rows_ref
):
    frames, cells = out_ref.shape[:2]
    step = frames * ALPHA
    pixels = H * W
    batch = cells // pixels
    total = sum(clip_ref[i, 0] for i in range(clip_ref.shape[0]))
    count_ref[1] = (total * pixels).astype(F32)
    count_ref[0] = (total * (pixels * ALPHA)).astype(F32)
    rows_ref[...] = in_ref[...].astype(F32)
    spot = lax.broadcasted_iota(jnp.int32, (cells, 128), 0)
    for frame in range(frames):
        place = lax.axis_index("mp") * frames + frame
        mask = jnp.zeros((cells, 128), F32)
        for b in range(batch):
            length = clip_ref[lax.axis_index("dp") * batch + b, 0]
            valid = (place < length).astype(F32)
            inside = (spot >= b * pixels) & (spot < (b + 1) * pixels)
            mask = jnp.where(inside, valid, mask)
        mask_ref[frame * cells : (frame + 1) * cells, :] = mask
        for j in range(ALPHA):
            values = rows_ref[pl.ds(frame * ALPHA + j, cells, step), :] * mask
            values = values.astype(BF)
            out_ref[frame, :, j * 128 : (j + 1) * 128] = values
            if frame == frames - 1 and j >= 2:
                (tail_ref, last_ref)[j - 2][...] = values
            if frame == 0 and j == 0:
                head_ref[...] = values


def copies():
    width = 128 // ALPHA
    lanes = jnp.bitwise_and(lax.broadcasted_iota(jnp.int32, (width, 128), 1), width - 1)
    rows = lax.broadcasted_iota(jnp.int32, (width, 128), 0)
    return jnp.where(lanes == rows, 1.0, 0.0).astype(BF)


def lane_mask(rows, j):
    group = lax.broadcasted_iota(jnp.int32, (rows, 128), 1) // (128 // ALPHA)
    return jnp.where(group == j, 1.0, 0.0)


def tiled_affine(ref, tile_ref):
    if ref.shape[1] == 128:
        return jnp.concatenate([ref[...]] * ALPHA, axis=1)
    tile_ref[...] = jnp.zeros_like(tile_ref)
    tile_ref[0:2, 0 : ref.shape[1]] = ref[...]
    return fold_lanes(tile_ref[0:2, :], ALPHA)


def build_a(w_ref, out_ref):
    tiles = mm(w_ref[...], copies())
    size = w_ref.shape[0] // 3
    masks = [lane_mask(size, j) for j in range(ALPHA)]
    for i in range(ALPHA + 2):
        total = sum(
            tiles[(i - j) * size : (i - j + 1) * size, :] * masks[j]
            for j in range(ALPHA)
            if 0 <= i - j < 3
        )
        out_ref[i * size : (i + 1) * size, :] = total.astype(BF)


def build_b(w_ref, out_ref, back):
    ci = w_ref.shape[1]
    for tap in range(9):
        block = w_ref[tap * ci : (tap + 1) * ci, :]
        tile = tn(block, copies()) if back else mm(block, copies())
        place = 8 - tap if back else tap
        for j in range(ALPHA):
            start = place * 128 + j * ci
            out_ref[start : start + ci, :] = (tile * lane_mask(ci, j)).astype(BF)


def build_c(w_ref, out_ref):
    ci, cf = w_ref.shape
    out_ref[...] = jnp.zeros_like(out_ref)
    for j in range(ALPHA):
        out_ref[j * ci : (j + 1) * ci, j * cf : (j + 1) * cf] = w_ref[...]


def build_back(w_ref, out_ref):
    ci = w_ref.shape[1]
    size = w_ref.shape[0] // 3
    one = jnp.where(
        lax.broadcasted_iota(jnp.int32, (ci, ci), 0) == lax.broadcasted_iota(jnp.int32, (ci, ci), 1),
        1.0,
        0.0,
    ).astype(BF)
    out_ref[...] = jnp.zeros_like(out_ref)
    for tap in range(3):
        block = mm_t(one, w_ref[tap * size : (tap + 1) * size, :]).astype(BF)
        for j in range(ALPHA):
            start = 128 + (j + 1 - tap) * ci
            out_ref[start : start + ci, j * size : (j + 1) * size] = block


def entry_kernel(
    mask_ref, fast_ref, before_ref, last_ref, after_ref, slow_ref, wa_ref, wl_ref,
    stack_ref, lateral_ref, first_ref, sums_ref, joined_ref, big_ref, rows_ref,
):
    cells = before_ref.shape[0]
    cs, cf = slow_ref.shape[2], 128
    build_a(wa_ref, big_ref)
    for column in range(0, cs, 128):
        values = slow_ref[:, :, column : column + 128].reshape(2 * cells, 128)
        rows_ref[column // 128] = values.astype(F32)
    tots, squares = [], []
    for frame in range(2):
        mask = mask_ref[frame * cells : (frame + 1) * cells, :]
        own = fast_ref[frame]
        past = (before_ref[...], last_ref[...])
        if frame:
            past = (fast_ref[0][:, 2 * cf : 3 * cf], fast_ref[0][:, 3 * cf :])
        following = fast_ref[1][:, :cf] if frame == 0 else after_ref[...]
        stack_ref[frame, :, 0:cf] = past[1]
        stack_ref[frame, :, cf : 5 * cf] = own
        stack_ref[frame, :, 5 * cf :] = following
        lateral_ref[frame, :, 0:cf] = past[0]
        lateral_ref[frame, :, cf : 2 * cf] = past[1]
        lateral_ref[frame, :, 2 * cf :] = own[:, : 3 * cf]
        value = mm(stack_ref[frame], big_ref[...])
        first_ref[frame * cells : (frame + 1) * cells, :] = value
        tots.append(total_row(value * mask))
        squares.append(total_row(value * mask * value))
        lateral = mm(lateral_ref[frame], wl_ref[...]).astype(BF)
        joined_ref[frame, :, cs:] = lateral * wide_mask(mask.astype(BF), 256)
        for column in range(0, cs, 128):
            values = rows_ref[column // 128, pl.ds(frame, cells, 2), :] * mask
            joined_ref[frame, :, column : column + 128] = values.astype(BF)
    sums_ref[:, :128] = tots[0] + tots[1]
    sums_ref[:, 128:] = squares[0] + squares[1]


def taps_kernel(joined_ref, wa_ref, base_ref, right_ref, left_ref, one_ref, two_ref):
    cells, cm = right_ref.shape
    one_ref[...] = mm_t(joined_ref[0], wa_ref[...])
    two_ref[...] = mm_t(joined_ref[1], wa_ref[...])
    base_ref[:cells, :] = one_ref[:, cm : 2 * cm] + two_ref[:, 2 * cm :]
    base_ref[cells:, :] = two_ref[:, cm : 2 * cm] + one_ref[:, :cm]
    right_ref[...] = two_ref[:, :cm].astype(BF)
    left_ref[...] = one_ref[:, 2 * cm :].astype(BF)


def first_sums_kernel(mask_ref, base_ref, left_ref, right_ref, fast_ref, first_ref, vec_ref):
    cells, cm = left_ref.shape
    tot = square = jnp.zeros((1, cm), F32)
    for frame, halo_ref in enumerate((left_ref, right_ref)):
        now = slice(frame * cells, (frame + 1) * cells)
        value = base_ref[now, :] + halo_ref[...].astype(F32)
        first_ref[now, :] = value
        masked = value * wide_mask(mask_ref[now, :], cm)
        tot = tot + total_row(masked)
        square = square + total_row(masked * value)
    send_all(vec_ref, [fast_ref[...], tot, square])


def sum_kernel(sums_ref, vec_ref):
    total = jnp.sum(sums_ref[...], axis=0)
    vec_ref[...] = jnp.broadcast_to(total[None], vec_ref.shape)


def fast_back_kernel(
    mask_ref, one_ref, two_ref, before_ref, after_ref, dl_ref, cot_ref, wl_ref, wa_ref,
    out_ref, rows_ref, big_ref,
):
    cells = one_ref.shape[0]
    cf = 128
    build_back(wa_ref, big_ref)
    for frame in range(2):
        now = slice(frame * cells, (frame + 1) * cells)
        mask = mask_ref[now, :]
        cl = dl_ref.shape[2]
        pieces = (before_ref[:, cl:], one_ref[...], two_ref[...])
        if frame:
            pieces = pieces[1:] + (after_ref[:, cl:],)
        taps = jnp.concatenate(pieces, axis=1)
        now_dl, next_dl = dl_ref[frame], after_ref[:, :cl] if frame else dl_ref[1]
        for j in range(ALPHA):
            part = slice(j * 128, (j + 1) * 128)
            grad = mm(taps, big_ref[:, part]) + cot_ref[now, part]
            if j < 3:
                grad = grad + mm_t(now_dl, wl_ref[(j + 2) * cf : (j + 3) * cf, :])
            if j >= 2:
                grad = grad + mm_t(next_dl, wl_ref[(j - 2) * cf : (j - 1) * cf, :])
            rows_ref[pl.ds(frame * ALPHA + j, cells, 2 * ALPHA), :] = grad * mask
    out_ref[...] = rows_ref[...].astype(BF)


def dot(left, right, left_dim, right_dim):
    return lax.dot_general(
        left, right, (((left_dim,), (right_dim,)), ((), ())), preferred_element_type=F32
    )


def rows_dot(left, right):
    return lax.dot_general(
        left, right, (((0, 1), (0, 1)), ((), ())), preferred_element_type=F32
    )


def folded(vector, groups):
    return jnp.sum(vector.reshape(groups, -1), axis=0)


def norm_terms(totals, squares, count, groups=1):
    average = totals / count
    inverse = lax.rsqrt(squares / count - average * average + NORM_EPSILON)
    return jnp.tile(average, groups), jnp.tile(inverse, groups)


ROWS_STEP = 112
TAPS = [(dh, dw) for dh in (-1, 0, 1) for dw in (-1, 0, 1)]


def row_chunks(rows, step):
    return [pl.ds(start, step) for start in range(0, rows, step)]


def loop_rows(rows, step, body, init):
    def turn(i, carry):
        return body(pl.ds(pl.multiple_of(i * step, step), step), carry)

    return lax.fori_loop(0, rows // step, turn, init)


def collapse(values):
    return jnp.sum(values.reshape(-1, 8, values.shape[-1]), axis=0)


def gate_of(values):
    return 0.5 * jnp.tanh(0.5 * values) + 0.5


def fold_lanes(vector, groups):
    width = vector.shape[-1] // groups
    total = vector
    for j in range(1, groups):
        total = total + pltpu.roll(vector, j * width, 1)
    return total


def mean_inverse(totals, squares, count):
    average = totals / count
    return average, lax.rsqrt(squares / count - average * average + NORM_EPSILON)


def line(average, inverse, affine):
    scale = affine[0:1] * inverse
    return scale, affine[1:2] - average * scale


def send_all(vec_ref, pieces):
    start = 0
    for piece in pieces:
        width = piece.shape[-1]
        spread = jnp.broadcast_to(piece[None], (vec_ref.shape[0], 1, width))
        vec_ref[:, :, start : start + width] = spread
        start += width


def received(sums_ref, widths):
    total = jnp.sum(sums_ref[...], axis=0)
    return split(total, widths)


def split(total, widths):
    pieces = []
    start = 0
    for width in widths:
        pieces.append(total[:, start : start + width])
        start += width
    return pieces


def total_row(vector):
    return jnp.sum(vector, axis=0, keepdims=True)


MARGIN = 16


def clear_margins(buffer):
    rows = buffer.shape[0]
    zeros = jnp.zeros((MARGIN, buffer.shape[1]), F32)
    buffer[0:MARGIN, :] = zeros
    buffer[rows - MARGIN : rows, :] = zeros


def write_patches(buffer, patches, edges):
    rows, channels = patches.shape[0], buffer.shape[1]
    for start in range(0, rows, ROWS_STEP):
        top, bottom, left, right = (edges[k, start : start + ROWS_STEP, :] for k in range(4))
        for tap, (dh, dw) in enumerate(TAPS):
            mask = None
            if dh:
                mask = top if dh < 0 else bottom
            if dw:
                side = left if dw < 0 else right
                mask = side if mask is None else mask * side
            offset = MARGIN + start + W * dh + dw
            for column in range(0, channels, 128):
                piece = buffer[offset : offset + ROWS_STEP, column : column + 128]
                if mask is not None:
                    piece = piece * mask
                place = tap * channels + column
                patches[start : start + ROWS_STEP, place : place + 128] = piece.astype(BF)


def mm(left, right):
    return jnp.dot(left, right, preferred_element_type=F32)


def mm_t(left, right):
    return lax.dot_general(left, right, (((1,), (1,)), ((), ())), preferred_element_type=F32)


def wide_mask(mask, width):
    return jnp.concatenate([mask] * (width // 128), axis=1) if width > 128 else mask


def conv_kernel(
    count_ref, sums_ref, vf_ref, vs_ref, af_ref, as_ref, mask_ref, edge_ref, wf_ref, ws_ref,
    hf_ref, hs_ref, of_ref, os_ref, total_ref, vec_ref, bf_ref, bs_ref, pf_ref, ps_ref, big_ref, tile_ref,
):
    fast_count, slow_count = count_ref[0], count_ref[1]
    total = jnp.sum(sums_ref[...], axis=0)
    total_ref[...] = total
    ft, fq, st, sq = split(total, (128, 128, 256, 256))
    lines = []
    build_b(wf_ref, big_ref, False)
    for tot, square, count, affine in ((ft, fq, fast_count, af_ref), (st, sq, slow_count, as_ref)):
        if tot.shape[-1] == 128:
            tot, square = fold_lanes(tot, ALPHA), fold_lanes(square, ALPHA)
            affine = tiled_affine(affine, tile_ref)
        else:
            affine = affine[...]
        lines.append(line(*mean_inverse(tot, square, count), affine))
    rows = vf_ref.shape[0]
    for value_ref, hidden_ref, buffer, (scale, shift) in (
        (vf_ref, hf_ref, bf_ref, lines[0]),
        (vs_ref, hs_ref, bs_ref, lines[1]),
    ):
        width = value_ref.shape[1]
        clear_margins(buffer)
        for start in range(0, rows, ROWS_STEP):
            z = value_ref[start : start + ROWS_STEP, :] * scale + shift
            hidden = z * gate_of(z) * wide_mask(mask_ref[start : start + ROWS_STEP, :], width)
            buffer[MARGIN + start : MARGIN + start + ROWS_STEP, :] = hidden
            hidden_ref[start : start + ROWS_STEP, :] = hidden.astype(BF)
    write_patches(bf_ref, pf_ref, edge_ref)
    write_patches(bs_ref, ps_ref, edge_ref)
    of_ref[...] = mm(pf_ref[...], big_ref[...])
    os_ref[...] = mm_t(ps_ref[...], ws_ref[...])
    pieces = []
    for out_ref in (of_ref, os_ref):
        width = out_ref.shape[1]

        def body(rows_now, carry):
            value = out_ref[rows_now, :]
            masked = value * wide_mask(mask_ref[rows_now, :], width)
            return carry[0] + collapse(masked), carry[1] + collapse(masked * value)

        zero = jnp.zeros((8, width), F32)
        pieces += [total_row(v) for v in loop_rows(rows, ROWS_STEP, body, (zero, zero))]
    send_all(vec_ref, pieces)


def expand_kernel(
    count_ref, sums_ref, short_ref, vf_ref, vs_ref, af_ref, as_ref, mask_ref, wf_ref, ws_ref,
    hf_ref, hs_ref, yf_ref, ys_ref, total_ref, vec_ref, of_ref, os_ref, big_ref, tile_ref,
):
    fast_count, slow_count = count_ref[0], count_ref[1]
    total = jnp.sum(sums_ref[...], axis=0)
    total_ref[...] = total
    ft, fq, st, sq = split(total, (128, 128, 256, 256))
    ft, fq = fold_lanes(ft, ALPHA), fold_lanes(fq, ALPHA)
    build_c(wf_ref, big_ref)
    lines = (
        line(*mean_inverse(ft, fq, fast_count), tiled_affine(af_ref, tile_ref)),
        line(*mean_inverse(st, sq, slow_count), as_ref[...]),
    )
    rows = vf_ref.shape[0]
    for value_ref, hidden_ref, (scale, shift) in ((vf_ref, hf_ref, lines[0]), (vs_ref, hs_ref, lines[1])):
        width = value_ref.shape[1]

        def body(rows_now, carry):
            z = value_ref[rows_now, :] * scale + shift
            hidden = z * gate_of(z) * wide_mask(mask_ref[rows_now, :], width)
            hidden_ref[rows_now, :] = hidden.astype(BF)
            return carry

        loop_rows(rows, ROWS_STEP, body, 0)
    of_ref[...] = mm(hf_ref[...], big_ref[...])
    os_ref[...] = mm(hs_ref[...], ws_ref[...])
    pieces = []
    for out_ref, low_ref in ((of_ref, yf_ref), (os_ref, ys_ref)):
        width = out_ref.shape[1]
        tots, squares = [], []
        for column in range(0, width, 512):

            def body(rows_now, carry):
                value = out_ref[rows_now, column : column + 512]
                low_ref[rows_now, column : column + 512] = value.astype(low_ref.dtype)
                value = value.astype(low_ref.dtype).astype(F32)
                masked = value * wide_mask(mask_ref[rows_now, :], 512)
                return carry[0] + collapse(masked), carry[1] + collapse(masked * value)

            zero = jnp.zeros((8, 512), F32)
            one, two = loop_rows(rows, 16, body, (zero, zero))
            tots.append(total_row(one))
            squares.append(total_row(two))
        if width == 512:
            pieces += [sum(v[:, j * 128 : (j + 1) * 128] for j in range(ALPHA)) for v in (tots[0], squares[0])]
        else:
            pieces += [jnp.concatenate(tots, 1), jnp.concatenate(squares, 1)]
    send_all(vec_ref, pieces + [short_ref[...]])


def short_kernel(mask_ref, joined_ref, ws_ref, out_ref, vec_ref):
    rows, wide = out_ref.shape
    for column in range(0, wide, 256):
        part = slice(column, column + 256)
        one = jnp.zeros((8, 256), F32)
        two = one
        for start in range(0, rows, 2 * ROWS_STEP):
            now = slice(start, min(start + 2 * ROWS_STEP, rows))
            value = mm(joined_ref[now, :], ws_ref[:, part])
            out_ref[now, part] = value.astype(BF)
            value = value.astype(BF).astype(F32)
            masked = value * wide_mask(mask_ref[now, :], 256)
            one = one + collapse(masked)
            two = two + collapse(masked * value)
        vec_ref[:, part] = total_row(one)
        vec_ref[:, wide + column : wide + column + 256] = total_row(two)


def output_kernel(
    count_ref, sums_ref, vf_ref, vs_ref, vh_ref, fast_ref, cf_ref, cs_ref,
    af_ref, as_ref, ah_ref, mask_ref,
    yf_ref, ys_ref, gf_ref, gs_ref, total_ref, vec_ref, rows_ref, cots_ref, *, sync,
):
    fast_count, slow_count = count_ref[0], count_ref[1]
    total = jnp.sum(sums_ref[...], axis=0)
    total_ref[...] = total
    wide = vs_ref.shape[1]
    ft, fq, st, sq, ht, hq = split(total, (128, 128, wide, wide, wide, wide))
    rows = vf_ref.shape[0]
    mean, inverse = mean_inverse(ft, fq, fast_count)
    mean, inverse = (jnp.concatenate([v] * ALPHA, 1) for v in (mean, inverse))
    scale, shift = line(mean, inverse, tiled_affine(af_ref, None))

    frames, cells = fast_ref.shape[:2]
    step = frames * ALPHA
    cots_ref[...] = cf_ref[...].astype(F32)
    zero = jnp.zeros((8, 512), F32)
    beta = gamma = jnp.zeros((1, 128), F32)
    for frame in range(frames):
        now = slice(frame * cells, (frame + 1) * cells)
        for j in range(ALPHA):
            part = slice(j * 128, (j + 1) * 128)
            place = pl.ds(frame * ALPHA + j, cells, step)
            mask = mask_ref[now, :]
            value = vf_ref[now, part]
            z = value * scale[:, part] + shift[:, part] + fast_ref[frame, :, part].astype(F32)
            gate = gate_of(z)
            rows_ref[place, :] = mask * z * gate
            grad = cots_ref[place, :] * mask * gate * (1.0 + z * (1.0 - gate))
            gf_ref[now, part] = grad
            beta = beta + total_row(grad)
            gamma = gamma + total_row(grad * value)
    yf_ref[...] = rows_ref[...].astype(BF)
    sync.send(0, 2)
    sync.arrive(2, 3, 6)
    pieces = [beta, (gamma - mean[:, :128] * beta) * inverse[:, :128]]
    mean_c, inverse_c = mean_inverse(st, sq, slow_count)
    mean_h, inverse_h = mean_inverse(ht, hq, slow_count)
    scale_c, shift_c = line(mean_c, inverse_c, as_ref[...])
    scale_h, shift_h = line(mean_h, inverse_h, ah_ref[...])
    betas, gammas, others = [], [], []
    for column in range(0, wide, 512):
        part = slice(column, column + 512)
        sc, sh, shift_both = scale_c[:, part], scale_h[:, part], shift_c[:, part] + shift_h[:, part]

        def body(rows_now, carry):
            third, short = vs_ref[rows_now, part].astype(F32), vh_ref[rows_now, part].astype(F32)
            mask = wide_mask(mask_ref[rows_now, :], 512)
            z = third * sc + short * sh + shift_both
            gate = gate_of(z)
            ys_ref[rows_now, part] = (mask * z * gate).astype(BF)
            grad = cs_ref[rows_now, part].astype(F32) * mask * gate * (1.0 + z * (1.0 - gate))
            gs_ref[rows_now, part] = grad.astype(BF)
            grad = grad.astype(BF).astype(F32)
            return (
                carry[0] + collapse(grad),
                carry[1] + collapse(grad * third),
                carry[2] + collapse(grad * short),
            )

        beta, gamma, other = (total_row(v) for v in loop_rows(rows, 16, body, (zero, zero, zero)))
        betas.append(beta)
        gammas.append((gamma - mean_c[:, part] * beta) * inverse_c[:, part])
        others.append((other - mean_h[:, part] * beta) * inverse_h[:, part])
    pieces += [jnp.concatenate(v, 1) for v in (betas, gammas, others)]
    sync.send(1, 3)
    send_all(vec_ref, pieces)


def back_line(mean, inverse, scale, beta, gamma, count):
    first = inverse * scale
    third = first * gamma * inverse / count
    return first, first * beta / count - mean * third, third


def narrow_kernel(
    count_ref, sums_ref, third_ref, second_ref,
    gf_ref, gs_ref, vf_ref, vs_ref, vh_ref, uf_ref, us_ref,
    afc_ref, asc_ref, ash_ref, afb_ref, asb_ref, mask_ref, wf_ref, ws_ref,
    df_ref, ds_ref, dh_ref, of_ref, os_ref, total_ref, vec_ref, big_ref, tile_ref, *, sync,
):
    fast_count, slow_count = count_ref[0], count_ref[1]
    total = jnp.sum(sums_ref[...], axis=0)
    total_ref[...] = total
    wide = vs_ref.shape[1]
    rows = vf_ref.shape[0]
    fast_beta, fast_gamma, beta, gamma_c, gamma_h = split(total, (128, 128, wide, wide, wide))
    ft, fq, st, sq, ht, hq = split(third_ref[...], (128, 128, wide, wide, wide, wide))
    mean, inverse = mean_inverse(ft, fq, fast_count)
    tiled = [jnp.concatenate([v] * ALPHA, 1) for v in (mean, inverse, fast_beta, fast_gamma)]
    build_c(wf_ref, big_ref)
    f1, f2, f3 = back_line(tiled[0], tiled[1], tiled_affine(afc_ref, None)[0:1], tiled[2], tiled[3], fast_count)

    def fast_body(rows_now, carry):
        mask = wide_mask(mask_ref[rows_now, :], 512)
        grad = mask * (gf_ref[rows_now, :].astype(F32) * f1 - f2 - vf_ref[rows_now, :].astype(F32) * f3)
        df_ref[rows_now, :] = grad.astype(BF)
        return carry

    loop_rows(rows, 16, fast_body, 0)
    sync.send(0)
    sync.arrive(4, 6, 7)
    mean_c, inverse_c = mean_inverse(st, sq, slow_count)
    mean_h, inverse_h = mean_inverse(ht, hq, slow_count)
    lines_c = back_line(mean_c, inverse_c, asc_ref[0:1, :], beta, gamma_c, slow_count)
    lines_h = back_line(mean_h, inverse_h, ash_ref[0:1, :], beta, gamma_h, slow_count)
    for column in range(0, wide, 512):
        part = slice(column, column + 512)
        c1, c2, c3 = (v[:, part] for v in lines_c)
        h1, h2, h3 = (v[:, part] for v in lines_h)

        def body(rows_now, carry):
            mask = wide_mask(mask_ref[rows_now, :], 512)
            grad = gs_ref[rows_now, part].astype(F32)
            third, short = vs_ref[rows_now, part].astype(F32), vh_ref[rows_now, part].astype(F32)
            ds_ref[rows_now, part] = (mask * (grad * c1 - c2 - third * c3)).astype(BF)
            dh_ref[rows_now, part] = (mask * (grad * h1 - h2 - short * h3)).astype(BF)
            return carry

        loop_rows(rows, 16, body, 0)
    sync.send(1, 2)
    sync.arrive(8, 9, 17)
    of_ref[...] = mm_t(df_ref[...], big_ref[...])
    os_ref[...] = mm_t(ds_ref[...], ws_ref[...])
    ft, fq, st, sq = split(second_ref[...], (128, 128, 256, 256))
    pieces = slope_sums(
        (of_ref, uf_ref, tiled_affine(afb_ref, tile_ref), fold_lanes(ft, ALPHA), fold_lanes(fq, ALPHA), fast_count),
        (os_ref, us_ref, asb_ref, st, sq, slow_count),
        mask_ref,
    )
    send_all(vec_ref, pieces)


def slope_sums(fast_parts, slow_parts, mask_ref):
    pieces = []
    for out_ref, value_ref, affine, tot, square, count in (fast_parts, slow_parts):
        width = out_ref.shape[1]
        mean, inverse = mean_inverse(tot, square, count)
        scale, shift = line(mean, inverse, affine[...])

        def body(rows_now, carry):
            value = value_ref[rows_now, :]
            z = value * scale + shift
            gate = gate_of(z)
            mask = wide_mask(mask_ref[rows_now, :], width)
            grad = out_ref[rows_now, :] * mask * gate * (1.0 + z * (1.0 - gate))
            out_ref[rows_now, :] = grad
            return carry[0] + collapse(grad), carry[1] + collapse(grad * value)

        zero = jnp.zeros((8, width), F32)
        rows = out_ref.shape[0]
        beta, gamma = (total_row(v) for v in loop_rows(rows, ROWS_STEP // 2, body, (zero, zero)))
        pieces += [beta, (gamma - mean * beta) * inverse]
    return pieces


def conv_back_kernel(
    count_ref, sums_ref, second_ref, first_ref,
    gf_ref, gs_ref, uf_ref, us_ref, vf_ref, vs_ref,
    afb_ref, asb_ref, afa_ref, asa_ref, mask_ref, edge_ref, wf_ref, ws_ref,
    df_ref, ds_ref, of_ref, os_ref, total_ref, vec_ref,
    bf_ref, bs_ref, pf_ref, ps_ref, big_ref, tile_ref,
):
    fast_count, slow_count = count_ref[0], count_ref[1]
    total = jnp.sum(sums_ref[...], axis=0)
    total_ref[...] = total
    rows = gf_ref.shape[0]
    build_b(wf_ref, big_ref, True)
    fast_beta, fast_gamma, beta, gamma = split(total, (128, 128, 256, 256))
    ft, fq, st, sq = split(second_ref[...], (128, 128, 256, 256))
    mean, inverse = mean_inverse(fold_lanes(ft, ALPHA), fold_lanes(fq, ALPHA), fast_count)
    fast_lines = back_line(
        mean, inverse, tiled_affine(afb_ref, tile_ref)[0:1], fold_lanes(fast_beta, ALPHA), fold_lanes(fast_gamma, ALPHA), fast_count
    )
    slow_lines = back_line(*mean_inverse(st, sq, slow_count), asb_ref[0:1, :], beta, gamma, slow_count)
    for grad_ref, value_ref, out_ref, buffer, lines in (
        (gf_ref, uf_ref, df_ref, bf_ref, fast_lines),
        (gs_ref, us_ref, ds_ref, bs_ref, slow_lines),
    ):
        width = grad_ref.shape[1]
        one, two, three = lines
        clear_margins(buffer)
        for start in range(0, rows, ROWS_STEP):
            now = slice(start, start + ROWS_STEP)
            grad = grad_ref[now, :] * one - two - value_ref[now, :] * three
            grad = grad * wide_mask(mask_ref[now, :], width)
            out_ref[now, :] = grad.astype(BF)
            buffer[MARGIN + start : MARGIN + start + ROWS_STEP, :] = grad
    write_patches(bf_ref, pf_ref, edge_ref)
    write_patches(bs_ref, ps_ref, edge_ref)
    of_ref[...] = mm(pf_ref[...], big_ref[...])
    os_ref[...] = mm(ps_ref[...], ws_ref[...])
    ft, fq, st, sq = split(first_ref[...], (128, 128, 256, 256))
    pieces = slope_sums(
        (of_ref, vf_ref, tiled_affine(afa_ref, tile_ref), fold_lanes(ft, ALPHA), fold_lanes(fq, ALPHA), fast_count),
        (os_ref, vs_ref, asa_ref, st, sq, slow_count),
        mask_ref,
    )
    send_all(vec_ref, pieces)


def exchange(vec):
    return lax.all_to_all(vec, ("dp", "mp"), 0, 0, tiled=True)


def fast_results_kernel(in_ref, a_ref, b_ref, c_ref, l_ref, rows_ref):
    if len(in_ref.shape) == 3:
        for device in range(in_ref.shape[0]):
            x, core, block = device // 16, device // 8 % 2, device % 8
            for k in range(4):
                start = core * 1024 + block * 128 + (x * 4 + k) * 16
                rows_ref[start : start + 16, :] = in_ref[device, :, k * 128 : (k + 1) * 128]
        in_ref = rows_ref
    taps, cf, ci = a_ref.shape
    for tap in range(taps):
        a_ref[tap] = in_ref[tap * cf : (tap + 1) * cf, :].astype(F32)[:, :ci]
    start = taps * cf
    for tap in range(9):
        b_ref[tap] = in_ref[start + tap * ci : start + (tap + 1) * ci, :].astype(F32)[:, :ci]
    start += 9 * ci
    c_ref[...] = in_ref[start : start + ci, :].astype(F32)
    start += ci
    for side in range(2):
        for tap in range(5):
            rows = slice(start + (side * 5 + tap) * cf, start + (side * 5 + tap + 1) * cf)
            l_ref[tap, :, side * 128 : (side + 1) * 128] = in_ref[rows, :].astype(F32)


def norms_kernel(c_ref, b_ref, a_ref, fa_ref, fb_ref, fc_ref, sa_ref, sb_ref, sc_ref, sh_ref):
    wide = sc_ref.shape[1]
    beta, gamma, slow, gamma_c, gamma_h = split(c_ref[...], (128, 128, wide, wide, wide))
    for out_ref, scale, shift in (
        (fc_ref, gamma, beta), (sc_ref, gamma_c, slow), (sh_ref, gamma_h, slow)
    ):
        out_ref[0:1, :] = scale
        out_ref[1:2, :] = shift
    for in_ref, fast_ref, slow_ref in ((b_ref, fb_ref, sb_ref), (a_ref, fa_ref, sa_ref)):
        width, cm = fast_ref.shape[1], slow_ref.shape[1]
        beta, gamma, slow, slow_gamma = split(in_ref[...], (128, 128, cm, cm))
        fast_ref[0:1, :] = fold_lanes(gamma, ALPHA)[:, :width]
        fast_ref[1:2, :] = fold_lanes(beta, ALPHA)[:, :width]
        slow_ref[0:1, :] = slow_gamma
        slow_ref[1:2, :] = slow


def per_device(
    fast_in,
    slow_in,
    clip_len,
    w_fast_a,
    w_fast_b,
    w_fast_c,
    w_lateral,
    w_slow_a,
    w_slow_b,
    w_slow_c,
    w_short,
    norm_fast_a,
    norm_fast_b,
    norm_fast_c,
    norm_slow_a,
    norm_slow_b,
    norm_slow_c,
    norm_short,
    cot_fast,
    cot_slow,
):
    batch, fast_frames, pixels, cf = fast_in.shape
    frames, cs = slow_in.shape[1], slow_in.shape[3]
    cells = batch * pixels
    ci = w_fast_a.shape[2]
    cl = w_lateral.shape[2]
    co = norm_slow_c.shape[1]
    cm = norm_slow_a.shape[1]
    cu = cs + cl
    mp = lax.axis_size("mp")
    me = lax.axis_index("mp")

    part, wide = w_slow_a.shape[2], w_short.shape[1]
    rows = frames * cells
    lane, fw = ALPHA * ci, ALPHA * cf
    small = 2 * lane + 2 * cm
    dp = lax.axis_size("dp")
    devices = dp * mp
    near_mesh = small_mesh()
    spot = np.arange(rows) % pixels
    edges = np.stack([spot >= W, spot < pixels - W, spot % W > 0, spot % W < W - 1])
    edges = jnp.asarray(np.repeat(edges.astype(np.float32)[:, :, None], 128, axis=2))
    buffers = [((rows + 2 * MARGIN, lane), F32), ((rows + 2 * MARGIN, cm), F32)]
    patches = [((rows, 9 * lane), BF), ((rows, 9 * cm), BF)]
    tile = ((8, 128), F32)

    def flat(values):
        return values.reshape(-1, values.shape[-1])

    def framed(values):
        return values.reshape(frames, cells, values.shape[-1])

    def by_pixel(values):
        return values.transpose(0, 2, 1, 3).reshape(cells, -1, values.shape[-1])

    def by_frame(values):
        return values.reshape(batch, pixels, -1, values.shape[-1]).transpose(0, 2, 1, 3)

    shards = jnp.swapaxes(w_slow_a, 1, 2), jnp.swapaxes(w_slow_b, 1, 2), w_slow_c, w_short
    if near_mesh:
        mine_a, mine_bc, mine_short = own_halves(*shards)
        line_a = line_pieces(mine_a)
        fast_in = held(fast_in, mine_a)
    mask, fast, tail, last, head, counts = local_call(
        unpack_kernel,
        [clip_len],
        [flat(by_pixel(fast_in))],
        [
            ((rows, 128), F32), ((frames, cells, fw), BF), ((cells, cf), BF), ((cells, cf), BF),
            ((cells, cf), BF), ((2,), F32),
        ],
        [((rows * ALPHA, cf), F32)],
        out_specs=[VMEM] * 5 + [SMEM],
    )
    if near_mesh:
        tail, last, head = held((tail, last, head), line_a[1])
    before = [shift_permute(values, "mp", 1) for values in (tail, last)]
    following = shift_permute(head, "mp", -1)
    if near_mesh:
        near_a = stacked(held(line_a, (before, following)))
    fast_stack, lateral_stack, fast_first, fast_sums, joined = local_call(
        entry_kernel,
        [],
        [
            mask, fast, *before, following, by_pixel(slow_in), w_fast_a.reshape(-1, ci),
            w_lateral.reshape(-1, cl),
        ],
        [
            ((frames, cells, 6 * cf), BF), ((frames, cells, 5 * cf), BF), ((rows, lane), F32),
            ((1, 2 * lane), F32), ((frames, cells, cu), BF),
        ],
        [((6 * cf, lane), BF), ((cs // 128, rows, 128), F32)],
    )

    if near_mesh:
        near_bc = stacked(held(line_pieces(held(mine_bc, near_a)), joined))
        line_short = line_pieces(held(mine_short, near_a))
        side_a = held(xor_permute(near_a, "mp", 1), (joined, near_bc))
        pieces_a = near_a, side_a, swap_cores(near_a), swap_cores(side_a)
        wa = place_call(place_a, pieces_a, [(3 * cm, cu)])[0]
    else:
        wa, wb, wb_back, wc, ws = gather_whole(*shards)
    base, to_right, to_left = local_call(
        taps_kernel,
        [],
        [joined, wa],
        [((rows, cm), F32), ((cells, cm), BF), ((cells, cm), BF)],
        [((cells, 3 * cm), F32)] * 2,
    )
    left = shift_permute(to_right, "mp", 1)
    right = shift_permute(to_left, "mp", -1)
    if near_mesh:
        pieces_bc = both_sides(near_bc)
        base = held(base, pieces_bc)
        near_short = stacked(held(line_short, (left, right)))
    slow_first, vec = local_call(
        first_sums_kernel,
        [],
        [mask, base, left, right, fast_sums],
        [((rows, cm), F32), ((devices, 1, small), F32)],
    )
    if near_mesh:
        wb, wb_back, wc = place_call(
            place_bc, pieces_bc, [(cm, 9 * cm), (9 * cm, cm), (cm, 8 * wide)]
        )
        side_short = xor_permute(near_short, "mp", 1)
        sums = held(exchange(vec), (wb, side_short))
    else:
        sums = exchange(vec)

    wfb = w_fast_b.reshape(-1, ci)
    hidden_a, hidden_c, fast_second, slow_second, total_1, vec = local_call(
        conv_kernel,
        [counts],
        [sums, fast_first, slow_first, norm_fast_a, norm_slow_a, mask, edges, wfb, wb],
        [
            ((rows, lane), BF), ((rows, cm), BF), ((rows, lane), F32), ((rows, cm), F32),
            ((1, small), F32), ((devices, 1, small), F32),
        ],
        buffers + patches + [((9 * lane, lane), BF), tile],
    )

    if near_mesh:
        side_short = held(side_short, vec)
        pieces = near_short, side_short, swap_cores(near_short), swap_cores(side_short)
        ws = place_call(place_short, pieces, [(cu, 8 * wide)])[0]
    shortcut, short_vec = local_call(
        short_kernel, [], [mask, flat(joined), ws], [((rows, co), BF), ((1, 2 * co), F32)]
    )
    sums = held(exchange(vec), short_vec)
    hidden_b, hidden_d, fast_third, slow_third, total_2, vec = local_call(
        expand_kernel,
        [counts],
        [sums, short_vec, fast_second, slow_second, norm_fast_b, norm_slow_b, mask, w_fast_c, wc],
        [
            ((rows, lane), BF), ((rows, cm), BF), ((rows, fw), F32), ((rows, co), BF),
            ((1, small), F32), ((dp, 1, 2 * cf + 4 * co), F32),
        ],
        [((rows, fw), F32), ((rows, co), F32), ((lane, fw), BF), tile],
    )
    slow_cots = held(cot_slow, vec).transpose(1, 0, 2, 3).reshape(frames, cells, co)
    slow_cots = flat(slow_cots)
    sums = lax.all_to_all(vec, "dp", 0, 0, tiled=True)
    (vec,) = quick_call(sum_kernel, [sums], [((mp, 1, vec.shape[2]), F32)])
    sums = lax.all_to_all(vec, "mp", 0, 0, tiled=True)

    fast_out, slow_out, fast_cot, slow_cot, total_3, vec = local_call(
        output_kernel,
        [counts],
        [
            sums, fast_third, slow_third, shortcut, fast, flat(by_pixel(cot_fast)),
            slow_cots, norm_fast_c, norm_slow_c, norm_short, mask,
        ],
        [
            ((rows * ALPHA, cf), BF), ((rows, co), BF), ((rows, fw), F32), ((rows, co), BF),
            ((1, 2 * cf + 4 * co), F32), ((devices, 1, 2 * cf + 3 * co), F32),
        ],
        [((rows * ALPHA, cf), F32)] * 2,
        late=(2, 3, 6),
        early=(0, 1, 2, 3),
    )
    slow_out = framed(slow_out).reshape(frames, batch, pixels, co).transpose(1, 0, 2, 3)
    sums = held(exchange(vec), slow_out)

    d_fast_third, d_slow_third, d_short, grad_fb, grad_sb, total_4, vec = local_call(
        narrow_kernel,
        [counts],
        [
            sums, total_3, total_2, fast_cot, slow_cot, fast_third, slow_third, shortcut,
            fast_second, slow_second, norm_fast_c, norm_slow_c, norm_short, norm_fast_b, norm_slow_b,
            mask, w_fast_c, wc,
        ],
        [
            ((rows, fw), BF), ((rows, co), BF), ((rows, co), BF), ((rows, lane), F32),
            ((rows, cm), F32), ((1, 2 * cf + 3 * co), F32), ((devices, 1, small), F32),
        ],
        [((lane, fw), BF), tile],
        late=(4, 6, 7, 8, 9, 17),
        early=(0, 1, 2),
    )

    def weight_grad(kernel, arrays, size, length, total, scratch=()):
        halves = ((mp, size, length), BF)
        return local_call(kernel, [], arrays, [halves, halves], [((total, length), BF), *scratch])

    if near_mesh:
        raw_cs = weight_grad(
            grad_cs_kernel, [d_short, d_slow_third, flat(joined), hidden_d], wide // 2, cu + cm, co
        )
        sums, raw_cs = lax.optimization_barrier((exchange(vec), raw_cs))
        sent_cs = swap_cores(raw_cs[0])
    else:
        raw_cs = jnp.concatenate(
            [rows_dot(framed(d_short), joined), rows_dot(framed(d_slow_third), framed(hidden_d))], -1
        )
        sum_cs = reduce_whole(raw_cs.reshape(mp, 2, wide // 2, cu + cm)).reshape(wide, cu + cm)
        sums = exchange(vec)

    d_fast_second, d_slow_second, grad_fa, grad_sa, total_5, vec = local_call(
        conv_back_kernel,
        [counts],
        [
            sums, total_2, total_1, grad_fb, grad_sb, fast_second, slow_second, fast_first,
            slow_first, norm_fast_b, norm_slow_b, norm_fast_a, norm_slow_a, mask, edges, wfb, wb_back,
        ],
        [
            ((rows, lane), BF), ((rows, cm), BF), ((rows, lane), F32), ((rows, cm), F32),
            ((1, small), F32), ((devices, 1, small), F32),
        ],
        buffers + patches + [((9 * lane, lane), BF), tile],
    )
    grad_b_scratch = [buffers[1], patches[1]]
    (fast_inner,) = local_call(
        fast_inner_kernel,
        [],
        [hidden_a, d_fast_second, hidden_b, d_fast_third, edges],
        [((10 * ci, 128), BF)],
        [buffers[0], patches[0]],
    )
    if near_mesh:
        raw_b = weight_grad(
            grad_b_kernel, [d_slow_second, hidden_c, edges], part // 2, 9 * cm, cm, grad_b_scratch
        )
        sums, raw_b, fast_inner = lax.optimization_barrier((exchange(vec), raw_b, fast_inner))
        sent_b = swap_cores(raw_b[0])
    else:
        (raw_b,) = local_call(
            grad_b_whole_kernel,
            [],
            [d_slow_second, hidden_c, edges],
            [((cm, 9 * cm), F32)],
            grad_b_scratch,
        )
        sum_b = reduce_whole(raw_b.reshape(mp, 2, part // 2, 9 * cm)).reshape(part, 9, cm)
        sums = exchange(vec)
    d_fast_0, d_fast_1, d_slow_0, d_slow_1, to_right, total_6 = local_call(
        first_kernel,
        [counts],
        [sums, total_1, grad_fa, grad_sa, fast_first, slow_first, norm_fast_a, norm_slow_a, mask],
        [((cells, lane), BF)] * 2 + [((cells, cm), BF)] * 2 + [((cells, cm + lane), BF), ((1, small), F32)],
        [tile],
    )
    slow_parts = [
        d_slow_0, d_slow_1, shift_permute(to_right, "mp", 1), shift_permute(d_slow_0, "mp", -1)
    ]
    if near_mesh:
        far_1, near_1 = merge((raw_cs[1], held(raw_b[1], d_slow_0)), (sent_cs, sent_b))
        raw_a = weight_grad(
            grad_a_kernel, held(slow_parts, far_1) + [joined], 3 * part // 2, cu, 3 * cm
        )
        sent_a = swap_cores(raw_a[0])
        slow_parts = held(slow_parts, raw_a)
    else:
        three = jnp.stack(
            [
                jnp.concatenate([d_slow_1, slow_parts[3]]),
                jnp.concatenate([d_slow_0, d_slow_1]),
                jnp.concatenate([slow_parts[2][:, :cm], d_slow_0]),
            ]
        )
        raw_a = jnp.einsum("kro,rc->koc", three, flat(joined), preferred_element_type=F32)
        raw_a = raw_a.reshape(3, mp, 2, part // 2, cu).transpose(1, 2, 0, 3, 4)
        sum_a = reduce_whole(raw_a.reshape(mp, 2, 3 * part // 2, cu))
        sum_a = sum_a.reshape(2, 3, part // 2, cu).transpose(1, 0, 2, 3).reshape(3, part, cu)
    d_lateral, lateral_edge = lateral_back(
        [mask, *slow_parts, d_fast_0, framed(d_short), wa, ws],
        [((frames, cells, cl), BF), ((cells, cl + lane), BF)],
    )
    lateral_after = shift_permute(lateral_edge, "mp", -1)
    fast_outer = [fast_stack, d_fast_0, d_fast_1, lateral_stack, d_lateral, fast_inner]
    if near_mesh:
        half_fast = ((8, 16, 1024), BF)
        fast_send, fast_keep = local_call(
            fast_outer_kernel, [], fast_outer, [half_fast] * 2, [((2048, 128), BF)]
        )
        turned_1 = turn(far_1, near_1)
        keeps = raw_a[1], held(fast_keep, turned_1)
        far_2, near_2 = merge(keeps, (sent_a, swap_cores(fast_send)))
        slow_parts = held(slow_parts, far_2)
    else:
        (raw_fast,) = local_call(fast_whole_kernel, [], fast_outer, [((2048, 128), F32)])
        raw_fast = lax.psum(raw_fast, ("dp", "mp"))
    (grad_slow_in,) = local_call(
        joined_back_kernel,
        [],
        [mask, *slow_parts, framed(d_short), wa, ws],
        [((cells, frames, cs), BF)],
    )
    norms = local_call(
        norms_kernel,
        [],
        [total_4, total_5, total_6],
        [((2, width), F32) for width in (ci, ci, cf, cm, cm, co, co)],
        limit=SMALL,
    )
    if near_mesh:
        turned_2 = turn(far_2, held(near_2, grad_slow_in))
        pieces = cut_lines(turned_1, turned_2)
        sent = [xor_permute(piece, "mp", 2 * step) for step, piece in enumerate(pieces) if step]
        mine = held(pieces[0], (norms, lateral_after))
        total, raw_fast = along_line(mine, sent, mine.shape[1] - 512)
        raw_fast = lax.all_to_all(raw_fast, ("dp", "mp"), 0, 0, tiled=True)
        d_lateral = held(d_lateral, total)
    (grad_fast_in,) = local_call(
        fast_back_kernel,
        [],
        [
            mask, d_fast_0, d_fast_1, slow_parts[2], lateral_after, d_lateral, fast_cot,
            w_lateral.reshape(-1, cl), w_fast_a.reshape(-1, ci),
        ],
        [((rows * ALPHA, cf), BF)],
        [((rows * ALPHA, cf), F32), ((3 * lane, fw), BF)],
    )
    if near_mesh:
        sum_c, sum_s, sum_b, sum_a = cross_clips(
            total,
            [(cm, wide), (cu, wide), (9, part, cm), (3, part, cu)],
            [((wide, cu + cm), F32)],
            grad_fast_in,
        )
    else:
        sum_c, sum_s = sum_cs[:, cu:].T, sum_cs[:, :cu].T
        sum_b = sum_b.transpose(1, 0, 2)
    if near_mesh:
        raw_fast = held(raw_fast, sum_a)
    fast_a, fast_b, fast_c, grad_lateral = local_call(
        fast_results_kernel,
        [],
        [raw_fast],
        [((3, cf, ci), F32), ((9, ci, ci), F32), ((ci, cf), F32), ((5, cf, cl), F32)],
        [((2048, 128), BF)],
        limit=SMALL,
    )
    return (
        by_frame(fast_out.reshape(cells, fast_frames, cf)),
        slow_out,
        by_frame(grad_fast_in.reshape(cells, fast_frames, cf)),
        by_frame(grad_slow_in),
        fast_a,
        fast_b,
        fast_c,
        grad_lateral,
        jnp.swapaxes(sum_a, 1, 2),
        jnp.swapaxes(sum_b, 1, 2),
        sum_c,
        sum_s,
        *norms,
    )


def solution(mesh):
    frames = P("dp", "mp", None, None)
    last = P(None, None, "mp")
    wide = P(None, "mp")
    return jax.shard_map(
        per_device,
        mesh=mesh,
        in_specs=(frames, frames, P(), P(), P(), P(), P(), last, last, wide, wide)
        + (P(),) * 7
        + (frames, frames),
        out_specs=(frames,) * 4 + (P(),) * 4 + (last, last, wide, wide) + (P(),) * 7,
        check_vma=False,
    )
```

```python
import functools

import jax
import jax.numpy as jnp
import numpy as np
from jax import lax
from jax.experimental import pallas as pl
from jax.experimental.pallas import tpu as pltpu
from jax.sharding import PartitionSpec as P

H = 14
W = 14
ALPHA = 4
NORM_EPSILON = 1e-05
BF = jnp.bfloat16
F32 = jnp.float32


def xor_permute(values, axis, bits):
    count = lax.axis_size(axis)
    return lax.ppermute(values, axis, [(i, i ^ bits) for i in range(count)])


def cross_permute(values, turn):
    members = lax.axis_size("mp")
    pairs = []
    for clip in range(lax.axis_size("dp")):
        for place in range(members):
            over_x = (clip % 2 == 0) == (turn == 0)
            other = (clip ^ 2, place) if over_x else (clip, place ^ 1)
            pairs.append((clip * members + place, other[0] * members + other[1]))
    return lax.ppermute(values, ("dp", "mp"), pairs)


def shift_permute(values, axis, step):
    count = lax.axis_size(axis)
    return lax.ppermute(
        values, axis, [(i, i + step) for i in range(count) if 0 <= i + step < count]
    )


def small_mesh():
    return lax.axis_size("dp") == 4 and lax.axis_size("mp") == 8


def pick(values, index, axis):
    return lax.dynamic_index_in_dim(values, index, axis, keepdims=False)


FREE = pl.CostEstimate(flops=0, bytes_accessed=1, transcendentals=0)
VMEM = pl.BlockSpec(memory_space=pltpu.VMEM)
SMEM = pl.BlockSpec(memory_space=pltpu.SMEM)
LARGE = 56 * 2**20
SMALL = 16 * 2**20


class Sync:
    def __init__(self, copies_in, copies_out):
        self.copies_in, self.copies_out = copies_in, copies_out

    def arrive(self, *places):
        for place in places:
            self.copies_in[place].wait()

    def send(self, *places):
        for place in places:
            self.copies_out[place].start()


def local_call(
    kernel, scalars, arrays, outs, scratch=(), limit=LARGE, out_specs=None, late=(), early=()
):
    count, total = len(scalars), len(arrays)
    anywhere = pl.BlockSpec(memory_space=pl.ANY)
    in_specs = [SMEM] * count + [anywhere if k in late else VMEM for k in range(total)]
    out_specs = out_specs or [anywhere if k in early else VMEM for k in range(len(outs))]
    own = [pltpu.VMEM(s, d) for s, d in scratch]
    buffers = [pltpu.VMEM(arrays[k].shape, arrays[k].dtype) for k in late]
    buffers += [pltpu.VMEM(*outs[k]) for k in early]

    def body(*refs):
        refs = list(refs)
        first_out = count + total
        sems = refs.pop()
        spare = refs[len(refs) - len(buffers) :]
        refs = refs[: len(refs) - len(buffers)]
        copies_in, copies_out = {}, {}
        for i, k in enumerate(late):
            copies_in[k] = pltpu.make_async_copy(refs[count + k], spare[i], sems.at[i])
            copies_in[k].start()
            refs[count + k] = spare[i]
        for i, k in enumerate(early, len(late)):
            copies_out[k] = pltpu.make_async_copy(spare[i], refs[first_out + k], sems.at[i])
            refs[first_out + k] = spare[i]
        kernel(*refs, sync=Sync(copies_in, copies_out))
        for copy in copies_out.values():
            copy.wait()

    moved = len(late) + len(early)
    return pl.pallas_call(
        body if moved else kernel,
        out_shape=[jax.ShapeDtypeStruct(s, d) for s, d in outs],
        in_specs=in_specs,
        out_specs=out_specs,
        scratch_shapes=own + buffers + ([pltpu.SemaphoreType.DMA((moved,))] if moved else []),
        compiler_params=pltpu.CompilerParams(vmem_limit_bytes=limit),
        cost_estimate=FREE,
    )(*scalars, *arrays)


def quick_call(kernel, arrays, outs):
    return local_call(kernel, [], arrays, outs, limit=SMALL)


def this_core():
    return lax.rem(lax.axis_index("dp"), 2)


def place_call(kernel, pieces, outs):
    def body(*refs):
        me, core = lax.axis_index("mp"), this_core()
        side = lax.rem(me, 2)
        for k in range(4):
            owner_side = side if k % 2 == 0 else 1 - side
            half = core if k < 2 else 1 - core
            for far in range(4):
                line = jnp.bitwise_xor(me - side, 2 * far)
                kernel(line + owner_side, half, refs[k].at[far], *refs[4:])

    return local_call(body, [], pieces, [(shape, BF) for shape in outs], limit=32 * 2**20)


def stack_kernel(*refs):
    for k, ref in enumerate(refs[:-1]):
        refs[-1][k] = ref[...]


def line_pieces(mine):
    return [mine] + [xor_permute(mine, "mp", 2 * step) for step in (1, 2, 3)]


def stacked(pieces):
    return quick_call(stack_kernel, pieces, [((4,) + pieces[0].shape, BF)])[0]


def both_sides(near):
    side = xor_permute(near, "mp", 1)
    return near, side, xor_permute(near, "dp", 1), xor_permute(side, "dp", 1)


def place_a(block, half, piece, out):
    part = piece.shape[0] // 3
    width = out.shape[0] // 3
    for tap in range(3):
        start = pl.multiple_of(tap * width + block * (2 * part) + half * part, part)
        out[pl.ds(start, part), :] = piece[tap * part : (tap + 1) * part, :]


def place_bc(block, half, piece, out_f, out_b, out_c):
    width = out_f.shape[0]
    part = width // 16
    for tap in range(9):
        values = piece[tap * part : (tap + 1) * part, :]
        start = pl.multiple_of(block * (2 * part) + half * part, part)
        out_f[pl.ds(start, part), tap * width : (tap + 1) * width] = values
        start = pl.multiple_of((8 - tap) * width + block * (2 * part) + half * part, part)
        out_b[pl.ds(start, part), :] = values
    rest = piece.shape[0] - 9 * part
    columns = pl.ds(pl.multiple_of(block * 128, 128), 128)
    for k in range(2):
        start = pl.multiple_of(half * (2 * rest) + k * rest, rest)
        out_c[pl.ds(start, rest), columns] = piece[9 * part :, k * 128 : (k + 1) * 128]


def place_short(block, half, piece, out):
    part = piece.shape[0]
    columns = pl.ds(pl.multiple_of(block * 128, 128), 128)
    out[pl.ds(pl.multiple_of(half * part, part), part), columns] = piece[...]


def held(values, other):
    return lax.optimization_barrier((values, other))[0]


def shards_kernel(a_ref, b_ref, c_ref, s_ref, a_out, bc_out, s_out):
    core = this_core()
    half = a_ref.shape[1] // 2
    mine = pl.ds(pl.multiple_of(core * half, half), half)
    for tap in range(3):
        a_out[tap * half : (tap + 1) * half, :] = a_ref[tap, mine, :]
    for tap in range(9):
        bc_out[tap * half : (tap + 1) * half, :] = b_ref[tap, mine, :]
    rest = c_ref.shape[0] // 4
    for k in range(2):
        rows = pl.ds(pl.multiple_of(core * (2 * rest) + k * rest, rest), rest)
        bc_out[9 * half :, k * 128 : (k + 1) * 128] = c_ref[rows, :]
    size = s_out.shape[0]
    s_out[...] = s_ref[pl.ds(pl.multiple_of(core * size, size), size), :]


def own_halves(a_t, b_t, w_slow_c, w_short):
    half, cu = a_t.shape[1] // 2, a_t.shape[2]
    cm = b_t.shape[2]
    outs = [((3 * half, cu), BF), ((9 * half + cm // 4, cm), BF), ((cu // 2, 128), BF)]
    return quick_call(shards_kernel, [a_t, b_t, w_slow_c, w_short], outs)


def gather_whole(a_t, b_t, w_slow_c, w_short):
    wa = lax.all_gather(a_t, "mp", axis=1, tiled=True)
    wb = lax.all_gather(b_t, "mp", axis=1, tiled=True)
    wc = lax.all_gather(w_slow_c, "mp", axis=1, tiled=True)
    ws = lax.all_gather(w_short, "mp", axis=1, tiled=True)
    cm = wb.shape[1]
    wb_back = wb[::-1].reshape(9 * cm, cm)
    return wa.reshape(-1, wa.shape[2]), wb.transpose(1, 0, 2).reshape(cm, 9 * cm), wb_back, wc, ws


def plus(*values):
    total = values[0].astype(F32)
    for value in values[1:]:
        total = total + value.astype(F32)
    return total.astype(BF)


def columns_of(index, width):
    return pl.ds(pl.multiple_of(index * width, 128), width)


def swap_cores(send):
    return xor_permute(send, "dp", 1)


def row_groups(rows, width):
    return [(row, row // 16 * width) for row in range(0, rows, 16)]


def merge_kernel(*refs):
    count = len(refs) // 2 - 1
    keeps, sents, (far_ref, near_ref) = refs[:count], refs[count:-2], refs[-2:]
    core = this_core()
    x, side = lax.axis_index("dp") // 2, lax.rem(lax.axis_index("mp"), 2)
    total = near_ref.shape[2] // 2
    for q in range(2):
        for other, out_ref in ((0, near_ref), (1, far_ref)):
            own_x = x if other == 0 else 1 - x
            own_side = side if other == 0 else 1 - side
            column = jnp.where(core == 0, own_x, q)
            place = jnp.where(core == 0, q, own_side)
            first = q * total
            for keep, sent in zip(keeps, sents):
                width = keep.shape[2] // 2
                columns = columns_of(column, width)
                for row, start in row_groups(keep.shape[1], width):
                    for line in range(4):
                        block = 2 * line + place
                        out_ref[line, :, first + start : first + start + width] = plus(
                            keep[block, row : row + 16, columns], sent[block, row : row + 16, columns]
                        )
                first += keep.shape[1] // 16 * width


def turn_kernel(near_ref, sent_ref, far_out, near_out):
    x, side = lax.axis_index("dp") // 2, lax.rem(lax.axis_index("mp"), 2)
    mine = jnp.where(this_core() == 0, side, x)
    width = near_out.shape[2]
    for index, out_ref in ((mine, near_out), (1 - mine, far_out)):
        columns = columns_of(index, width)
        out_ref[...] = plus(near_ref[:, :, columns], sent_ref[:, :, columns])


def lines_kernel(near_ref, sent_ref, *out_refs):
    mine = lax.axis_index("mp") // 2
    for step, out_ref in enumerate(out_refs):
        place = jnp.bitwise_xor(mine, step)
        out_ref[...] = plus(near_ref[place], sent_ref[place])


def along_kernel(*refs):
    count = 4
    main_ref = refs[count]
    width = main_ref.shape[1]
    main_ref[...] = plus(*[ref[:, :width] for ref in refs[:count]])
    for fast_ref in refs[count + 1 :]:
        fast = plus(*[ref[:, width:] for ref in refs[:count]])
        fast_ref[...] = jnp.broadcast_to(fast[None], fast_ref.shape)


def merge(keeps, sents):
    columns = sum(keep.shape[1] // 16 * keep.shape[2] for keep in keeps)
    return quick_call(merge_kernel, [*keeps, *sents], [((4, 16, columns), BF)] * 2)


def turn(far, near):
    outs = [((4, 16, near.shape[2] // 2), BF)] * 2
    return quick_call(turn_kernel, [near, cross_permute(far, 0)], outs)


def cut_lines(far, near):
    arrays = [near, cross_permute(far, 1)]
    return quick_call(lines_kernel, arrays, [((16, near.shape[2]), BF)] * 4)


def along_line(mine, sent, width):
    outs = [((16, width), BF)]
    if mine.shape[1] > width:
        outs.append(((32, 16, mine.shape[1] - width), BF))
    return quick_call(along_kernel, [mine, *sent], outs)


def over_z(pieces):
    return [xor_permute(piece, "mp", 2 * step) for step, piece in enumerate(pieces) if step]


def clip_values(refs):
    core, x = this_core(), lax.axis_index("dp") // 2
    places = ((core, x), (core, 1 - x), (1 - core, x), (1 - core, 1 - x))
    return [(half, side, ref) for (half, side), ref in zip(places, refs)]


def clips_kernel(
    mine_ref, far_ref, other_ref, far_other_ref, c_ref, s_ref, b_ref, block_ref
):
    cu = s_ref.shape[0]
    wide = block_ref.shape[1] // 2
    half_rows = block_ref.shape[0] // 2
    for half, side, ref in clip_values((mine_ref, far_ref, other_ref, far_other_ref)):
        for group in range(half_rows // 16):
            rows = pl.ds(pl.multiple_of(half * half_rows + group * 16, 16), 16)
            values = ref[:, group * wide : (group + 1) * wide].astype(F32)
            block_ref[rows, columns_of(side, wide)] = values
        start = half_rows // 16 * wide
        count = b_ref.shape[0] * b_ref.shape[2] // 256
        rows = pl.ds(pl.multiple_of(half * 16, 16), 16)
        for k in range(count):
            unit = side * count + k
            columns = pl.ds(pl.multiple_of(lax.rem(unit, 2) * 128, 128), 128)
            values = ref[:, start + k * 128 : start + (k + 1) * 128].astype(F32)
            b_ref[unit // 2, rows, columns] = values
    for column in range(0, cu, 128):
        s_ref[column : column + 128, :] = block_ref[:, column : column + 128].T
    for column in range(cu, block_ref.shape[1], 128):
        c_ref[column - cu : column - cu + 128, :] = block_ref[:, column : column + 128].T


def clips_a_kernel(mine_ref, far_ref, other_ref, far_other_ref, a_ref):
    part = a_ref.shape[2] // 2
    for half, side, ref in clip_values((mine_ref, far_ref, other_ref, far_other_ref)):
        rows = pl.ds(pl.multiple_of(half * 16, 16), 16)
        for tap in range(3):
            values = ref[:, tap * part : (tap + 1) * part].astype(F32)
            a_ref[tap, rows, columns_of(side, part)] = values


def cross_clips(kernel, total, outs, scratch, other):
    sent = [xor_permute(total, "dp", bits) for bits in (2, 1, 3)]
    arrays = [held(total, other), *sent]
    return local_call(kernel, [], arrays, [(shape, F32) for shape in outs], scratch, SMALL)


def reduce_whole(blocks):
    whole = lax.psum(blocks.astype(BF), "dp")
    return lax.psum_scatter(whole, "mp", scatter_dimension=0, tiled=True)[0].astype(F32)


def tn(left, right):
    return lax.dot_general(left, right, (((0,), (0,)), ((), ())), preferred_element_type=F32)


def cut_halves(core, whole_ref, send_ref, keep_ref, groups=1):
    blocks, size = keep_ref.shape[0], keep_ref.shape[1] // groups
    for group in range(groups):
        for block in range(blocks):
            start = (group * blocks + block) * 2 * size
            place = slice(group * size, (group + 1) * size)
            send_ref[block, place, :] = whole_ref[pl.ds(pl.multiple_of(start + (1 - core) * size, size), size), :]
            keep_ref[block, place, :] = whole_ref[pl.ds(pl.multiple_of(start + core * size, size), size), :]


def grad_cs_kernel(dh_ref, ds_ref, joined_ref, hidden_ref, send_ref, keep_ref, whole_ref):
    wide, cu = dh_ref.shape[1], joined_ref.shape[1]
    for start in range(0, wide, 256):
        part = slice(start, start + 256)
        whole_ref[part, 0:cu] = tn(dh_ref[:, part], joined_ref[...]).astype(BF)
    whole_ref[:, cu:] = tn(ds_ref[...], hidden_ref[...]).astype(BF)
    cut_halves(this_core(), whole_ref, send_ref, keep_ref)


def fill_buffer(buffer, values_ref):
    clear_margins(buffer)
    for start in range(0, values_ref.shape[0], ROWS_STEP):
        rows = values_ref[start : start + ROWS_STEP, :].astype(F32)
        buffer[MARGIN + start : MARGIN + start + ROWS_STEP, :] = rows


def grad_b_kernel(
    ds_ref, hidden_ref, edge_ref, send_ref, keep_ref, whole_ref, buffer_ref, patches_ref
):
    fill_buffer(buffer_ref, hidden_ref)
    write_patches(buffer_ref, patches_ref, edge_ref)
    whole_ref[...] = tn(ds_ref[...], patches_ref[...]).astype(BF)
    cut_halves(this_core(), whole_ref, send_ref, keep_ref)


def grad_b_whole_kernel(
    ds_ref, hidden_ref, edge_ref, out_ref, buffer_ref, patches_ref
):
    fill_buffer(buffer_ref, hidden_ref)
    write_patches(buffer_ref, patches_ref, edge_ref)
    out_ref[...] = tn(ds_ref[...], patches_ref[...])


def grad_a_kernel(
    one_ref, two_ref, before_ref, after_ref, joined_ref, send_ref, keep_ref, whole_ref
):
    cm = whole_ref.shape[0] // 3
    pairs = ((two_ref, after_ref), (one_ref, two_ref), (before_ref, one_ref))
    for tap, (left_ref, right_ref) in enumerate(pairs):
        total = tn(left_ref[:, :cm], joined_ref[0]) + tn(right_ref[...], joined_ref[1])
        whole_ref[tap * cm : (tap + 1) * cm, :] = total.astype(BF)
    cut_halves(this_core(), whole_ref, send_ref, keep_ref, 3)


def leftward(values, j):
    return pltpu.roll(values, 128 - j * (128 // ALPHA), 1) if j else values


def fast_inner_kernel(
    hidden_a_ref, second_ref, hidden_ref, third_ref, edge_ref, out_ref, buffer_ref, patches_ref
):
    ci, cf = 128 // ALPHA, 128
    fill_buffer(buffer_ref, hidden_a_ref)
    write_patches(buffer_ref, patches_ref, edge_ref)
    raw = tn(patches_ref[...], second_ref[...])
    for tap in range(9):
        total = sum(
            leftward(raw[tap * 128 + j * ci : tap * 128 + (j + 1) * ci, :], j) for j in range(ALPHA)
        )
        out_ref[tap * ci : (tap + 1) * ci, :] = total.astype(BF)
    raw = tn(hidden_ref[...], third_ref[...])
    out_ref[9 * ci :, :] = sum(
        raw[j * ci : (j + 1) * ci, j * cf : (j + 1) * cf] for j in range(ALPHA)
    ).astype(BF)


def fast_outer_kernel(
    stack_ref, one_ref, two_ref, lateral_ref, dl_ref, inner_ref, send_ref, keep_ref, whole_ref
):
    cf = 128
    raw = tn(stack_ref[0], one_ref[...]) + tn(stack_ref[1], two_ref[...])
    whole_ref[0 : 3 * cf, :] = sum(
        leftward(raw[j * cf : (j + 3) * cf, :], j) for j in range(ALPHA)
    ).astype(BF)
    start = 3 * cf
    count = inner_ref.shape[0]
    whole_ref[start : start + count, :] = inner_ref[...]
    start += count
    raw = tn(lateral_ref[0], dl_ref[0]) + tn(lateral_ref[1], dl_ref[1])
    size = raw.shape[0]
    whole_ref[start : start + size, :] = raw[:, :128].astype(BF)
    whole_ref[start + size : start + 2 * size, :] = raw[:, 128:].astype(BF)
    start += 2 * size
    whole_ref[start:, :] = jnp.zeros((whole_ref.shape[0] - start, 128), BF)
    core = this_core()
    for half, out_ref in ((core, keep_ref), (1 - core, send_ref)):
        for block in range(8):
            for group in range(8):
                row = half * 1024 + block * 128 + group * 16
                rows = pl.ds(pl.multiple_of(row, 16), 16)
                out_ref[block, :, group * 128 : (group + 1) * 128] = whole_ref[rows, :]


def fast_whole_kernel(stack_ref, one_ref, two_ref, lateral_ref, dl_ref, inner_ref, out_ref):
    cf = 128
    raw = tn(stack_ref[0], one_ref[...]) + tn(stack_ref[1], two_ref[...])
    out_ref[0 : 3 * cf, :] = sum(leftward(raw[j * cf : (j + 3) * cf, :], j) for j in range(ALPHA))
    start = 3 * cf
    out_ref[start : start + inner_ref.shape[0], :] = inner_ref[...].astype(F32)
    start += inner_ref.shape[0]
    raw = tn(lateral_ref[0], dl_ref[0]) + tn(lateral_ref[1], dl_ref[1])
    size = raw.shape[0]
    out_ref[start : start + size, :] = raw[:, :128]
    out_ref[start + size : start + 2 * size, :] = raw[:, 128:]
    start += 2 * size
    out_ref[start:, :] = jnp.zeros((out_ref.shape[0] - start, 128), F32)


def first_kernel(
    count_ref, sums_ref, first_ref, gf_ref, gs_ref, vf_ref, vs_ref, afa_ref, asa_ref, mask_ref,
    f0_ref, f1_ref, s0_ref, s1_ref, total_ref, tile_ref,
):
    fast_count, slow_count = count_ref[0], count_ref[1]
    total = jnp.sum(sums_ref[...], axis=0)
    total_ref[...] = total
    cells = f0_ref.shape[0]
    fast_beta, fast_gamma, beta, gamma = split(total, (128, 128, 256, 256))
    ft, fq, st, sq = split(first_ref[...], (128, 128, 256, 256))
    mean, inverse = mean_inverse(fold_lanes(ft, ALPHA), fold_lanes(fq, ALPHA), fast_count)
    fast_lines = back_line(
        mean, inverse, tiled_affine(afa_ref, tile_ref)[0:1], fold_lanes(fast_beta, ALPHA), fold_lanes(fast_gamma, ALPHA), fast_count
    )
    slow_lines = back_line(*mean_inverse(st, sq, slow_count), asa_ref[0:1, :], beta, gamma, slow_count)
    for grad_ref, value_ref, outs, (one, two, three) in (
        (gf_ref, vf_ref, (f0_ref, f1_ref), fast_lines),
        (gs_ref, vs_ref, (s0_ref, s1_ref), slow_lines),
    ):
        for frame, out_ref in enumerate(outs):
            now = slice(frame * cells, (frame + 1) * cells)
            mask = wide_mask(mask_ref[now, :], grad_ref.shape[1])
            grad = mask * (grad_ref[now, :] * one - two - value_ref[now, :] * three)
            out_ref[...] = grad.astype(BF)


def joined_back_kernel(
    mask_ref, one_ref, two_ref, before_ref, after_ref, dh_ref, wa_ref, ws_ref, out_ref
):
    cells = one_ref.shape[0]
    cs = out_ref.shape[2]
    cm = wa_ref.shape[0] // 3
    for frame, pieces in enumerate(
        ((two_ref, one_ref, before_ref), (after_ref, two_ref, one_ref))
    ):
        mask = mask_ref[frame * cells : (frame + 1) * cells, :]
        taps = jnp.concatenate([piece[:, :cm] for piece in pieces], axis=1)
        for start in range(0, cs, 256):
            part = slice(start, start + 256)
            grad = mm(taps, wa_ref[:, part]) + mm_t(dh_ref[frame], ws_ref[part, :])
            out_ref[:, frame, part] = (grad * wide_mask(mask, 256)).astype(BF)


def lateral_back_kernel(
    mask_ref, one_ref, two_ref, before_ref, after_ref, fast_ref, dh_ref, wa_ref, ws_ref,
    lat_ref, edge_ref, a_ref, s_ref, sems,
):
    cells, cl = one_ref.shape[0], lat_ref.shape[2]
    cm = wa_ref.shape[0] // 3
    cs = ws_ref.shape[0] - cl
    copies = [
        pltpu.make_async_copy(wa_ref.at[:, pl.ds(cs, cl)], a_ref, sems.at[0]),
        pltpu.make_async_copy(ws_ref.at[pl.ds(cs, cl), :], s_ref, sems.at[1]),
    ]
    for copy in copies:
        copy.start()
    for copy in copies:
        copy.wait()
    for frame, pieces in enumerate(
        ((two_ref, one_ref, before_ref), (after_ref, two_ref, one_ref))
    ):
        mask = mask_ref[frame * cells : (frame + 1) * cells, :]
        taps = jnp.concatenate([piece[:, :cm] for piece in pieces], axis=1)
        grad = mm(taps, a_ref[...]) + mm_t(dh_ref[frame], s_ref[...])
        grad = (grad * wide_mask(mask, cl)).astype(BF)
        lat_ref[frame] = grad
        if frame == 0:
            edge_ref[:, :cl] = grad
            edge_ref[:, cl:] = fast_ref[...]


def lateral_back(arrays, outs):
    wa, ws = arrays[-2:]
    cl = outs[0][0][2]
    anywhere = pl.BlockSpec(memory_space=pl.ANY)
    return pl.pallas_call(
        lateral_back_kernel,
        out_shape=[jax.ShapeDtypeStruct(s, d) for s, d in outs],
        in_specs=[VMEM] * (len(arrays) - 2) + [anywhere] * 2,
        out_specs=[VMEM] * len(outs),
        scratch_shapes=[
            pltpu.VMEM((wa.shape[0], cl), BF),
            pltpu.VMEM((cl, ws.shape[1]), BF),
            pltpu.SemaphoreType.DMA((2,)),
        ],
        compiler_params=pltpu.CompilerParams(vmem_limit_bytes=LARGE),
        cost_estimate=FREE,
    )(*arrays)


def unpack_kernel(
    clip_ref, in_ref, mask_ref, out_ref, tail_ref, last_ref, head_ref, count_ref, rows_ref
):
    frames, cells = out_ref.shape[:2]
    step = frames * ALPHA
    pixels = H * W
    batch = cells // pixels
    total = sum(clip_ref[i, 0] for i in range(clip_ref.shape[0]))
    count_ref[1] = (total * pixels).astype(F32)
    count_ref[0] = (total * (pixels * ALPHA)).astype(F32)
    rows_ref[...] = in_ref[...].astype(F32)
    spot = lax.broadcasted_iota(jnp.int32, (cells, 128), 0)
    for frame in range(frames):
        place = lax.axis_index("mp") * frames + frame
        mask = jnp.zeros((cells, 128), F32)
        for b in range(batch):
            length = clip_ref[lax.axis_index("dp") * batch + b, 0]
            valid = (place < length).astype(F32)
            inside = (spot >= b * pixels) & (spot < (b + 1) * pixels)
            mask = jnp.where(inside, valid, mask)
        mask_ref[frame * cells : (frame + 1) * cells, :] = mask
        for j in range(ALPHA):
            values = rows_ref[pl.ds(frame * ALPHA + j, cells, step), :] * mask
            values = values.astype(BF)
            out_ref[frame, :, j * 128 : (j + 1) * 128] = values
            if frame == frames - 1 and j >= 2:
                (tail_ref, last_ref)[j - 2][...] = values
            if frame == 0 and j == 0:
                head_ref[...] = values


def copies():
    width = 128 // ALPHA
    lanes = jnp.bitwise_and(lax.broadcasted_iota(jnp.int32, (width, 128), 1), width - 1)
    rows = lax.broadcasted_iota(jnp.int32, (width, 128), 0)
    return jnp.where(lanes == rows, 1.0, 0.0).astype(BF)


def lane_mask(rows, j):
    group = lax.broadcasted_iota(jnp.int32, (rows, 128), 1) // (128 // ALPHA)
    return jnp.where(group == j, 1.0, 0.0)


def tiled_affine(ref, tile_ref):
    if ref.shape[1] == 128:
        return jnp.concatenate([ref[...]] * ALPHA, axis=1)
    tile_ref[...] = jnp.zeros_like(tile_ref)
    tile_ref[0:2, 0 : ref.shape[1]] = ref[...]
    return fold_lanes(tile_ref[0:2, :], ALPHA)


def build_a(w_ref, out_ref):
    tiles = mm(w_ref[...], copies())
    size = w_ref.shape[0] // 3
    masks = [lane_mask(size, j) for j in range(ALPHA)]
    for i in range(ALPHA + 2):
        total = sum(
            tiles[(i - j) * size : (i - j + 1) * size, :] * masks[j]
            for j in range(ALPHA)
            if 0 <= i - j < 3
        )
        out_ref[i * size : (i + 1) * size, :] = total.astype(BF)


def build_b(w_ref, out_ref, back):
    ci = w_ref.shape[1]
    for tap in range(9):
        block = w_ref[tap * ci : (tap + 1) * ci, :]
        tile = tn(block, copies()) if back else mm(block, copies())
        place = 8 - tap if back else tap
        for j in range(ALPHA):
            start = place * 128 + j * ci
            out_ref[start : start + ci, :] = (tile * lane_mask(ci, j)).astype(BF)


def build_c(w_ref, out_ref):
    ci, cf = w_ref.shape
    out_ref[...] = jnp.zeros_like(out_ref)
    for j in range(ALPHA):
        out_ref[j * ci : (j + 1) * ci, j * cf : (j + 1) * cf] = w_ref[...]


def build_back(w_ref, out_ref):
    ci = w_ref.shape[1]
    size = w_ref.shape[0] // 3
    one = jnp.where(
        lax.broadcasted_iota(jnp.int32, (ci, ci), 0) == lax.broadcasted_iota(jnp.int32, (ci, ci), 1),
        1.0,
        0.0,
    ).astype(BF)
    out_ref[...] = jnp.zeros_like(out_ref)
    for tap in range(3):
        block = mm_t(one, w_ref[tap * size : (tap + 1) * size, :]).astype(BF)
        for j in range(ALPHA):
            start = 128 + (j + 1 - tap) * ci
            out_ref[start : start + ci, j * size : (j + 1) * size] = block


def entry_kernel(
    mask_ref, fast_ref, before_ref, last_ref, after_ref, slow_ref, wa_ref, wl_ref,
    stack_ref, lateral_ref, first_ref, sums_ref, joined_ref, big_ref, rows_ref,
):
    cells = before_ref.shape[0]
    cs, cf = slow_ref.shape[2], 128
    build_a(wa_ref, big_ref)
    for column in range(0, cs, 128):
        values = slow_ref[:, :, column : column + 128].reshape(2 * cells, 128)
        rows_ref[column // 128] = values.astype(F32)
    tots, squares = [], []
    for frame in range(2):
        mask = mask_ref[frame * cells : (frame + 1) * cells, :]
        own = fast_ref[frame]
        past = (before_ref[...], last_ref[...])
        if frame:
            past = (fast_ref[0][:, 2 * cf : 3 * cf], fast_ref[0][:, 3 * cf :])
        following = fast_ref[1][:, :cf] if frame == 0 else after_ref[...]
        stack_ref[frame, :, 0:cf] = past[1]
        stack_ref[frame, :, cf : 5 * cf] = own
        stack_ref[frame, :, 5 * cf :] = following
        lateral_ref[frame, :, 0:cf] = past[0]
        lateral_ref[frame, :, cf : 2 * cf] = past[1]
        lateral_ref[frame, :, 2 * cf :] = own[:, : 3 * cf]
        value = mm(stack_ref[frame], big_ref[...])
        first_ref[frame * cells : (frame + 1) * cells, :] = value
        tots.append(total_row(value * mask))
        squares.append(total_row(value * mask * value))
        lateral = mm(lateral_ref[frame], wl_ref[...]).astype(BF)
        joined_ref[frame, :, cs:] = lateral * wide_mask(mask.astype(BF), 256)
        for column in range(0, cs, 128):
            values = rows_ref[column // 128, pl.ds(frame, cells, 2), :] * mask
            joined_ref[frame, :, column : column + 128] = values.astype(BF)
    sums_ref[:, :128] = tots[0] + tots[1]
    sums_ref[:, 128:] = squares[0] + squares[1]


def taps_kernel(joined_ref, wa_ref, base_ref, right_ref, left_ref, one_ref, two_ref):
    cells, cm = right_ref.shape
    one_ref[...] = mm_t(joined_ref[0], wa_ref[...])
    two_ref[...] = mm_t(joined_ref[1], wa_ref[...])
    base_ref[:cells, :] = one_ref[:, cm : 2 * cm] + two_ref[:, 2 * cm :]
    base_ref[cells:, :] = two_ref[:, cm : 2 * cm] + one_ref[:, :cm]
    right_ref[...] = two_ref[:, :cm].astype(BF)
    left_ref[...] = one_ref[:, 2 * cm :].astype(BF)


def first_sums_kernel(mask_ref, base_ref, left_ref, right_ref, fast_ref, first_ref, vec_ref):
    cells, cm = left_ref.shape
    tot = square = jnp.zeros((1, cm), F32)
    for frame, halo_ref in enumerate((left_ref, right_ref)):
        now = slice(frame * cells, (frame + 1) * cells)
        value = base_ref[now, :] + halo_ref[...].astype(F32)
        first_ref[now, :] = value
        masked = value * wide_mask(mask_ref[now, :], cm)
        tot = tot + total_row(masked)
        square = square + total_row(masked * value)
    send_all(vec_ref, [fast_ref[...], tot, square])


def sum_kernel(sums_ref, vec_ref):
    total = jnp.sum(sums_ref[...], axis=0)
    vec_ref[...] = jnp.broadcast_to(total[None], vec_ref.shape)


def fast_back_kernel(
    mask_ref, one_ref, two_ref, before_ref, after_ref, dl_ref, cot_ref, wl_ref, wa_ref,
    out_ref, rows_ref, big_ref,
):
    cells = one_ref.shape[0]
    cf = 128
    build_back(wa_ref, big_ref)
    for frame in range(2):
        now = slice(frame * cells, (frame + 1) * cells)
        mask = mask_ref[now, :]
        cl = dl_ref.shape[2]
        pieces = (before_ref[...], one_ref[...], two_ref[...])
        if frame:
            pieces = pieces[1:] + (after_ref[:, cl:],)
        taps = jnp.concatenate(pieces, axis=1)
        now_dl, next_dl = dl_ref[frame], after_ref[:, :cl] if frame else dl_ref[1]
        for j in range(ALPHA):
            part = slice(j * 128, (j + 1) * 128)
            grad = mm(taps, big_ref[:, part]) + cot_ref[now, part]
            if j < 3:
                grad = grad + mm_t(now_dl, wl_ref[(j + 2) * cf : (j + 3) * cf, :])
            if j >= 2:
                grad = grad + mm_t(next_dl, wl_ref[(j - 2) * cf : (j - 1) * cf, :])
            rows_ref[pl.ds(frame * ALPHA + j, cells, 2 * ALPHA), :] = grad * mask
    out_ref[...] = rows_ref[...].astype(BF)


def dot(left, right, left_dim, right_dim):
    return lax.dot_general(
        left, right, (((left_dim,), (right_dim,)), ((), ())), preferred_element_type=F32
    )


def rows_dot(left, right):
    return lax.dot_general(
        left, right, (((0, 1), (0, 1)), ((), ())), preferred_element_type=F32
    )


def folded(vector, groups):
    return jnp.sum(vector.reshape(groups, -1), axis=0)


def norm_terms(totals, squares, count, groups=1):
    average = totals / count
    inverse = lax.rsqrt(squares / count - average * average + NORM_EPSILON)
    return jnp.tile(average, groups), jnp.tile(inverse, groups)


ROWS_STEP = 112
TAPS = [(dh, dw) for dh in (-1, 0, 1) for dw in (-1, 0, 1)]


def row_chunks(rows, step):
    return [pl.ds(start, step) for start in range(0, rows, step)]


def loop_rows(rows, step, body, init):
    def turn(i, carry):
        return body(pl.ds(pl.multiple_of(i * step, step), step), carry)

    return lax.fori_loop(0, rows // step, turn, init)


def collapse(values):
    return jnp.sum(values.reshape(-1, 8, values.shape[-1]), axis=0)


def gate_of(values):
    return 0.5 * jnp.tanh(0.5 * values) + 0.5


def fold_lanes(vector, groups):
    width = vector.shape[-1] // groups
    total = vector
    for j in range(1, groups):
        total = total + pltpu.roll(vector, j * width, 1)
    return total


def mean_inverse(totals, squares, count):
    average = totals / count
    return average, lax.rsqrt(squares / count - average * average + NORM_EPSILON)


def line(average, inverse, affine):
    scale = affine[0:1] * inverse
    return scale, affine[1:2] - average * scale


def send_all(vec_ref, pieces):
    start = 0
    for piece in pieces:
        width = piece.shape[-1]
        spread = jnp.broadcast_to(piece[None], (vec_ref.shape[0], 1, width))
        vec_ref[:, :, start : start + width] = spread
        start += width


def received(sums_ref, widths):
    total = jnp.sum(sums_ref[...], axis=0)
    return split(total, widths)


def split(total, widths):
    pieces = []
    start = 0
    for width in widths:
        pieces.append(total[:, start : start + width])
        start += width
    return pieces


def total_row(vector):
    return jnp.sum(vector, axis=0, keepdims=True)


MARGIN = 16


def clear_margins(buffer):
    rows = buffer.shape[0]
    zeros = jnp.zeros((MARGIN, buffer.shape[1]), F32)
    buffer[0:MARGIN, :] = zeros
    buffer[rows - MARGIN : rows, :] = zeros


def write_patches(buffer, patches, edges):
    rows, channels = patches.shape[0], buffer.shape[1]
    for start in range(0, rows, ROWS_STEP):
        top, bottom, left, right = (edges[k, start : start + ROWS_STEP, :] for k in range(4))
        for tap, (dh, dw) in enumerate(TAPS):
            mask = None
            if dh:
                mask = top if dh < 0 else bottom
            if dw:
                side = left if dw < 0 else right
                mask = side if mask is None else mask * side
            offset = MARGIN + start + W * dh + dw
            for column in range(0, channels, 128):
                piece = buffer[offset : offset + ROWS_STEP, column : column + 128]
                if mask is not None:
                    piece = piece * mask
                place = tap * channels + column
                patches[start : start + ROWS_STEP, place : place + 128] = piece.astype(BF)


def mm(left, right):
    return jnp.dot(left, right, preferred_element_type=F32)


def mm_t(left, right):
    return lax.dot_general(left, right, (((1,), (1,)), ((), ())), preferred_element_type=F32)


def wide_mask(mask, width):
    return jnp.concatenate([mask] * (width // 128), axis=1) if width > 128 else mask


def conv_kernel(
    count_ref, sums_ref, vf_ref, vs_ref, af_ref, as_ref, mask_ref, edge_ref, wf_ref, ws_ref,
    hf_ref, hs_ref, of_ref, os_ref, total_ref, vec_ref, bf_ref, bs_ref, pf_ref, ps_ref, big_ref, tile_ref,
):
    fast_count, slow_count = count_ref[0], count_ref[1]
    total = jnp.sum(sums_ref[...], axis=0)
    total_ref[...] = total
    ft, fq, st, sq = split(total, (128, 128, 256, 256))
    lines = []
    build_b(wf_ref, big_ref, False)
    for tot, square, count, affine in ((ft, fq, fast_count, af_ref), (st, sq, slow_count, as_ref)):
        if tot.shape[-1] == 128:
            tot, square = fold_lanes(tot, ALPHA), fold_lanes(square, ALPHA)
            affine = tiled_affine(affine, tile_ref)
        else:
            affine = affine[...]
        lines.append(line(*mean_inverse(tot, square, count), affine))
    rows = vf_ref.shape[0]
    for value_ref, hidden_ref, buffer, (scale, shift) in (
        (vf_ref, hf_ref, bf_ref, lines[0]),
        (vs_ref, hs_ref, bs_ref, lines[1]),
    ):
        width = value_ref.shape[1]
        clear_margins(buffer)
        for start in range(0, rows, ROWS_STEP):
            z = value_ref[start : start + ROWS_STEP, :] * scale + shift
            hidden = z * gate_of(z) * wide_mask(mask_ref[start : start + ROWS_STEP, :], width)
            buffer[MARGIN + start : MARGIN + start + ROWS_STEP, :] = hidden
            hidden_ref[start : start + ROWS_STEP, :] = hidden.astype(BF)
    write_patches(bf_ref, pf_ref, edge_ref)
    write_patches(bs_ref, ps_ref, edge_ref)
    of_ref[...] = mm(pf_ref[...], big_ref[...])
    os_ref[...] = mm_t(ps_ref[...], ws_ref[...])
    pieces = []
    for out_ref in (of_ref, os_ref):
        width = out_ref.shape[1]

        def body(rows_now, carry):
            value = out_ref[rows_now, :]
            masked = value * wide_mask(mask_ref[rows_now, :], width)
            return carry[0] + collapse(masked), carry[1] + collapse(masked * value)

        zero = jnp.zeros((8, width), F32)
        pieces += [total_row(v) for v in loop_rows(rows, ROWS_STEP, body, (zero, zero))]
    send_all(vec_ref, pieces)


def expand_kernel(
    count_ref, sums_ref, short_ref, vf_ref, vs_ref, af_ref, as_ref, mask_ref, wf_ref, ws_ref,
    hf_ref, hs_ref, yf_ref, ys_ref, total_ref, vec_ref, of_ref, os_ref, big_ref, tile_ref,
):
    fast_count, slow_count = count_ref[0], count_ref[1]
    total = jnp.sum(sums_ref[...], axis=0)
    total_ref[...] = total
    ft, fq, st, sq = split(total, (128, 128, 256, 256))
    ft, fq = fold_lanes(ft, ALPHA), fold_lanes(fq, ALPHA)
    build_c(wf_ref, big_ref)
    lines = (
        line(*mean_inverse(ft, fq, fast_count), tiled_affine(af_ref, tile_ref)),
        line(*mean_inverse(st, sq, slow_count), as_ref[...]),
    )
    rows = vf_ref.shape[0]
    for value_ref, hidden_ref, (scale, shift) in ((vf_ref, hf_ref, lines[0]), (vs_ref, hs_ref, lines[1])):
        width = value_ref.shape[1]

        def body(rows_now, carry):
            z = value_ref[rows_now, :] * scale + shift
            hidden = z * gate_of(z) * wide_mask(mask_ref[rows_now, :], width)
            hidden_ref[rows_now, :] = hidden.astype(BF)
            return carry

        loop_rows(rows, ROWS_STEP, body, 0)
    of_ref[...] = mm(hf_ref[...], big_ref[...])
    os_ref[...] = mm(hs_ref[...], ws_ref[...])
    pieces = []
    for out_ref, low_ref in ((of_ref, yf_ref), (os_ref, ys_ref)):
        width = out_ref.shape[1]
        tots, squares = [], []
        for column in range(0, width, 512):

            def body(rows_now, carry):
                value = out_ref[rows_now, column : column + 512]
                low_ref[rows_now, column : column + 512] = value.astype(low_ref.dtype)
                value = value.astype(low_ref.dtype).astype(F32)
                masked = value * wide_mask(mask_ref[rows_now, :], 512)
                return carry[0] + collapse(masked), carry[1] + collapse(masked * value)

            zero = jnp.zeros((8, 512), F32)
            one, two = loop_rows(rows, 16, body, (zero, zero))
            tots.append(total_row(one))
            squares.append(total_row(two))
        if width == 512:
            pieces += [sum(v[:, j * 128 : (j + 1) * 128] for j in range(ALPHA)) for v in (tots[0], squares[0])]
        else:
            pieces += [jnp.concatenate(tots, 1), jnp.concatenate(squares, 1)]
    send_all(vec_ref, pieces + [short_ref[...]])


def short_kernel(mask_ref, joined_ref, ws_ref, out_ref, vec_ref):
    rows, wide = out_ref.shape
    for column in range(0, wide, 256):
        part = slice(column, column + 256)
        one = jnp.zeros((8, 256), F32)
        two = one
        for start in range(0, rows, 2 * ROWS_STEP):
            now = slice(start, min(start + 2 * ROWS_STEP, rows))
            value = mm(joined_ref[now, :], ws_ref[:, part])
            out_ref[now, part] = value.astype(BF)
            value = value.astype(BF).astype(F32)
            masked = value * wide_mask(mask_ref[now, :], 256)
            one = one + collapse(masked)
            two = two + collapse(masked * value)
        vec_ref[:, part] = total_row(one)
        vec_ref[:, wide + column : wide + column + 256] = total_row(two)


def output_kernel(
    count_ref, sums_ref, vf_ref, vs_ref, vh_ref, fast_ref, cf_ref, cs_ref,
    af_ref, as_ref, ah_ref, mask_ref,
    yf_ref, ys_ref, gf_ref, gs_ref, total_ref, vec_ref, rows_ref, cots_ref, *, sync,
):
    fast_count, slow_count = count_ref[0], count_ref[1]
    total = jnp.sum(sums_ref[...], axis=0)
    total_ref[...] = total
    wide = vs_ref.shape[1]
    ft, fq, st, sq, ht, hq = split(total, (128, 128, wide, wide, wide, wide))
    rows = vf_ref.shape[0]
    mean, inverse = mean_inverse(ft, fq, fast_count)
    mean, inverse = (jnp.concatenate([v] * ALPHA, 1) for v in (mean, inverse))
    scale, shift = line(mean, inverse, tiled_affine(af_ref, None))

    frames, cells = fast_ref.shape[:2]
    step = frames * ALPHA
    cots_ref[...] = cf_ref[...].astype(F32)
    zero = jnp.zeros((8, 512), F32)
    beta = gamma = jnp.zeros((1, 128), F32)
    for frame in range(frames):
        now = slice(frame * cells, (frame + 1) * cells)
        for j in range(ALPHA):
            part = slice(j * 128, (j + 1) * 128)
            place = pl.ds(frame * ALPHA + j, cells, step)
            mask = mask_ref[now, :]
            value = vf_ref[now, part]
            z = value * scale[:, part] + shift[:, part] + fast_ref[frame, :, part].astype(F32)
            gate = gate_of(z)
            rows_ref[place, :] = mask * z * gate
            grad = cots_ref[place, :] * mask * gate * (1.0 + z * (1.0 - gate))
            gf_ref[now, part] = grad
            beta = beta + total_row(grad)
            gamma = gamma + total_row(grad * value)
    yf_ref[...] = rows_ref[...].astype(BF)
    sync.send(0, 2)
    sync.arrive(2, 3, 6)
    pieces = [beta, (gamma - mean[:, :128] * beta) * inverse[:, :128]]
    mean_c, inverse_c = mean_inverse(st, sq, slow_count)
    mean_h, inverse_h = mean_inverse(ht, hq, slow_count)
    scale_c, shift_c = line(mean_c, inverse_c, as_ref[...])
    scale_h, shift_h = line(mean_h, inverse_h, ah_ref[...])
    betas, gammas, others = [], [], []
    for column in range(0, wide, 512):
        part = slice(column, column + 512)
        sc, sh, shift_both = scale_c[:, part], scale_h[:, part], shift_c[:, part] + shift_h[:, part]

        def body(rows_now, carry):
            third, short = vs_ref[rows_now, part].astype(F32), vh_ref[rows_now, part].astype(F32)
            mask = wide_mask(mask_ref[rows_now, :], 512)
            z = third * sc + short * sh + shift_both
            gate = gate_of(z)
            ys_ref[rows_now, part] = (mask * z * gate).astype(BF)
            grad = cs_ref[rows_now, part].astype(F32) * mask * gate * (1.0 + z * (1.0 - gate))
            gs_ref[rows_now, part] = grad.astype(BF)
            grad = grad.astype(BF).astype(F32)
            return (
                carry[0] + collapse(grad),
                carry[1] + collapse(grad * third),
                carry[2] + collapse(grad * short),
            )

        beta, gamma, other = (total_row(v) for v in loop_rows(rows, 16, body, (zero, zero, zero)))
        betas.append(beta)
        gammas.append((gamma - mean_c[:, part] * beta) * inverse_c[:, part])
        others.append((other - mean_h[:, part] * beta) * inverse_h[:, part])
    pieces += [jnp.concatenate(v, 1) for v in (betas, gammas, others)]
    sync.send(1, 3)
    send_all(vec_ref, pieces)


def back_line(mean, inverse, scale, beta, gamma, count):
    first = inverse * scale
    third = first * gamma * inverse / count
    return first, first * beta / count - mean * third, third


def narrow_kernel(
    count_ref, sums_ref, third_ref, second_ref,
    gf_ref, gs_ref, vf_ref, vs_ref, vh_ref, uf_ref, us_ref,
    afc_ref, asc_ref, ash_ref, afb_ref, asb_ref, mask_ref, wf_ref, ws_ref,
    df_ref, ds_ref, dh_ref, of_ref, os_ref, total_ref, vec_ref, big_ref, tile_ref, *, sync,
):
    fast_count, slow_count = count_ref[0], count_ref[1]
    total = jnp.sum(sums_ref[...], axis=0)
    total_ref[...] = total
    wide = vs_ref.shape[1]
    rows = vf_ref.shape[0]
    fast_beta, fast_gamma, beta, gamma_c, gamma_h = split(total, (128, 128, wide, wide, wide))
    ft, fq, st, sq, ht, hq = split(third_ref[...], (128, 128, wide, wide, wide, wide))
    mean, inverse = mean_inverse(ft, fq, fast_count)
    tiled = [jnp.concatenate([v] * ALPHA, 1) for v in (mean, inverse, fast_beta, fast_gamma)]
    build_c(wf_ref, big_ref)
    f1, f2, f3 = back_line(tiled[0], tiled[1], tiled_affine(afc_ref, None)[0:1], tiled[2], tiled[3], fast_count)

    def fast_body(rows_now, carry):
        mask = wide_mask(mask_ref[rows_now, :], 512)
        grad = mask * (gf_ref[rows_now, :].astype(F32) * f1 - f2 - vf_ref[rows_now, :].astype(F32) * f3)
        df_ref[rows_now, :] = grad.astype(BF)
        return carry

    loop_rows(rows, 16, fast_body, 0)
    sync.send(0)
    sync.arrive(4, 6, 7)
    mean_c, inverse_c = mean_inverse(st, sq, slow_count)
    mean_h, inverse_h = mean_inverse(ht, hq, slow_count)
    lines_c = back_line(mean_c, inverse_c, asc_ref[0:1, :], beta, gamma_c, slow_count)
    lines_h = back_line(mean_h, inverse_h, ash_ref[0:1, :], beta, gamma_h, slow_count)
    for column in range(0, wide, 512):
        part = slice(column, column + 512)
        c1, c2, c3 = (v[:, part] for v in lines_c)
        h1, h2, h3 = (v[:, part] for v in lines_h)

        def body(rows_now, carry):
            mask = wide_mask(mask_ref[rows_now, :], 512)
            grad = gs_ref[rows_now, part].astype(F32)
            third, short = vs_ref[rows_now, part].astype(F32), vh_ref[rows_now, part].astype(F32)
            ds_ref[rows_now, part] = (mask * (grad * c1 - c2 - third * c3)).astype(BF)
            dh_ref[rows_now, part] = (mask * (grad * h1 - h2 - short * h3)).astype(BF)
            return carry

        loop_rows(rows, 16, body, 0)
    sync.send(1, 2)
    sync.arrive(8, 9, 17)
    of_ref[...] = mm_t(df_ref[...], big_ref[...])
    os_ref[...] = mm_t(ds_ref[...], ws_ref[...])
    ft, fq, st, sq = split(second_ref[...], (128, 128, 256, 256))
    pieces = slope_sums(
        (of_ref, uf_ref, tiled_affine(afb_ref, tile_ref), fold_lanes(ft, ALPHA), fold_lanes(fq, ALPHA), fast_count),
        (os_ref, us_ref, asb_ref, st, sq, slow_count),
        mask_ref,
    )
    send_all(vec_ref, pieces)


def slope_sums(fast_parts, slow_parts, mask_ref):
    pieces = []
    for out_ref, value_ref, affine, tot, square, count in (fast_parts, slow_parts):
        width = out_ref.shape[1]
        mean, inverse = mean_inverse(tot, square, count)
        scale, shift = line(mean, inverse, affine[...])

        def body(rows_now, carry):
            value = value_ref[rows_now, :]
            z = value * scale + shift
            gate = gate_of(z)
            mask = wide_mask(mask_ref[rows_now, :], width)
            grad = out_ref[rows_now, :] * mask * gate * (1.0 + z * (1.0 - gate))
            out_ref[rows_now, :] = grad
            return carry[0] + collapse(grad), carry[1] + collapse(grad * value)

        zero = jnp.zeros((8, width), F32)
        rows = out_ref.shape[0]
        beta, gamma = (total_row(v) for v in loop_rows(rows, ROWS_STEP // 2, body, (zero, zero)))
        pieces += [beta, (gamma - mean * beta) * inverse]
    return pieces


def conv_back_kernel(
    count_ref, sums_ref, second_ref, first_ref,
    gf_ref, gs_ref, uf_ref, us_ref, vf_ref, vs_ref,
    afb_ref, asb_ref, afa_ref, asa_ref, mask_ref, edge_ref, wf_ref, ws_ref,
    df_ref, ds_ref, of_ref, os_ref, total_ref, vec_ref,
    bf_ref, bs_ref, pf_ref, ps_ref, big_ref, tile_ref,
):
    fast_count, slow_count = count_ref[0], count_ref[1]
    total = jnp.sum(sums_ref[...], axis=0)
    total_ref[...] = total
    rows = gf_ref.shape[0]
    build_b(wf_ref, big_ref, True)
    fast_beta, fast_gamma, beta, gamma = split(total, (128, 128, 256, 256))
    ft, fq, st, sq = split(second_ref[...], (128, 128, 256, 256))
    mean, inverse = mean_inverse(fold_lanes(ft, ALPHA), fold_lanes(fq, ALPHA), fast_count)
    fast_lines = back_line(
        mean, inverse, tiled_affine(afb_ref, tile_ref)[0:1], fold_lanes(fast_beta, ALPHA), fold_lanes(fast_gamma, ALPHA), fast_count
    )
    slow_lines = back_line(*mean_inverse(st, sq, slow_count), asb_ref[0:1, :], beta, gamma, slow_count)
    for grad_ref, value_ref, out_ref, buffer, lines in (
        (gf_ref, uf_ref, df_ref, bf_ref, fast_lines),
        (gs_ref, us_ref, ds_ref, bs_ref, slow_lines),
    ):
        width = grad_ref.shape[1]
        one, two, three = lines
        clear_margins(buffer)
        for start in range(0, rows, ROWS_STEP):
            now = slice(start, start + ROWS_STEP)
            grad = grad_ref[now, :] * one - two - value_ref[now, :] * three
            grad = grad * wide_mask(mask_ref[now, :], width)
            out_ref[now, :] = grad.astype(BF)
            buffer[MARGIN + start : MARGIN + start + ROWS_STEP, :] = grad
    write_patches(bf_ref, pf_ref, edge_ref)
    write_patches(bs_ref, ps_ref, edge_ref)
    of_ref[...] = mm(pf_ref[...], big_ref[...])
    os_ref[...] = mm(ps_ref[...], ws_ref[...])
    ft, fq, st, sq = split(first_ref[...], (128, 128, 256, 256))
    pieces = slope_sums(
        (of_ref, vf_ref, tiled_affine(afa_ref, tile_ref), fold_lanes(ft, ALPHA), fold_lanes(fq, ALPHA), fast_count),
        (os_ref, vs_ref, asa_ref, st, sq, slow_count),
        mask_ref,
    )
    send_all(vec_ref, pieces)


def exchange(vec):
    return lax.all_to_all(vec, ("dp", "mp"), 0, 0, tiled=True)


def fast_results_kernel(in_ref, a_ref, b_ref, c_ref, l_ref, rows_ref):
    if len(in_ref.shape) == 3:
        for device in range(in_ref.shape[0]):
            x, core, block = device // 16, device // 8 % 2, device % 8
            for k in range(4):
                start = core * 1024 + block * 128 + (x * 4 + k) * 16
                rows_ref[start : start + 16, :] = in_ref[device, :, k * 128 : (k + 1) * 128]
        in_ref = rows_ref
    taps, cf, ci = a_ref.shape
    for tap in range(taps):
        a_ref[tap] = in_ref[tap * cf : (tap + 1) * cf, :].astype(F32)[:, :ci]
    start = taps * cf
    for tap in range(9):
        b_ref[tap] = in_ref[start + tap * ci : start + (tap + 1) * ci, :].astype(F32)[:, :ci]
    start += 9 * ci
    c_ref[...] = in_ref[start : start + ci, :].astype(F32)
    start += ci
    for side in range(2):
        for tap in range(5):
            rows = slice(start + (side * 5 + tap) * cf, start + (side * 5 + tap + 1) * cf)
            l_ref[tap, :, side * 128 : (side + 1) * 128] = in_ref[rows, :].astype(F32)


def norms_kernel(c_ref, b_ref, a_ref, fa_ref, fb_ref, fc_ref, sa_ref, sb_ref, sc_ref, sh_ref):
    wide = sc_ref.shape[1]
    beta, gamma, slow, gamma_c, gamma_h = split(c_ref[...], (128, 128, wide, wide, wide))
    for out_ref, scale, shift in (
        (fc_ref, gamma, beta), (sc_ref, gamma_c, slow), (sh_ref, gamma_h, slow)
    ):
        out_ref[0:1, :] = scale
        out_ref[1:2, :] = shift
    for in_ref, fast_ref, slow_ref in ((b_ref, fb_ref, sb_ref), (a_ref, fa_ref, sa_ref)):
        width, cm = fast_ref.shape[1], slow_ref.shape[1]
        beta, gamma, slow, slow_gamma = split(in_ref[...], (128, 128, cm, cm))
        fast_ref[0:1, :] = fold_lanes(gamma, ALPHA)[:, :width]
        fast_ref[1:2, :] = fold_lanes(beta, ALPHA)[:, :width]
        slow_ref[0:1, :] = slow_gamma
        slow_ref[1:2, :] = slow


def per_device(
    fast_in,
    slow_in,
    clip_len,
    w_fast_a,
    w_fast_b,
    w_fast_c,
    w_lateral,
    w_slow_a,
    w_slow_b,
    w_slow_c,
    w_short,
    norm_fast_a,
    norm_fast_b,
    norm_fast_c,
    norm_slow_a,
    norm_slow_b,
    norm_slow_c,
    norm_short,
    cot_fast,
    cot_slow,
):
    batch, fast_frames, pixels, cf = fast_in.shape
    frames, cs = slow_in.shape[1], slow_in.shape[3]
    cells = batch * pixels
    ci = w_fast_a.shape[2]
    cl = w_lateral.shape[2]
    co = norm_slow_c.shape[1]
    cm = norm_slow_a.shape[1]
    cu = cs + cl
    mp = lax.axis_size("mp")
    me = lax.axis_index("mp")

    part, wide = w_slow_a.shape[2], w_short.shape[1]
    rows = frames * cells
    lane, fw = ALPHA * ci, ALPHA * cf
    small = 2 * lane + 2 * cm
    dp = lax.axis_size("dp")
    devices = dp * mp
    near_mesh = small_mesh()
    spot = np.arange(rows) % pixels
    edges = np.stack([spot >= W, spot < pixels - W, spot % W > 0, spot % W < W - 1])
    edges = jnp.asarray(np.repeat(edges.astype(np.float32)[:, :, None], 128, axis=2))
    buffers = [((rows + 2 * MARGIN, lane), F32), ((rows + 2 * MARGIN, cm), F32)]
    patches = [((rows, 9 * lane), BF), ((rows, 9 * cm), BF)]
    tile = ((8, 128), F32)

    def flat(values):
        return values.reshape(-1, values.shape[-1])

    def framed(values):
        return values.reshape(frames, cells, values.shape[-1])

    def by_pixel(values):
        return values.transpose(0, 2, 1, 3).reshape(cells, -1, values.shape[-1])

    def by_frame(values):
        return values.reshape(batch, pixels, -1, values.shape[-1]).transpose(0, 2, 1, 3)

    shards = jnp.swapaxes(w_slow_a, 1, 2), jnp.swapaxes(w_slow_b, 1, 2), w_slow_c, w_short
    if near_mesh:
        mine_a, mine_bc, mine_short = own_halves(*shards)
        line_a = line_pieces(mine_a)
        fast_in = held(fast_in, mine_a)
    mask, fast, tail, last, head, counts = local_call(
        unpack_kernel,
        [clip_len],
        [flat(by_pixel(fast_in))],
        [
            ((rows, 128), F32), ((frames, cells, fw), BF), ((cells, cf), BF), ((cells, cf), BF),
            ((cells, cf), BF), ((2,), F32),
        ],
        [((rows * ALPHA, cf), F32)],
        out_specs=[VMEM] * 5 + [SMEM],
    )
    if near_mesh:
        tail, last, head = held((tail, last, head), line_a[1])
    before = [shift_permute(values, "mp", 1) for values in (tail, last)]
    following = shift_permute(head, "mp", -1)
    if near_mesh:
        near_a = stacked(held(line_a, (before, following)))
    fast_stack, lateral_stack, fast_first, fast_sums, joined = local_call(
        entry_kernel,
        [],
        [
            mask, fast, *before, following, by_pixel(slow_in), w_fast_a.reshape(-1, ci),
            w_lateral.reshape(-1, cl),
        ],
        [
            ((frames, cells, 6 * cf), BF), ((frames, cells, 5 * cf), BF), ((rows, lane), F32),
            ((1, 2 * lane), F32), ((frames, cells, cu), BF),
        ],
        [((6 * cf, lane), BF), ((cs // 128, rows, 128), F32)],
    )

    if near_mesh:
        near_bc = stacked(held(line_pieces(held(mine_bc, near_a)), joined))
        line_short = line_pieces(held(mine_short, near_a))
        side_a = held(xor_permute(near_a, "mp", 1), (joined, near_bc))
        pieces_a = near_a, side_a, swap_cores(near_a), swap_cores(side_a)
        wa = place_call(place_a, pieces_a, [(3 * cm, cu)])[0]
    else:
        wa, wb, wb_back, wc, ws = gather_whole(*shards)
    base, to_right, to_left = local_call(
        taps_kernel,
        [],
        [joined, wa],
        [((rows, cm), F32), ((cells, cm), BF), ((cells, cm), BF)],
        [((cells, 3 * cm), F32)] * 2,
    )
    left = shift_permute(to_right, "mp", 1)
    right = shift_permute(to_left, "mp", -1)
    if near_mesh:
        pieces_bc = both_sides(near_bc)
        base = held(base, pieces_bc)
        near_short = stacked(held(line_short, (left, right)))
    slow_first, vec = local_call(
        first_sums_kernel,
        [],
        [mask, base, left, right, fast_sums],
        [((rows, cm), F32), ((devices, 1, small), F32)],
    )
    if near_mesh:
        wb, wb_back, wc = place_call(
            place_bc, pieces_bc, [(cm, 9 * cm), (9 * cm, cm), (cm, 8 * wide)]
        )
        side_short = xor_permute(near_short, "mp", 1)
        sums = held(exchange(vec), (wb, side_short))
    else:
        sums = exchange(vec)

    wfb = w_fast_b.reshape(-1, ci)
    hidden_a, hidden_c, fast_second, slow_second, total_1, vec = local_call(
        conv_kernel,
        [counts],
        [sums, fast_first, slow_first, norm_fast_a, norm_slow_a, mask, edges, wfb, wb],
        [
            ((rows, lane), BF), ((rows, cm), BF), ((rows, lane), F32), ((rows, cm), F32),
            ((1, small), F32), ((devices, 1, small), F32),
        ],
        buffers + patches + [((9 * lane, lane), BF), tile],
    )

    if near_mesh:
        side_short = held(side_short, vec)
        pieces = near_short, side_short, swap_cores(near_short), swap_cores(side_short)
        ws = place_call(place_short, pieces, [(cu, 8 * wide)])[0]
    shortcut, short_vec = local_call(
        short_kernel, [], [mask, flat(joined), ws], [((rows, co), BF), ((1, 2 * co), F32)]
    )
    sums = held(exchange(vec), short_vec)
    hidden_b, hidden_d, fast_third, slow_third, total_2, vec = local_call(
        expand_kernel,
        [counts],
        [sums, short_vec, fast_second, slow_second, norm_fast_b, norm_slow_b, mask, w_fast_c, wc],
        [
            ((rows, lane), BF), ((rows, cm), BF), ((rows, fw), F32), ((rows, co), BF),
            ((1, small), F32), ((dp, 1, 2 * cf + 4 * co), F32),
        ],
        [((rows, fw), F32), ((rows, co), F32), ((lane, fw), BF), tile],
    )
    slow_cots = held(cot_slow, vec).transpose(1, 0, 2, 3).reshape(frames, cells, co)
    slow_cots = flat(slow_cots)
    sums = lax.all_to_all(vec, "dp", 0, 0, tiled=True)
    (vec,) = quick_call(sum_kernel, [sums], [((mp, 1, vec.shape[2]), F32)])
    sums = lax.all_to_all(vec, "mp", 0, 0, tiled=True)

    fast_out, slow_out, fast_cot, slow_cot, total_3, vec = local_call(
        output_kernel,
        [counts],
        [
            sums, fast_third, slow_third, shortcut, fast, flat(by_pixel(cot_fast)),
            slow_cots, norm_fast_c, norm_slow_c, norm_short, mask,
        ],
        [
            ((rows * ALPHA, cf), BF), ((rows, co), BF), ((rows, fw), F32), ((rows, co), BF),
            ((1, 2 * cf + 4 * co), F32), ((devices, 1, 2 * cf + 3 * co), F32),
        ],
        [((rows * ALPHA, cf), F32)] * 2,
        late=(2, 3, 6),
        early=(0, 1, 2, 3),
    )
    slow_out = framed(slow_out).reshape(frames, batch, pixels, co).transpose(1, 0, 2, 3)
    sums = held(exchange(vec), slow_out)

    d_fast_third, d_slow_third, d_short, grad_fb, grad_sb, total_4, vec = local_call(
        narrow_kernel,
        [counts],
        [
            sums, total_3, total_2, fast_cot, slow_cot, fast_third, slow_third, shortcut,
            fast_second, slow_second, norm_fast_c, norm_slow_c, norm_short, norm_fast_b, norm_slow_b,
            mask, w_fast_c, wc,
        ],
        [
            ((rows, fw), BF), ((rows, co), BF), ((rows, co), BF), ((rows, lane), F32),
            ((rows, cm), F32), ((1, 2 * cf + 3 * co), F32), ((devices, 1, small), F32),
        ],
        [((lane, fw), BF), tile],
        late=(4, 6, 7, 8, 9, 17),
        early=(0, 1, 2),
    )

    def weight_grad(kernel, arrays, size, length, total, scratch=()):
        halves = ((mp, size, length), BF)
        return local_call(kernel, [], arrays, [halves, halves], [((total, length), BF), *scratch])

    if near_mesh:
        raw_cs = weight_grad(
            grad_cs_kernel, [d_short, d_slow_third, flat(joined), hidden_d], wide // 2, cu + cm, co
        )
        sums, raw_cs = lax.optimization_barrier((exchange(vec), raw_cs))
        sent_cs = swap_cores(raw_cs[0])
    else:
        raw_cs = jnp.concatenate(
            [rows_dot(framed(d_short), joined), rows_dot(framed(d_slow_third), framed(hidden_d))], -1
        )
        sum_cs = reduce_whole(raw_cs.reshape(mp, 2, wide // 2, cu + cm)).reshape(wide, cu + cm)
        sums = exchange(vec)

    d_fast_second, d_slow_second, grad_fa, grad_sa, total_5, vec = local_call(
        conv_back_kernel,
        [counts],
        [
            sums, total_2, total_1, grad_fb, grad_sb, fast_second, slow_second, fast_first,
            slow_first, norm_fast_b, norm_slow_b, norm_fast_a, norm_slow_a, mask, edges, wfb, wb_back,
        ],
        [
            ((rows, lane), BF), ((rows, cm), BF), ((rows, lane), F32), ((rows, cm), F32),
            ((1, small), F32), ((devices, 1, small), F32),
        ],
        buffers + patches + [((9 * lane, lane), BF), tile],
    )
    grad_b_scratch = [buffers[1], patches[1]]
    if near_mesh:
        raw_b = weight_grad(
            grad_b_kernel, [d_slow_second, hidden_c, edges], part // 2, 9 * cm, cm, grad_b_scratch
        )
        sums, raw_b = lax.optimization_barrier((exchange(vec), raw_b))
        sent_b = swap_cores(raw_b[0])
    else:
        (raw_b,) = local_call(
            grad_b_whole_kernel,
            [],
            [d_slow_second, hidden_c, edges],
            [((cm, 9 * cm), F32)],
            grad_b_scratch,
        )
        sum_b = reduce_whole(raw_b.reshape(mp, 2, part // 2, 9 * cm)).reshape(part, 9, cm)
        sums = exchange(vec)
    d_fast_0, d_fast_1, d_slow_0, d_slow_1, total_6 = local_call(
        first_kernel,
        [counts],
        [sums, total_1, grad_fa, grad_sa, fast_first, slow_first, norm_fast_a, norm_slow_a, mask],
        [((cells, lane), BF)] * 2 + [((cells, cm), BF)] * 2 + [((1, small), F32)],
        [tile],
    )
    slow_parts = [
        d_slow_0, d_slow_1, shift_permute(d_slow_1, "mp", 1), shift_permute(d_slow_0, "mp", -1)
    ]
    (fast_inner,) = local_call(
        fast_inner_kernel,
        [],
        [held(hidden_a, d_slow_0), d_fast_second, hidden_b, d_fast_third, edges],
        [((10 * ci, 128), BF)],
        [buffers[0], patches[0]],
    )
    if near_mesh:
        far_1, near_1 = merge((raw_cs[1], held(raw_b[1], d_slow_0)), (sent_cs, sent_b))
        raw_a = weight_grad(
            grad_a_kernel, held(slow_parts, (far_1, fast_inner)) + [joined], 3 * part // 2, cu, 3 * cm
        )
        sent_a = swap_cores(raw_a[0])
        slow_parts = held(slow_parts, raw_a)
    else:
        three = jnp.stack(
            [
                jnp.concatenate([d_slow_1, slow_parts[3]]),
                jnp.concatenate([d_slow_0, d_slow_1]),
                jnp.concatenate([slow_parts[2][:, :cm], d_slow_0]),
            ]
        )
        raw_a = jnp.einsum("kro,rc->koc", three, flat(joined), preferred_element_type=F32)
        raw_a = raw_a.reshape(3, mp, 2, part // 2, cu).transpose(1, 2, 0, 3, 4)
        sum_a = reduce_whole(raw_a.reshape(mp, 2, 3 * part // 2, cu))
        sum_a = sum_a.reshape(2, 3, part // 2, cu).transpose(1, 0, 2, 3).reshape(3, part, cu)
    d_lateral, lateral_edge = lateral_back(
        [mask, *slow_parts, d_fast_0, framed(d_short), wa, ws],
        [((frames, cells, cl), BF), ((cells, cl + lane), BF)],
    )
    lateral_after = shift_permute(lateral_edge, "mp", -1)
    fast_before = shift_permute(held(d_fast_1, d_lateral), "mp", 1)
    fast_outer = [fast_stack, d_fast_0, d_fast_1, lateral_stack, d_lateral, fast_inner]
    if near_mesh:
        half_fast = ((8, 16, 1024), BF)
        fast_send, fast_keep = local_call(
            fast_outer_kernel, [], fast_outer, [half_fast] * 2, [((2048, 128), BF)]
        )
        turned_1 = turn(far_1, near_1)
        keeps = raw_a[1], held(fast_keep, turned_1)
        far_2, near_2 = merge(keeps, (sent_a, swap_cores(fast_send)))
        slow_parts = held(slow_parts, far_2)
    else:
        (raw_fast,) = local_call(fast_whole_kernel, [], fast_outer, [((2048, 128), F32)])
        raw_fast = lax.psum(raw_fast, ("dp", "mp"))
    (grad_slow_in,) = local_call(
        joined_back_kernel,
        [],
        [mask, *slow_parts, framed(d_short), wa, ws],
        [((cells, frames, cs), BF)],
    )
    norms = local_call(
        norms_kernel,
        [],
        [total_4, total_5, total_6],
        [((2, width), F32) for width in (ci, ci, cf, cm, cm, co, co)],
        limit=SMALL,
    )
    if near_mesh:
        pieces_1 = cut_lines(turned_1[0], held(turned_1[1], grad_slow_in))
        sent_1 = over_z(pieces_1)
        pieces_2 = cut_lines(*turn(far_2, held(near_2, pieces_1)))
        sent_2 = over_z(pieces_2)
        (total_1,) = along_line(held(pieces_1[0], pieces_2), sent_1, pieces_1[0].shape[1])
        sum_c, sum_s, sum_b = cross_clips(
            clips_kernel,
            total_1,
            [(cm, wide), (cu, wide), (9, part, cm)],
            [((wide, cu + cm), F32)],
            norms,
        )
        mine = held(pieces_2[0], (lateral_after, fast_before, sum_c))
        total, raw_fast = along_line(mine, sent_2, mine.shape[1] - 512)
        raw_fast = lax.all_to_all(raw_fast, ("dp", "mp"), 0, 0, tiled=True)
        d_lateral = held(d_lateral, total)
    (grad_fast_in,) = local_call(
        fast_back_kernel,
        [],
        [
            mask, d_fast_0, d_fast_1, fast_before, lateral_after, d_lateral, fast_cot,
            w_lateral.reshape(-1, cl), w_fast_a.reshape(-1, ci),
        ],
        [((rows * ALPHA, cf), BF)],
        [((rows * ALPHA, cf), F32), ((3 * lane, fw), BF)],
    )
    if near_mesh:
        (sum_a,) = cross_clips(clips_a_kernel, total, [(3, part, cu)], [], grad_fast_in)
    else:
        sum_c, sum_s = sum_cs[:, cu:].T, sum_cs[:, :cu].T
        sum_b = sum_b.transpose(1, 0, 2)
    if near_mesh:
        raw_fast = held(raw_fast, sum_a)
    fast_a, fast_b, fast_c, grad_lateral = local_call(
        fast_results_kernel,
        [],
        [raw_fast],
        [((3, cf, ci), F32), ((9, ci, ci), F32), ((ci, cf), F32), ((5, cf, cl), F32)],
        [((2048, 128), BF)],
        limit=SMALL,
    )
    return (
        by_frame(fast_out.reshape(cells, fast_frames, cf)),
        slow_out,
        by_frame(grad_fast_in.reshape(cells, fast_frames, cf)),
        by_frame(grad_slow_in),
        fast_a,
        fast_b,
        fast_c,
        grad_lateral,
        jnp.swapaxes(sum_a, 1, 2),
        jnp.swapaxes(sum_b, 1, 2),
        sum_c,
        sum_s,
        *norms,
    )


def solution(mesh):
    frames = P("dp", "mp", None, None)
    last = P(None, None, "mp")
    wide = P(None, "mp")
    return jax.shard_map(
        per_device,
        mesh=mesh,
        in_specs=(frames, frames, P(), P(), P(), P(), P(), last, last, wide, wide)
        + (P(),) * 7
        + (frames, frames),
        out_specs=(frames,) * 4 + (P(),) * 4 + (last, last, wide, wide) + (P(),) * 7,
        check_vma=False,
    )
```

```python
import functools

import jax
import jax.numpy as jnp
import numpy as np
from jax import lax
from jax.experimental import pallas as pl
from jax.experimental.pallas import tpu as pltpu
from jax.sharding import PartitionSpec as P

H = 14
W = 14
ALPHA = 4
NORM_EPSILON = 1e-05
BF = jnp.bfloat16
F32 = jnp.float32


def xor_permute(values, axis, bits):
    count = lax.axis_size(axis)
    return lax.ppermute(values, axis, [(i, i ^ bits) for i in range(count)])


def cross_permute(values, turn):
    members = lax.axis_size("mp")
    pairs = []
    for clip in range(lax.axis_size("dp")):
        for place in range(members):
            over_x = (clip % 2 == 0) == (turn == 0)
            other = (clip ^ 2, place) if over_x else (clip, place ^ 1)
            pairs.append((clip * members + place, other[0] * members + other[1]))
    return lax.ppermute(values, ("dp", "mp"), pairs)


def shift_permute(values, axis, step):
    count = lax.axis_size(axis)
    return lax.ppermute(
        values, axis, [(i, i + step) for i in range(count) if 0 <= i + step < count]
    )


def small_mesh():
    return lax.axis_size("dp") == 4 and lax.axis_size("mp") == 8


def pick(values, index, axis):
    return lax.dynamic_index_in_dim(values, index, axis, keepdims=False)


FREE = pl.CostEstimate(flops=0, bytes_accessed=1, transcendentals=0)
VMEM = pl.BlockSpec(memory_space=pltpu.VMEM)
SMEM = pl.BlockSpec(memory_space=pltpu.SMEM)
LARGE = 56 * 2**20
SMALL = 16 * 2**20


class Sync:
    def __init__(self, copies_in, copies_out):
        self.copies_in, self.copies_out = copies_in, copies_out

    def arrive(self, *places):
        for place in places:
            self.copies_in[place].wait()

    def send(self, *places):
        for place in places:
            self.copies_out[place].start()


def local_call(
    kernel, scalars, arrays, outs, scratch=(), limit=LARGE, out_specs=None, late=(), early=()
):
    count, total = len(scalars), len(arrays)
    anywhere = pl.BlockSpec(memory_space=pl.ANY)
    in_specs = [SMEM] * count + [anywhere if k in late else VMEM for k in range(total)]
    out_specs = out_specs or [anywhere if k in early else VMEM for k in range(len(outs))]
    own = [pltpu.VMEM(s, d) for s, d in scratch]
    buffers = [pltpu.VMEM(arrays[k].shape, arrays[k].dtype) for k in late]
    buffers += [pltpu.VMEM(*outs[k]) for k in early]

    def body(*refs):
        refs = list(refs)
        first_out = count + total
        sems = refs.pop()
        spare = refs[len(refs) - len(buffers) :]
        refs = refs[: len(refs) - len(buffers)]
        copies_in, copies_out = {}, {}
        for i, k in enumerate(late):
            copies_in[k] = pltpu.make_async_copy(refs[count + k], spare[i], sems.at[i])
            copies_in[k].start()
            refs[count + k] = spare[i]
        for i, k in enumerate(early, len(late)):
            copies_out[k] = pltpu.make_async_copy(spare[i], refs[first_out + k], sems.at[i])
            refs[first_out + k] = spare[i]
        kernel(*refs, sync=Sync(copies_in, copies_out))
        for copy in copies_out.values():
            copy.wait()

    moved = len(late) + len(early)
    return pl.pallas_call(
        body if moved else kernel,
        out_shape=[jax.ShapeDtypeStruct(s, d) for s, d in outs],
        in_specs=in_specs,
        out_specs=out_specs,
        scratch_shapes=own + buffers + ([pltpu.SemaphoreType.DMA((moved,))] if moved else []),
        compiler_params=pltpu.CompilerParams(vmem_limit_bytes=limit),
        cost_estimate=FREE,
    )(*scalars, *arrays)


def quick_call(kernel, arrays, outs):
    return local_call(kernel, [], arrays, outs, limit=SMALL)


def this_core():
    return lax.rem(lax.axis_index("dp"), 2)


def place_pieces(kernel, pieces, outs):
    me, core = lax.axis_index("mp"), this_core()
    side = lax.rem(me, 2)
    for k in range(4):
        owner_side = side if k % 2 == 0 else 1 - side
        half = core if k < 2 else 1 - core
        for far in range(4):
            line = jnp.bitwise_xor(me - side, 2 * far)
            kernel(line + owner_side, half, pieces[k].at[far], *outs)


def place_call(kernel, pieces, outs):
    def body(*refs):
        place_pieces(kernel, refs[:4], refs[4:])

    return local_call(body, [], pieces, [(shape, BF) for shape in outs], limit=32 * 2**20)


def stack_kernel(*refs):
    for k, ref in enumerate(refs[:-1]):
        refs[-1][k] = ref[...]


def line_pieces(mine):
    return [mine] + [xor_permute(mine, "mp", 2 * step) for step in (1, 2, 3)]


def stacked(pieces):
    return quick_call(stack_kernel, pieces, [((4,) + pieces[0].shape, BF)])[0]


def both_sides(near):
    side = xor_permute(near, "mp", 1)
    return near, side, xor_permute(near, "dp", 1), xor_permute(side, "dp", 1)


def place_a(block, half, piece, out):
    part = piece.shape[0] // 3
    width = out.shape[0] // 3
    for tap in range(3):
        start = pl.multiple_of(tap * width + block * (2 * part) + half * part, part)
        out[pl.ds(start, part), :] = piece[tap * part : (tap + 1) * part, :]


def place_bc(block, half, piece, out_f, out_b, out_c):
    width = out_f.shape[0]
    part = width // 16
    for tap in range(9):
        values = piece[tap * part : (tap + 1) * part, :]
        start = pl.multiple_of(block * (2 * part) + half * part, part)
        out_f[pl.ds(start, part), tap * width : (tap + 1) * width] = values
        start = pl.multiple_of((8 - tap) * width + block * (2 * part) + half * part, part)
        out_b[pl.ds(start, part), :] = values
    rest = piece.shape[0] - 9 * part
    columns = pl.ds(pl.multiple_of(block * 128, 128), 128)
    for k in range(2):
        start = pl.multiple_of(half * (2 * rest) + k * rest, rest)
        out_c[pl.ds(start, rest), columns] = piece[9 * part :, k * 128 : (k + 1) * 128]


def place_short(block, half, piece, out):
    part = piece.shape[0]
    columns = pl.ds(pl.multiple_of(block * 128, 128), 128)
    out[pl.ds(pl.multiple_of(half * part, part), part), columns] = piece[...]


def held(values, other):
    return lax.optimization_barrier((values, other))[0]


def shards_kernel(a_ref, b_ref, c_ref, s_ref, a_out, bc_out, s_out):
    core = this_core()
    half = a_ref.shape[1] // 2
    mine = pl.ds(pl.multiple_of(core * half, half), half)
    for tap in range(3):
        a_out[tap * half : (tap + 1) * half, :] = a_ref[tap, mine, :]
    for tap in range(9):
        bc_out[tap * half : (tap + 1) * half, :] = b_ref[tap, mine, :]
    rest = c_ref.shape[0] // 4
    for k in range(2):
        rows = pl.ds(pl.multiple_of(core * (2 * rest) + k * rest, rest), rest)
        bc_out[9 * half :, k * 128 : (k + 1) * 128] = c_ref[rows, :]
    size = s_out.shape[0]
    s_out[...] = s_ref[pl.ds(pl.multiple_of(core * size, size), size), :]


def own_halves(a_t, b_t, w_slow_c, w_short):
    half, cu = a_t.shape[1] // 2, a_t.shape[2]
    cm = b_t.shape[2]
    outs = [((3 * half, cu), BF), ((9 * half + cm // 4, cm), BF), ((cu // 2, 128), BF)]
    return quick_call(shards_kernel, [a_t, b_t, w_slow_c, w_short], outs)


def gather_whole(a_t, b_t, w_slow_c, w_short):
    wa = lax.all_gather(a_t, "mp", axis=1, tiled=True)
    wb = lax.all_gather(b_t, "mp", axis=1, tiled=True)
    wc = lax.all_gather(w_slow_c, "mp", axis=1, tiled=True)
    ws = lax.all_gather(w_short, "mp", axis=1, tiled=True)
    cm = wb.shape[1]
    wb_back = wb[::-1].reshape(9 * cm, cm)
    return wa.reshape(-1, wa.shape[2]), wb.transpose(1, 0, 2).reshape(cm, 9 * cm), wb_back, wc, ws


def plus(*values):
    total = values[0].astype(F32)
    for value in values[1:]:
        total = total + value.astype(F32)
    return total.astype(BF)


def columns_of(index, width):
    return pl.ds(pl.multiple_of(index * width, 128), width)


def swap_cores(send):
    return xor_permute(send, "dp", 1)


def row_groups(rows, width):
    return [(row, row // 16 * width) for row in range(0, rows, 16)]


def merge_kernel(*refs):
    count = len(refs) // 2 - 1
    keeps, sents, (far_ref, near_ref) = refs[:count], refs[count:-2], refs[-2:]
    core = this_core()
    x, side = lax.axis_index("dp") // 2, lax.rem(lax.axis_index("mp"), 2)
    total = near_ref.shape[2] // 2
    for q in range(2):
        for other, out_ref in ((0, near_ref), (1, far_ref)):
            own_x = x if other == 0 else 1 - x
            own_side = side if other == 0 else 1 - side
            column = jnp.where(core == 0, own_x, q)
            place = jnp.where(core == 0, q, own_side)
            first = q * total
            for keep, sent in zip(keeps, sents):
                width = keep.shape[2] // 2
                columns = columns_of(column, width)
                for row, start in row_groups(keep.shape[1], width):
                    for line in range(4):
                        block = 2 * line + place
                        out_ref[line, :, first + start : first + start + width] = plus(
                            keep[block, row : row + 16, columns], sent[block, row : row + 16, columns]
                        )
                first += keep.shape[1] // 16 * width


def turn_kernel(near_ref, sent_ref, far_out, near_out):
    x, side = lax.axis_index("dp") // 2, lax.rem(lax.axis_index("mp"), 2)
    mine = jnp.where(this_core() == 0, side, x)
    width = near_out.shape[2]
    for index, out_ref in ((mine, near_out), (1 - mine, far_out)):
        columns = columns_of(index, width)
        out_ref[...] = plus(near_ref[:, :, columns], sent_ref[:, :, columns])


def lines_kernel(near_ref, sent_ref, *out_refs):
    mine = lax.axis_index("mp") // 2
    for step, out_ref in enumerate(out_refs):
        place = jnp.bitwise_xor(mine, step)
        out_ref[...] = plus(near_ref[place], sent_ref[place])


def along_kernel(*refs):
    count = 4
    main_ref = refs[count]
    width = main_ref.shape[1]
    main_ref[...] = plus(*[ref[:, :width] for ref in refs[:count]])
    for fast_ref in refs[count + 1 :]:
        fast = plus(*[ref[:, width:] for ref in refs[:count]])
        fast_ref[...] = jnp.broadcast_to(fast[None], fast_ref.shape)


def merge(keeps, sents):
    columns = sum(keep.shape[1] // 16 * keep.shape[2] for keep in keeps)
    return quick_call(merge_kernel, [*keeps, *sents], [((4, 16, columns), BF)] * 2)


def turn(far, near):
    outs = [((4, 16, near.shape[2] // 2), BF)] * 2
    return quick_call(turn_kernel, [near, cross_permute(far, 0)], outs)


def cut_lines(far, near):
    arrays = [near, cross_permute(far, 1)]
    return quick_call(lines_kernel, arrays, [((16, near.shape[2]), BF)] * 4)


def along_line(mine, sent, width):
    outs = [((16, width), BF)]
    if mine.shape[1] > width:
        outs.append(((32, 16, mine.shape[1] - width), BF))
    return quick_call(along_kernel, [mine, *sent], outs)


def over_z(pieces):
    return [xor_permute(piece, "mp", 2 * step) for step, piece in enumerate(pieces) if step]


def clip_values(refs):
    core, x = this_core(), lax.axis_index("dp") // 2
    places = ((core, x), (core, 1 - x), (1 - core, x), (1 - core, 1 - x))
    return [(half, side, ref) for (half, side), ref in zip(places, refs)]


def clips_kernel(
    mine_ref, far_ref, other_ref, far_other_ref, c_ref, s_ref, b_ref, block_ref
):
    cu = s_ref.shape[0]
    wide = block_ref.shape[1] // 2
    half_rows = block_ref.shape[0] // 2
    for half, side, ref in clip_values((mine_ref, far_ref, other_ref, far_other_ref)):
        for group in range(half_rows // 16):
            rows = pl.ds(pl.multiple_of(half * half_rows + group * 16, 16), 16)
            values = ref[:, group * wide : (group + 1) * wide].astype(F32)
            block_ref[rows, columns_of(side, wide)] = values
        start = half_rows // 16 * wide
        count = b_ref.shape[0] * b_ref.shape[2] // 256
        rows = pl.ds(pl.multiple_of(half * 16, 16), 16)
        for k in range(count):
            unit = side * count + k
            columns = pl.ds(pl.multiple_of(lax.rem(unit, 2) * 128, 128), 128)
            values = ref[:, start + k * 128 : start + (k + 1) * 128].astype(F32)
            b_ref[unit // 2, rows, columns] = values
    for column in range(0, cu, 128):
        s_ref[column : column + 128, :] = block_ref[:, column : column + 128].T
    for column in range(cu, block_ref.shape[1], 128):
        c_ref[column - cu : column - cu + 128, :] = block_ref[:, column : column + 128].T


def clips_a_kernel(mine_ref, far_ref, other_ref, far_other_ref, a_ref):
    part = a_ref.shape[2] // 2
    for half, side, ref in clip_values((mine_ref, far_ref, other_ref, far_other_ref)):
        rows = pl.ds(pl.multiple_of(half * 16, 16), 16)
        for tap in range(3):
            values = ref[:, tap * part : (tap + 1) * part].astype(F32)
            a_ref[tap, rows, columns_of(side, part)] = values


def cross_clips(kernel, total, outs, scratch, other):
    sent = [xor_permute(total, "dp", bits) for bits in (2, 1, 3)]
    arrays = [held(total, other), *sent]
    return local_call(kernel, [], arrays, [(shape, F32) for shape in outs], scratch, SMALL)


def reduce_whole(blocks):
    whole = lax.psum(blocks.astype(BF), "dp")
    return lax.psum_scatter(whole, "mp", scatter_dimension=0, tiled=True)[0].astype(F32)


def tn(left, right):
    return lax.dot_general(left, right, (((0,), (0,)), ((), ())), preferred_element_type=F32)


def cut_halves(core, whole_ref, send_ref, keep_ref, groups=1):
    blocks, size = keep_ref.shape[0], keep_ref.shape[1] // groups
    for group in range(groups):
        for block in range(blocks):
            start = (group * blocks + block) * 2 * size
            place = slice(group * size, (group + 1) * size)
            send_ref[block, place, :] = whole_ref[pl.ds(pl.multiple_of(start + (1 - core) * size, size), size), :]
            keep_ref[block, place, :] = whole_ref[pl.ds(pl.multiple_of(start + core * size, size), size), :]


def grad_cs_kernel(dh_ref, ds_ref, joined_ref, hidden_ref, send_ref, keep_ref, whole_ref):
    wide, cu = dh_ref.shape[1], joined_ref.shape[1]
    for start in range(0, wide, 256):
        part = slice(start, start + 256)
        whole_ref[part, 0:cu] = tn(dh_ref[:, part], joined_ref[...]).astype(BF)
    whole_ref[:, cu:] = tn(ds_ref[...], hidden_ref[...]).astype(BF)
    cut_halves(this_core(), whole_ref, send_ref, keep_ref)


def fill_buffer(buffer, values_ref):
    clear_margins(buffer)
    for start in range(0, values_ref.shape[0], ROWS_STEP):
        rows = values_ref[start : start + ROWS_STEP, :].astype(F32)
        buffer[MARGIN + start : MARGIN + start + ROWS_STEP, :] = rows


def grad_b_kernel(
    ds_ref, hidden_ref, edge_ref, send_ref, keep_ref, whole_ref, buffer_ref, patches_ref
):
    fill_buffer(buffer_ref, hidden_ref)
    write_patches(buffer_ref, patches_ref, edge_ref)
    whole_ref[...] = tn(ds_ref[...], patches_ref[...]).astype(BF)
    cut_halves(this_core(), whole_ref, send_ref, keep_ref)


def grad_b_whole_kernel(
    ds_ref, hidden_ref, edge_ref, out_ref, buffer_ref, patches_ref
):
    fill_buffer(buffer_ref, hidden_ref)
    write_patches(buffer_ref, patches_ref, edge_ref)
    out_ref[...] = tn(ds_ref[...], patches_ref[...])


def grad_a_kernel(
    one_ref, two_ref, before_ref, after_ref, joined_ref, send_ref, keep_ref, whole_ref
):
    cm = whole_ref.shape[0] // 3
    pairs = ((two_ref, after_ref), (one_ref, two_ref), (before_ref, one_ref))
    for tap, (left_ref, right_ref) in enumerate(pairs):
        total = tn(left_ref[:, :cm], joined_ref[0]) + tn(right_ref[...], joined_ref[1])
        whole_ref[tap * cm : (tap + 1) * cm, :] = total.astype(BF)
    cut_halves(this_core(), whole_ref, send_ref, keep_ref, 3)


def leftward(values, j):
    return pltpu.roll(values, 128 - j * (128 // ALPHA), 1) if j else values


def packed(values, groups):
    size, width = values.shape[0] // groups, 128 // groups
    mask = lane_mask(size, 0)
    total = values[:size, :] * mask
    for k in range(1, groups):
        total = total + pltpu.roll(values[k * size : (k + 1) * size, :] * mask, k * width, 1)
    return total


def unpacked(values, groups):
    return [leftward(values, k) for k in range(groups)]


def fast_inner_kernel(
    hidden_a_ref, second_ref, hidden_ref, third_ref, edge_ref, out_ref, buffer_ref, patches_ref
):
    ci, cf = 128 // ALPHA, 128
    fill_buffer(buffer_ref, hidden_a_ref)
    write_patches(buffer_ref, patches_ref, edge_ref)
    raw = tn(patches_ref[...], second_ref[...])
    taps = [
        sum(leftward(raw[tap * 128 + j * ci : tap * 128 + (j + 1) * ci, :], j) for j in range(ALPHA))
        for tap in range(9)
    ]
    both = packed(jnp.concatenate(taps, axis=0), ALPHA)
    start = out_ref.shape[0] - ci
    rest = jnp.zeros((start - both.shape[0], 128), F32)
    out_ref[:start, :] = jnp.concatenate([both, rest], axis=0).astype(BF)
    raw = tn(hidden_ref[...], third_ref[...])
    out_ref[start:, :] = sum(
        raw[j * ci : (j + 1) * ci, j * cf : (j + 1) * cf] for j in range(ALPHA)
    ).astype(BF)


FAST_ROWS = 1536


def outer_rows(stack_ref, one_ref, two_ref, lateral_ref, dl_ref, inner_ref, out_ref):
    cf, kind = 128, out_ref.dtype
    raw = tn(stack_ref[0], one_ref[...]) + tn(stack_ref[1], two_ref[...])
    total = sum(leftward(raw[j * cf : (j + 3) * cf, :], j) for j in range(ALPHA))
    start = 3 * cf // ALPHA
    out_ref[:start, :] = packed(total, ALPHA).astype(kind)
    count = inner_ref.shape[0]
    out_ref[start : start + count, :] = inner_ref[...].astype(kind)
    start += count
    raw = tn(lateral_ref[0], dl_ref[0]) + tn(lateral_ref[1], dl_ref[1])
    size = raw.shape[0]
    out_ref[start : start + size, :] = raw[:, :128].astype(kind)
    out_ref[start + size : start + 2 * size, :] = raw[:, 128:].astype(kind)
    start += 2 * size
    out_ref[start:, :] = jnp.zeros((out_ref.shape[0] - start, 128), kind)


def fast_outer_kernel(
    stack_ref, one_ref, two_ref, lateral_ref, dl_ref, inner_ref, send_ref, keep_ref, whole_ref
):
    outer_rows(stack_ref, one_ref, two_ref, lateral_ref, dl_ref, inner_ref, whole_ref)
    core = this_core()
    groups = FAST_ROWS // 256
    for half, out_ref in ((core, keep_ref), (1 - core, send_ref)):
        for block in range(8):
            for group in range(groups):
                row = half * (FAST_ROWS // 2) + (block * groups + group) * 16
                rows = pl.ds(pl.multiple_of(row, 16), 16)
                out_ref[block, :, group * 128 : (group + 1) * 128] = whole_ref[rows, :]


def first_kernel(
    count_ref, sums_ref, first_ref, gf_ref, gs_ref, vf_ref, vs_ref, afa_ref, asa_ref, mask_ref,
    f0_ref, f1_ref, s0_ref, s1_ref, total_ref, tile_ref,
):
    fast_count, slow_count = count_ref[0], count_ref[1]
    total = jnp.sum(sums_ref[...], axis=0)
    total_ref[...] = total
    cells = f0_ref.shape[0]
    fast_beta, fast_gamma, beta, gamma = split(total, (128, 128, 256, 256))
    ft, fq, st, sq = split(first_ref[...], (128, 128, 256, 256))
    mean, inverse = mean_inverse(fold_lanes(ft, ALPHA), fold_lanes(fq, ALPHA), fast_count)
    fast_lines = back_line(
        mean, inverse, tiled_affine(afa_ref, tile_ref)[0:1], fold_lanes(fast_beta, ALPHA), fold_lanes(fast_gamma, ALPHA), fast_count
    )
    slow_lines = back_line(*mean_inverse(st, sq, slow_count), asa_ref[0:1, :], beta, gamma, slow_count)
    for grad_ref, value_ref, outs, (one, two, three) in (
        (gf_ref, vf_ref, (f0_ref, f1_ref), fast_lines),
        (gs_ref, vs_ref, (s0_ref, s1_ref), slow_lines),
    ):
        for frame, out_ref in enumerate(outs):
            now = slice(frame * cells, (frame + 1) * cells)
            mask = wide_mask(mask_ref[now, :], grad_ref.shape[1])
            grad = mask * (grad_ref[now, :] * one - two - value_ref[now, :] * three)
            out_ref[...] = grad.astype(BF)


def joined_back_kernel(
    mask_ref, one_ref, two_ref, before_ref, after_ref, dh_ref, wa_ref, ws_ref, out_ref
):
    cells = one_ref.shape[0]
    cs = out_ref.shape[2]
    cm = wa_ref.shape[0] // 3
    for frame, pieces in enumerate(
        ((two_ref, one_ref, before_ref), (after_ref, two_ref, one_ref))
    ):
        mask = mask_ref[frame * cells : (frame + 1) * cells, :]
        taps = jnp.concatenate([piece[:, :cm] for piece in pieces], axis=1)
        for start in range(0, cs, 256):
            part = slice(start, start + 256)
            grad = mm(taps, wa_ref[:, part]) + mm_t(dh_ref[frame], ws_ref[part, :])
            out_ref[:, frame, part] = (grad * wide_mask(mask, 256)).astype(BF)


def lateral_back_kernel(
    mask_ref, one_ref, two_ref, before_ref, after_ref, fast_ref, dh_ref, wa_ref, ws_ref,
    lat_ref, edge_ref, a_ref, s_ref, sems,
):
    cells, cl = one_ref.shape[0], lat_ref.shape[2]
    cm = wa_ref.shape[0] // 3
    cs = ws_ref.shape[0] - cl
    copies = [
        pltpu.make_async_copy(wa_ref.at[:, pl.ds(cs, cl)], a_ref, sems.at[0]),
        pltpu.make_async_copy(ws_ref.at[pl.ds(cs, cl), :], s_ref, sems.at[1]),
    ]
    for copy in copies:
        copy.start()
    for copy in copies:
        copy.wait()
    for frame, pieces in enumerate(
        ((two_ref, one_ref, before_ref), (after_ref, two_ref, one_ref))
    ):
        mask = mask_ref[frame * cells : (frame + 1) * cells, :]
        taps = jnp.concatenate([piece[:, :cm] for piece in pieces], axis=1)
        grad = mm(taps, a_ref[...]) + mm_t(dh_ref[frame], s_ref[...])
        grad = (grad * wide_mask(mask, cl)).astype(BF)
        lat_ref[frame] = grad
        if frame == 0:
            edge_ref[:, :cl] = grad
            edge_ref[:, cl:] = fast_ref[...]


def lateral_back(arrays, outs):
    wa, ws = arrays[-2:]
    cl = outs[0][0][2]
    anywhere = pl.BlockSpec(memory_space=pl.ANY)
    return pl.pallas_call(
        lateral_back_kernel,
        out_shape=[jax.ShapeDtypeStruct(s, d) for s, d in outs],
        in_specs=[VMEM] * (len(arrays) - 2) + [anywhere] * 2,
        out_specs=[VMEM] * len(outs),
        scratch_shapes=[
            pltpu.VMEM((wa.shape[0], cl), BF),
            pltpu.VMEM((cl, ws.shape[1]), BF),
            pltpu.SemaphoreType.DMA((2,)),
        ],
        compiler_params=pltpu.CompilerParams(vmem_limit_bytes=LARGE),
        cost_estimate=FREE,
    )(*arrays)


def unpack_kernel(
    clip_ref, in_ref, mask_ref, out_ref, tail_ref, last_ref, head_ref, count_ref, rows_ref
):
    frames, cells = out_ref.shape[:2]
    step = frames * ALPHA
    pixels = H * W
    batch = cells // pixels
    total = sum(clip_ref[i, 0] for i in range(clip_ref.shape[0]))
    count_ref[1] = (total * pixels).astype(F32)
    count_ref[0] = (total * (pixels * ALPHA)).astype(F32)
    rows_ref[...] = in_ref[...].astype(F32)
    spot = lax.broadcasted_iota(jnp.int32, (cells, 128), 0)
    for frame in range(frames):
        place = lax.axis_index("mp") * frames + frame
        mask = jnp.zeros((cells, 128), F32)
        for b in range(batch):
            length = clip_ref[lax.axis_index("dp") * batch + b, 0]
            valid = (place < length).astype(F32)
            inside = (spot >= b * pixels) & (spot < (b + 1) * pixels)
            mask = jnp.where(inside, valid, mask)
        mask_ref[frame * cells : (frame + 1) * cells, :] = mask
        for j in range(ALPHA):
            values = rows_ref[pl.ds(frame * ALPHA + j, cells, step), :] * mask
            values = values.astype(BF)
            out_ref[frame, :, j * 128 : (j + 1) * 128] = values
            if frame == frames - 1 and j >= 2:
                (tail_ref, last_ref)[j - 2][...] = values
            if frame == 0 and j == 0:
                head_ref[...] = values


def copies():
    width = 128 // ALPHA
    lanes = jnp.bitwise_and(lax.broadcasted_iota(jnp.int32, (width, 128), 1), width - 1)
    rows = lax.broadcasted_iota(jnp.int32, (width, 128), 0)
    return jnp.where(lanes == rows, 1.0, 0.0).astype(BF)


def lane_mask(rows, j):
    group = lax.broadcasted_iota(jnp.int32, (rows, 128), 1) // (128 // ALPHA)
    return jnp.where(group == j, 1.0, 0.0)


def tiled_affine(ref, tile_ref):
    if ref.shape[1] == 128:
        return jnp.concatenate([ref[...]] * ALPHA, axis=1)
    tile_ref[...] = jnp.zeros_like(tile_ref)
    tile_ref[0:2, 0 : ref.shape[1]] = ref[...]
    return fold_lanes(tile_ref[0:2, :], ALPHA)


def build_a(w_ref, out_ref):
    tiles = mm(w_ref[...], copies())
    size = w_ref.shape[0] // 3
    masks = [lane_mask(size, j) for j in range(ALPHA)]
    for i in range(ALPHA + 2):
        total = sum(
            tiles[(i - j) * size : (i - j + 1) * size, :] * masks[j]
            for j in range(ALPHA)
            if 0 <= i - j < 3
        )
        out_ref[i * size : (i + 1) * size, :] = total.astype(BF)


def build_b(w_ref, out_ref, back):
    ci = w_ref.shape[1]
    for tap in range(9):
        block = w_ref[tap * ci : (tap + 1) * ci, :]
        tile = tn(block, copies()) if back else mm(block, copies())
        place = 8 - tap if back else tap
        for j in range(ALPHA):
            start = place * 128 + j * ci
            out_ref[start : start + ci, :] = (tile * lane_mask(ci, j)).astype(BF)


def build_c(w_ref, out_ref):
    ci, cf = w_ref.shape
    out_ref[...] = jnp.zeros_like(out_ref)
    for j in range(ALPHA):
        out_ref[j * ci : (j + 1) * ci, j * cf : (j + 1) * cf] = w_ref[...]


def build_back(w_ref, out_ref):
    ci = w_ref.shape[1]
    size = w_ref.shape[0] // 3
    one = jnp.where(
        lax.broadcasted_iota(jnp.int32, (ci, ci), 0) == lax.broadcasted_iota(jnp.int32, (ci, ci), 1),
        1.0,
        0.0,
    ).astype(BF)
    out_ref[...] = jnp.zeros_like(out_ref)
    for tap in range(3):
        block = mm_t(one, w_ref[tap * size : (tap + 1) * size, :]).astype(BF)
        for j in range(ALPHA):
            start = 128 + (j + 1 - tap) * ci
            out_ref[start : start + ci, j * size : (j + 1) * size] = block


def entry_kernel(
    mask_ref, fast_ref, before_ref, last_ref, after_ref, slow_ref, wa_ref, wl_ref,
    stack_ref, lateral_ref, first_ref, sums_ref, joined_ref, big_ref, rows_ref,
):
    cells = before_ref.shape[0]
    cs, cf = slow_ref.shape[2], 128
    build_a(wa_ref, big_ref)
    for column in range(0, cs, 128):
        values = slow_ref[:, :, column : column + 128].reshape(2 * cells, 128)
        rows_ref[column // 128] = values.astype(F32)
    tots, squares = [], []
    for frame in range(2):
        mask = mask_ref[frame * cells : (frame + 1) * cells, :]
        own = fast_ref[frame]
        past = (before_ref[...], last_ref[...])
        if frame:
            past = (fast_ref[0][:, 2 * cf : 3 * cf], fast_ref[0][:, 3 * cf :])
        following = fast_ref[1][:, :cf] if frame == 0 else after_ref[...]
        stack_ref[frame, :, 0:cf] = past[1]
        stack_ref[frame, :, cf : 5 * cf] = own
        stack_ref[frame, :, 5 * cf :] = following
        lateral_ref[frame, :, 0:cf] = past[0]
        lateral_ref[frame, :, cf : 2 * cf] = past[1]
        lateral_ref[frame, :, 2 * cf :] = own[:, : 3 * cf]
        value = mm(stack_ref[frame], big_ref[...])
        first_ref[frame * cells : (frame + 1) * cells, :] = value
        tots.append(total_row(value * mask))
        squares.append(total_row(value * mask * value))
        lateral = mm(lateral_ref[frame], wl_ref[...]).astype(BF)
        joined_ref[frame, :, cs:] = lateral * wide_mask(mask.astype(BF), 256)
        for column in range(0, cs, 128):
            values = rows_ref[column // 128, pl.ds(frame, cells, 2), :] * mask
            joined_ref[frame, :, column : column + 128] = values.astype(BF)
    sums_ref[:, :128] = tots[0] + tots[1]
    sums_ref[:, 128:] = squares[0] + squares[1]


def taps_kernel(joined_ref, wa_ref, base_ref, right_ref, left_ref, one_ref, two_ref):
    cells, cm = right_ref.shape
    one_ref[...] = mm_t(joined_ref[0], wa_ref[...])
    two_ref[...] = mm_t(joined_ref[1], wa_ref[...])
    base_ref[:cells, :] = one_ref[:, cm : 2 * cm] + two_ref[:, 2 * cm :]
    base_ref[cells:, :] = two_ref[:, cm : 2 * cm] + one_ref[:, :cm]
    right_ref[...] = two_ref[:, :cm].astype(BF)
    left_ref[...] = one_ref[:, 2 * cm :].astype(BF)


def placed_taps_kernel(
    joined_ref, own_ref, side_ref, core_ref, both_ref,
    wa_ref, base_ref, right_ref, left_ref, one_ref, two_ref, *, sync,
):
    place_pieces(place_a, (own_ref, side_ref, core_ref, both_ref), (wa_ref,))
    sync.send(0)
    taps_kernel(joined_ref, wa_ref, base_ref, right_ref, left_ref, one_ref, two_ref)


def first_sums_kernel(mask_ref, base_ref, left_ref, right_ref, fast_ref, first_ref, vec_ref):
    cells, cm = left_ref.shape
    tot = square = jnp.zeros((1, cm), F32)
    for frame, halo_ref in enumerate((left_ref, right_ref)):
        now = slice(frame * cells, (frame + 1) * cells)
        value = base_ref[now, :] + halo_ref[...].astype(F32)
        first_ref[now, :] = value
        masked = value * wide_mask(mask_ref[now, :], cm)
        tot = tot + total_row(masked)
        square = square + total_row(masked * value)
    send_all(vec_ref, [fast_ref[...], tot, square])


def sum_kernel(sums_ref, vec_ref):
    total = jnp.sum(sums_ref[...], axis=0)
    vec_ref[...] = jnp.broadcast_to(total[None], vec_ref.shape)


def fast_back_kernel(
    mask_ref, one_ref, two_ref, before_ref, after_ref, dl_ref, cot_ref, wl_ref, wa_ref,
    out_ref, rows_ref, big_ref,
):
    cells = one_ref.shape[0]
    cf = 128
    build_back(wa_ref, big_ref)
    for frame in range(2):
        now = slice(frame * cells, (frame + 1) * cells)
        mask = mask_ref[now, :]
        cl = dl_ref.shape[2]
        pieces = (before_ref[...], one_ref[...], two_ref[...])
        if frame:
            pieces = pieces[1:] + (after_ref[:, cl:],)
        taps = jnp.concatenate(pieces, axis=1)
        now_dl, next_dl = dl_ref[frame], after_ref[:, :cl] if frame else dl_ref[1]
        for j in range(ALPHA):
            part = slice(j * 128, (j + 1) * 128)
            grad = mm(taps, big_ref[:, part]) + cot_ref[now, part]
            if j < 3:
                grad = grad + mm_t(now_dl, wl_ref[(j + 2) * cf : (j + 3) * cf, :])
            if j >= 2:
                grad = grad + mm_t(next_dl, wl_ref[(j - 2) * cf : (j - 1) * cf, :])
            rows_ref[pl.ds(frame * ALPHA + j, cells, 2 * ALPHA), :] = grad * mask
    out_ref[...] = rows_ref[...].astype(BF)


def dot(left, right, left_dim, right_dim):
    return lax.dot_general(
        left, right, (((left_dim,), (right_dim,)), ((), ())), preferred_element_type=F32
    )


def rows_dot(left, right):
    return lax.dot_general(
        left, right, (((0, 1), (0, 1)), ((), ())), preferred_element_type=F32
    )


def folded(vector, groups):
    return jnp.sum(vector.reshape(groups, -1), axis=0)


def norm_terms(totals, squares, count, groups=1):
    average = totals / count
    inverse = lax.rsqrt(squares / count - average * average + NORM_EPSILON)
    return jnp.tile(average, groups), jnp.tile(inverse, groups)


ROWS_STEP = 112
TAPS = [(dh, dw) for dh in (-1, 0, 1) for dw in (-1, 0, 1)]


def row_chunks(rows, step):
    return [pl.ds(start, step) for start in range(0, rows, step)]


def loop_rows(rows, step, body, init):
    def turn(i, carry):
        return body(pl.ds(pl.multiple_of(i * step, step), step), carry)

    return lax.fori_loop(0, rows // step, turn, init)


def collapse(values):
    return jnp.sum(values.reshape(-1, 8, values.shape[-1]), axis=0)


def gate_of(values):
    return 0.5 * jnp.tanh(0.5 * values) + 0.5


def fold_lanes(vector, groups):
    width = vector.shape[-1] // groups
    total = vector
    for j in range(1, groups):
        total = total + pltpu.roll(vector, j * width, 1)
    return total


def mean_inverse(totals, squares, count):
    average = totals / count
    return average, lax.rsqrt(squares / count - average * average + NORM_EPSILON)


def line(average, inverse, affine):
    scale = affine[0:1] * inverse
    return scale, affine[1:2] - average * scale


def send_all(vec_ref, pieces):
    start = 0
    for piece in pieces:
        width = piece.shape[-1]
        spread = jnp.broadcast_to(piece[None], (vec_ref.shape[0], 1, width))
        vec_ref[:, :, start : start + width] = spread
        start += width


def received(sums_ref, widths):
    total = jnp.sum(sums_ref[...], axis=0)
    return split(total, widths)


def split(total, widths):
    pieces = []
    start = 0
    for width in widths:
        pieces.append(total[:, start : start + width])
        start += width
    return pieces


def total_row(vector):
    return jnp.sum(vector, axis=0, keepdims=True)


MARGIN = 16


def clear_margins(buffer):
    rows = buffer.shape[0]
    zeros = jnp.zeros((MARGIN, buffer.shape[1]), F32)
    buffer[0:MARGIN, :] = zeros
    buffer[rows - MARGIN : rows, :] = zeros


def write_patches(buffer, patches, edges):
    rows, channels = patches.shape[0], buffer.shape[1]
    for start in range(0, rows, ROWS_STEP):
        top, bottom, left, right = (edges[k, start : start + ROWS_STEP, :] for k in range(4))
        for tap, (dh, dw) in enumerate(TAPS):
            mask = None
            if dh:
                mask = top if dh < 0 else bottom
            if dw:
                side = left if dw < 0 else right
                mask = side if mask is None else mask * side
            offset = MARGIN + start + W * dh + dw
            for column in range(0, channels, 128):
                piece = buffer[offset : offset + ROWS_STEP, column : column + 128]
                if mask is not None:
                    piece = piece * mask
                place = tap * channels + column
                patches[start : start + ROWS_STEP, place : place + 128] = piece.astype(BF)


def mm(left, right):
    return jnp.dot(left, right, preferred_element_type=F32)


def mm_t(left, right):
    return lax.dot_general(left, right, (((1,), (1,)), ((), ())), preferred_element_type=F32)


def wide_mask(mask, width):
    return jnp.concatenate([mask] * (width // 128), axis=1) if width > 128 else mask


def conv_kernel(
    count_ref, sums_ref, vf_ref, vs_ref, af_ref, as_ref, mask_ref, edge_ref, wf_ref, ws_ref,
    hf_ref, hs_ref, of_ref, os_ref, total_ref, vec_ref, bf_ref, bs_ref, pf_ref, ps_ref, big_ref, tile_ref,
):
    fast_count, slow_count = count_ref[0], count_ref[1]
    total = jnp.sum(sums_ref[...], axis=0)
    total_ref[...] = total
    ft, fq, st, sq = split(total, (128, 128, 256, 256))
    lines = []
    build_b(wf_ref, big_ref, False)
    for tot, square, count, affine in ((ft, fq, fast_count, af_ref), (st, sq, slow_count, as_ref)):
        if tot.shape[-1] == 128:
            tot, square = fold_lanes(tot, ALPHA), fold_lanes(square, ALPHA)
            affine = tiled_affine(affine, tile_ref)
        else:
            affine = affine[...]
        lines.append(line(*mean_inverse(tot, square, count), affine))
    rows = vf_ref.shape[0]
    for value_ref, hidden_ref, buffer, (scale, shift) in (
        (vf_ref, hf_ref, bf_ref, lines[0]),
        (vs_ref, hs_ref, bs_ref, lines[1]),
    ):
        width = value_ref.shape[1]
        clear_margins(buffer)
        for start in range(0, rows, ROWS_STEP):
            z = value_ref[start : start + ROWS_STEP, :] * scale + shift
            hidden = z * gate_of(z) * wide_mask(mask_ref[start : start + ROWS_STEP, :], width)
            buffer[MARGIN + start : MARGIN + start + ROWS_STEP, :] = hidden
            hidden_ref[start : start + ROWS_STEP, :] = hidden.astype(BF)
    write_patches(bf_ref, pf_ref, edge_ref)
    write_patches(bs_ref, ps_ref, edge_ref)
    of_ref[...] = mm(pf_ref[...], big_ref[...])
    os_ref[...] = mm_t(ps_ref[...], ws_ref[...])
    pieces = []
    for out_ref in (of_ref, os_ref):
        width = out_ref.shape[1]

        def body(rows_now, carry):
            value = out_ref[rows_now, :]
            masked = value * wide_mask(mask_ref[rows_now, :], width)
            return carry[0] + collapse(masked), carry[1] + collapse(masked * value)

        zero = jnp.zeros((8, width), F32)
        pieces += [total_row(v) for v in loop_rows(rows, ROWS_STEP, body, (zero, zero))]
    send_all(vec_ref, pieces)


def expand_kernel(
    count_ref, sums_ref, short_ref, vf_ref, vs_ref, af_ref, as_ref, mask_ref, wf_ref, ws_ref,
    hf_ref, hs_ref, yf_ref, ys_ref, total_ref, vec_ref, of_ref, os_ref, big_ref, tile_ref,
):
    fast_count, slow_count = count_ref[0], count_ref[1]
    total = jnp.sum(sums_ref[...], axis=0)
    total_ref[...] = total
    ft, fq, st, sq = split(total, (128, 128, 256, 256))
    ft, fq = fold_lanes(ft, ALPHA), fold_lanes(fq, ALPHA)
    build_c(wf_ref, big_ref)
    lines = (
        line(*mean_inverse(ft, fq, fast_count), tiled_affine(af_ref, tile_ref)),
        line(*mean_inverse(st, sq, slow_count), as_ref[...]),
    )
    rows = vf_ref.shape[0]
    for value_ref, hidden_ref, (scale, shift) in ((vf_ref, hf_ref, lines[0]), (vs_ref, hs_ref, lines[1])):
        width = value_ref.shape[1]

        def body(rows_now, carry):
            z = value_ref[rows_now, :] * scale + shift
            hidden = z * gate_of(z) * wide_mask(mask_ref[rows_now, :], width)
            hidden_ref[rows_now, :] = hidden.astype(BF)
            return carry

        loop_rows(rows, ROWS_STEP, body, 0)
    of_ref[...] = mm(hf_ref[...], big_ref[...])
    os_ref[...] = mm(hs_ref[...], ws_ref[...])
    pieces = []
    for out_ref, low_ref in ((of_ref, yf_ref), (os_ref, ys_ref)):
        width = out_ref.shape[1]
        tots, squares = [], []
        for column in range(0, width, 512):

            def body(rows_now, carry):
                value = out_ref[rows_now, column : column + 512]
                low_ref[rows_now, column : column + 512] = value.astype(low_ref.dtype)
                value = value.astype(low_ref.dtype).astype(F32)
                masked = value * wide_mask(mask_ref[rows_now, :], 512)
                return carry[0] + collapse(masked), carry[1] + collapse(masked * value)

            zero = jnp.zeros((8, 512), F32)
            one, two = loop_rows(rows, 16, body, (zero, zero))
            tots.append(total_row(one))
            squares.append(total_row(two))
        if width == 512:
            pieces += [sum(v[:, j * 128 : (j + 1) * 128] for j in range(ALPHA)) for v in (tots[0], squares[0])]
        else:
            pieces += [jnp.concatenate(tots, 1), jnp.concatenate(squares, 1)]
    send_all(vec_ref, pieces + [short_ref[...]])


def short_kernel(mask_ref, joined_ref, ws_ref, out_ref, vec_ref):
    rows, wide = out_ref.shape
    for column in range(0, wide, 256):
        part = slice(column, column + 256)
        one = jnp.zeros((8, 256), F32)
        two = one
        for start in range(0, rows, 2 * ROWS_STEP):
            now = slice(start, min(start + 2 * ROWS_STEP, rows))
            value = mm(joined_ref[now, :], ws_ref[:, part])
            out_ref[now, part] = value.astype(BF)
            value = value.astype(BF).astype(F32)
            masked = value * wide_mask(mask_ref[now, :], 256)
            one = one + collapse(masked)
            two = two + collapse(masked * value)
        vec_ref[:, part] = total_row(one)
        vec_ref[:, wide + column : wide + column + 256] = total_row(two)


def placed_short_kernel(
    mask_ref, joined_ref, own_ref, side_ref, core_ref, both_ref, ws_ref, out_ref, vec_ref, *, sync
):
    place_pieces(place_short, (own_ref, side_ref, core_ref, both_ref), (ws_ref,))
    sync.send(0)
    short_kernel(mask_ref, joined_ref, ws_ref, out_ref, vec_ref)


def output_kernel(
    count_ref, sums_ref, vf_ref, vs_ref, vh_ref, fast_ref, cf_ref, cs_ref,
    af_ref, as_ref, ah_ref, mask_ref,
    yf_ref, ys_ref, gf_ref, gs_ref, total_ref, vec_ref, rows_ref, cots_ref, *, sync,
):
    fast_count, slow_count = count_ref[0], count_ref[1]
    total = jnp.sum(sums_ref[...], axis=0)
    total_ref[...] = total
    wide = vs_ref.shape[1]
    ft, fq, st, sq, ht, hq = split(total, (128, 128, wide, wide, wide, wide))
    rows = vf_ref.shape[0]
    mean, inverse = mean_inverse(ft, fq, fast_count)
    mean, inverse = (jnp.concatenate([v] * ALPHA, 1) for v in (mean, inverse))
    scale, shift = line(mean, inverse, tiled_affine(af_ref, None))

    frames, cells = fast_ref.shape[:2]
    step = frames * ALPHA
    cots_ref[...] = cf_ref[...].astype(F32)
    zero = jnp.zeros((8, 512), F32)
    beta = gamma = jnp.zeros((1, 128), F32)
    for frame in range(frames):
        now = slice(frame * cells, (frame + 1) * cells)
        for j in range(ALPHA):
            part = slice(j * 128, (j + 1) * 128)
            place = pl.ds(frame * ALPHA + j, cells, step)
            mask = mask_ref[now, :]
            value = vf_ref[now, part]
            z = value * scale[:, part] + shift[:, part] + fast_ref[frame, :, part].astype(F32)
            gate = gate_of(z)
            rows_ref[place, :] = mask * z * gate
            grad = cots_ref[place, :] * mask * gate * (1.0 + z * (1.0 - gate))
            gf_ref[now, part] = grad
            beta = beta + total_row(grad)
            gamma = gamma + total_row(grad * value)
    yf_ref[...] = rows_ref[...].astype(BF)
    sync.send(0, 2)
    sync.arrive(2, 3, 6)
    pieces = [beta, (gamma - mean[:, :128] * beta) * inverse[:, :128]]
    mean_c, inverse_c = mean_inverse(st, sq, slow_count)
    mean_h, inverse_h = mean_inverse(ht, hq, slow_count)
    scale_c, shift_c = line(mean_c, inverse_c, as_ref[...])
    scale_h, shift_h = line(mean_h, inverse_h, ah_ref[...])
    betas, gammas, others = [], [], []
    for column in range(0, wide, 512):
        part = slice(column, column + 512)
        sc, sh, shift_both = scale_c[:, part], scale_h[:, part], shift_c[:, part] + shift_h[:, part]

        def body(rows_now, carry):
            third, short = vs_ref[rows_now, part].astype(F32), vh_ref[rows_now, part].astype(F32)
            mask = wide_mask(mask_ref[rows_now, :], 512)
            z = third * sc + short * sh + shift_both
            gate = gate_of(z)
            ys_ref[rows_now, part] = (mask * z * gate).astype(BF)
            grad = cs_ref[rows_now, part].astype(F32) * mask * gate * (1.0 + z * (1.0 - gate))
            gs_ref[rows_now, part] = grad.astype(BF)
            grad = grad.astype(BF).astype(F32)
            return (
                carry[0] + collapse(grad),
                carry[1] + collapse(grad * third),
                carry[2] + collapse(grad * short),
            )

        beta, gamma, other = (total_row(v) for v in loop_rows(rows, 16, body, (zero, zero, zero)))
        betas.append(beta)
        gammas.append((gamma - mean_c[:, part] * beta) * inverse_c[:, part])
        others.append((other - mean_h[:, part] * beta) * inverse_h[:, part])
    pieces += [jnp.concatenate(v, 1) for v in (betas, gammas, others)]
    sync.send(1, 3)
    send_all(vec_ref, pieces)


def back_line(mean, inverse, scale, beta, gamma, count):
    first = inverse * scale
    third = first * gamma * inverse / count
    return first, first * beta / count - mean * third, third


def narrow_kernel(
    count_ref, sums_ref, third_ref, second_ref,
    gf_ref, gs_ref, vf_ref, vs_ref, vh_ref, uf_ref, us_ref,
    afc_ref, asc_ref, ash_ref, afb_ref, asb_ref, mask_ref, wf_ref, ws_ref,
    df_ref, ds_ref, dh_ref, of_ref, os_ref, total_ref, vec_ref, big_ref, tile_ref, *, sync,
):
    fast_count, slow_count = count_ref[0], count_ref[1]
    total = jnp.sum(sums_ref[...], axis=0)
    total_ref[...] = total
    wide = vs_ref.shape[1]
    rows = vf_ref.shape[0]
    fast_beta, fast_gamma, beta, gamma_c, gamma_h = split(total, (128, 128, wide, wide, wide))
    ft, fq, st, sq, ht, hq = split(third_ref[...], (128, 128, wide, wide, wide, wide))
    mean, inverse = mean_inverse(ft, fq, fast_count)
    tiled = [jnp.concatenate([v] * ALPHA, 1) for v in (mean, inverse, fast_beta, fast_gamma)]
    build_c(wf_ref, big_ref)
    f1, f2, f3 = back_line(tiled[0], tiled[1], tiled_affine(afc_ref, None)[0:1], tiled[2], tiled[3], fast_count)

    def fast_body(rows_now, carry):
        mask = wide_mask(mask_ref[rows_now, :], 512)
        grad = mask * (gf_ref[rows_now, :].astype(F32) * f1 - f2 - vf_ref[rows_now, :].astype(F32) * f3)
        df_ref[rows_now, :] = grad.astype(BF)
        return carry

    loop_rows(rows, 16, fast_body, 0)
    sync.send(0)
    sync.arrive(4, 6, 7)
    mean_c, inverse_c = mean_inverse(st, sq, slow_count)
    mean_h, inverse_h = mean_inverse(ht, hq, slow_count)
    lines_c = back_line(mean_c, inverse_c, asc_ref[0:1, :], beta, gamma_c, slow_count)
    lines_h = back_line(mean_h, inverse_h, ash_ref[0:1, :], beta, gamma_h, slow_count)
    for column in range(0, wide, 512):
        part = slice(column, column + 512)
        c1, c2, c3 = (v[:, part] for v in lines_c)
        h1, h2, h3 = (v[:, part] for v in lines_h)

        def body(rows_now, carry):
            mask = wide_mask(mask_ref[rows_now, :], 512)
            grad = gs_ref[rows_now, part].astype(F32)
            third, short = vs_ref[rows_now, part].astype(F32), vh_ref[rows_now, part].astype(F32)
            ds_ref[rows_now, part] = (mask * (grad * c1 - c2 - third * c3)).astype(BF)
            dh_ref[rows_now, part] = (mask * (grad * h1 - h2 - short * h3)).astype(BF)
            return carry

        loop_rows(rows, 16, body, 0)
    sync.send(1, 2)
    sync.arrive(8, 9, 17)
    of_ref[...] = mm_t(df_ref[...], big_ref[...])
    os_ref[...] = mm_t(ds_ref[...], ws_ref[...])
    ft, fq, st, sq = split(second_ref[...], (128, 128, 256, 256))
    pieces = slope_sums(
        (of_ref, uf_ref, tiled_affine(afb_ref, tile_ref), fold_lanes(ft, ALPHA), fold_lanes(fq, ALPHA), fast_count),
        (os_ref, us_ref, asb_ref, st, sq, slow_count),
        mask_ref,
    )
    send_all(vec_ref, pieces)


def slope_sums(fast_parts, slow_parts, mask_ref):
    pieces = []
    for out_ref, value_ref, affine, tot, square, count in (fast_parts, slow_parts):
        width = out_ref.shape[1]
        mean, inverse = mean_inverse(tot, square, count)
        scale, shift = line(mean, inverse, affine[...])

        def body(rows_now, carry):
            value = value_ref[rows_now, :]
            z = value * scale + shift
            gate = gate_of(z)
            mask = wide_mask(mask_ref[rows_now, :], width)
            grad = out_ref[rows_now, :] * mask * gate * (1.0 + z * (1.0 - gate))
            out_ref[rows_now, :] = grad
            return carry[0] + collapse(grad), carry[1] + collapse(grad * value)

        zero = jnp.zeros((8, width), F32)
        rows = out_ref.shape[0]
        beta, gamma = (total_row(v) for v in loop_rows(rows, ROWS_STEP // 2, body, (zero, zero)))
        pieces += [beta, (gamma - mean * beta) * inverse]
    return pieces


def conv_back_kernel(
    count_ref, sums_ref, second_ref, first_ref,
    gf_ref, gs_ref, uf_ref, us_ref, vf_ref, vs_ref,
    afb_ref, asb_ref, afa_ref, asa_ref, mask_ref, edge_ref, wf_ref, ws_ref,
    df_ref, ds_ref, of_ref, os_ref, total_ref, vec_ref,
    bf_ref, bs_ref, pf_ref, ps_ref, big_ref, tile_ref,
):
    fast_count, slow_count = count_ref[0], count_ref[1]
    total = jnp.sum(sums_ref[...], axis=0)
    total_ref[...] = total
    rows = gf_ref.shape[0]
    build_b(wf_ref, big_ref, True)
    fast_beta, fast_gamma, beta, gamma = split(total, (128, 128, 256, 256))
    ft, fq, st, sq = split(second_ref[...], (128, 128, 256, 256))
    mean, inverse = mean_inverse(fold_lanes(ft, ALPHA), fold_lanes(fq, ALPHA), fast_count)
    fast_lines = back_line(
        mean, inverse, tiled_affine(afb_ref, tile_ref)[0:1], fold_lanes(fast_beta, ALPHA), fold_lanes(fast_gamma, ALPHA), fast_count
    )
    slow_lines = back_line(*mean_inverse(st, sq, slow_count), asb_ref[0:1, :], beta, gamma, slow_count)
    for grad_ref, value_ref, out_ref, buffer, lines in (
        (gf_ref, uf_ref, df_ref, bf_ref, fast_lines),
        (gs_ref, us_ref, ds_ref, bs_ref, slow_lines),
    ):
        width = grad_ref.shape[1]
        one, two, three = lines
        clear_margins(buffer)
        for start in range(0, rows, ROWS_STEP):
            now = slice(start, start + ROWS_STEP)
            grad = grad_ref[now, :] * one - two - value_ref[now, :] * three
            grad = grad * wide_mask(mask_ref[now, :], width)
            out_ref[now, :] = grad.astype(BF)
            buffer[MARGIN + start : MARGIN + start + ROWS_STEP, :] = grad
    write_patches(bf_ref, pf_ref, edge_ref)
    write_patches(bs_ref, ps_ref, edge_ref)
    of_ref[...] = mm(pf_ref[...], big_ref[...])
    os_ref[...] = mm(ps_ref[...], ws_ref[...])
    ft, fq, st, sq = split(first_ref[...], (128, 128, 256, 256))
    pieces = slope_sums(
        (of_ref, vf_ref, tiled_affine(afa_ref, tile_ref), fold_lanes(ft, ALPHA), fold_lanes(fq, ALPHA), fast_count),
        (os_ref, vs_ref, asa_ref, st, sq, slow_count),
        mask_ref,
    )
    send_all(vec_ref, pieces)


def exchange(vec):
    return lax.all_to_all(vec, ("dp", "mp"), 0, 0, tiled=True)


def fast_results_kernel(in_ref, a_ref, b_ref, c_ref, l_ref, rows_ref, taps_ref):
    if len(in_ref.shape) == 3:
        groups = FAST_ROWS // 512
        for device in range(in_ref.shape[0]):
            x, core, block = device // 16, device // 8 % 2, device % 8
            for k in range(groups):
                start = core * (FAST_ROWS // 2) + ((block * 2 + x) * groups + k) * 16
                rows_ref[start : start + 16, :] = in_ref[device, :, k * 128 : (k + 1) * 128]
        in_ref = rows_ref
    taps, cf, ci = a_ref.shape
    start = 0
    for out_ref, rest in ((a_ref, 0), (b_ref, 8)):
        count, rows = out_ref.shape[:2]
        size = count * rows // ALPHA
        values = in_ref[start : start + size + rest, :].astype(F32)[:size, :]
        for k, piece in enumerate(unpacked(values, ALPHA)):
            taps_ref[k * size : (k + 1) * size, :] = piece
        for tap in range(count):
            out_ref[tap] = taps_ref[tap * rows : (tap + 1) * rows, :][:, :ci]
        start += size + rest
    c_ref[...] = in_ref[start : start + ci, :].astype(F32)
    start += ci
    for side in range(2):
        for tap in range(5):
            rows = slice(start + (side * 5 + tap) * cf, start + (side * 5 + tap + 1) * cf)
            l_ref[tap, :, side * 128 : (side + 1) * 128] = in_ref[rows, :].astype(F32)


def norms_kernel(c_ref, b_ref, a_ref, fa_ref, fb_ref, fc_ref, sa_ref, sb_ref, sc_ref, sh_ref):
    wide = sc_ref.shape[1]
    beta, gamma, slow, gamma_c, gamma_h = split(c_ref[...], (128, 128, wide, wide, wide))
    for out_ref, scale, shift in (
        (fc_ref, gamma, beta), (sc_ref, gamma_c, slow), (sh_ref, gamma_h, slow)
    ):
        out_ref[0:1, :] = scale
        out_ref[1:2, :] = shift
    for in_ref, fast_ref, slow_ref in ((b_ref, fb_ref, sb_ref), (a_ref, fa_ref, sa_ref)):
        width, cm = fast_ref.shape[1], slow_ref.shape[1]
        beta, gamma, slow, slow_gamma = split(in_ref[...], (128, 128, cm, cm))
        fast_ref[0:1, :] = fold_lanes(gamma, ALPHA)[:, :width]
        fast_ref[1:2, :] = fold_lanes(beta, ALPHA)[:, :width]
        slow_ref[0:1, :] = slow_gamma
        slow_ref[1:2, :] = slow


def per_device(
    fast_in,
    slow_in,
    clip_len,
    w_fast_a,
    w_fast_b,
    w_fast_c,
    w_lateral,
    w_slow_a,
    w_slow_b,
    w_slow_c,
    w_short,
    norm_fast_a,
    norm_fast_b,
    norm_fast_c,
    norm_slow_a,
    norm_slow_b,
    norm_slow_c,
    norm_short,
    cot_fast,
    cot_slow,
):
    batch, fast_frames, pixels, cf = fast_in.shape
    frames, cs = slow_in.shape[1], slow_in.shape[3]
    cells = batch * pixels
    ci = w_fast_a.shape[2]
    cl = w_lateral.shape[2]
    co = norm_slow_c.shape[1]
    cm = norm_slow_a.shape[1]
    cu = cs + cl
    mp = lax.axis_size("mp")
    me = lax.axis_index("mp")

    part, wide = w_slow_a.shape[2], w_short.shape[1]
    rows = frames * cells
    lane, fw = ALPHA * ci, ALPHA * cf
    small = 2 * lane + 2 * cm
    dp = lax.axis_size("dp")
    devices = dp * mp
    near_mesh = small_mesh()
    spot = np.arange(rows) % pixels
    edges = np.stack([spot >= W, spot < pixels - W, spot % W > 0, spot % W < W - 1])
    edges = jnp.asarray(np.repeat(edges.astype(np.float32)[:, :, None], 128, axis=2))
    buffers = [((rows + 2 * MARGIN, lane), F32), ((rows + 2 * MARGIN, cm), F32)]
    patches = [((rows, 9 * lane), BF), ((rows, 9 * cm), BF)]
    tile = ((8, 128), F32)

    def flat(values):
        return values.reshape(-1, values.shape[-1])

    def framed(values):
        return values.reshape(frames, cells, values.shape[-1])

    def by_pixel(values):
        return values.transpose(0, 2, 1, 3).reshape(cells, -1, values.shape[-1])

    def by_frame(values):
        return values.reshape(batch, pixels, -1, values.shape[-1]).transpose(0, 2, 1, 3)

    shards = jnp.swapaxes(w_slow_a, 1, 2), jnp.swapaxes(w_slow_b, 1, 2), w_slow_c, w_short
    if near_mesh:
        mine_a, mine_bc, mine_short = own_halves(*shards)
        line_a = line_pieces(mine_a)
        fast_in = held(fast_in, mine_a)
    mask, fast, tail, last, head, counts = local_call(
        unpack_kernel,
        [clip_len],
        [flat(by_pixel(fast_in))],
        [
            ((rows, 128), F32), ((frames, cells, fw), BF), ((cells, cf), BF), ((cells, cf), BF),
            ((cells, cf), BF), ((2,), F32),
        ],
        [((rows * ALPHA, cf), F32)],
        out_specs=[VMEM] * 5 + [SMEM],
    )
    if near_mesh:
        tail, last, head = held((tail, last, head), line_a[1])
    before = [shift_permute(values, "mp", 1) for values in (tail, last)]
    following = shift_permute(head, "mp", -1)
    if near_mesh:
        near_a = stacked(held(line_a, (before, following)))
    fast_stack, lateral_stack, fast_first, fast_sums, joined = local_call(
        entry_kernel,
        [],
        [
            mask, fast, *before, following, by_pixel(slow_in), w_fast_a.reshape(-1, ci),
            w_lateral.reshape(-1, cl),
        ],
        [
            ((frames, cells, 6 * cf), BF), ((frames, cells, 5 * cf), BF), ((rows, lane), F32),
            ((1, 2 * lane), F32), ((frames, cells, cu), BF),
        ],
        [((6 * cf, lane), BF), ((cs // 128, rows, 128), F32)],
    )

    if near_mesh:
        near_bc = stacked(held(line_pieces(held(mine_bc, near_a)), joined))
        line_short = line_pieces(held(mine_short, near_a))
        side_a = held(xor_permute(near_a, "mp", 1), (joined, near_bc))
        pieces_a = near_a, side_a, swap_cores(near_a), swap_cores(side_a)
        arrays = [joined, *pieces_a]
        placed = [((3 * cm, cu), BF)]
    else:
        wa, wb, wb_back, wc, ws = gather_whole(*shards)
        arrays = [joined, wa]
        placed = []
    *placed, base, to_right, to_left = local_call(
        placed_taps_kernel if near_mesh else taps_kernel,
        [],
        arrays,
        placed + [((rows, cm), F32), ((cells, cm), BF), ((cells, cm), BF)],
        [((cells, 3 * cm), F32)] * 2,
        early=(0,) if near_mesh else (),
    )
    if near_mesh:
        (wa,) = placed
    left = shift_permute(to_right, "mp", 1)
    right = shift_permute(to_left, "mp", -1)
    if near_mesh:
        pieces_bc = both_sides(near_bc)
        base = held(base, pieces_bc)
        near_short = stacked(held(line_short, (left, right)))
    slow_first, vec = local_call(
        first_sums_kernel,
        [],
        [mask, base, left, right, fast_sums],
        [((rows, cm), F32), ((devices, 1, small), F32)],
    )
    if near_mesh:
        wb, wb_back, wc = place_call(
            place_bc, pieces_bc, [(cm, 9 * cm), (9 * cm, cm), (cm, 8 * wide)]
        )
        side_short = xor_permute(near_short, "mp", 1)
        sums = held(exchange(vec), (wb, side_short))
    else:
        sums = exchange(vec)

    wfb = w_fast_b.reshape(-1, ci)
    hidden_a, hidden_c, fast_second, slow_second, total_1, vec = local_call(
        conv_kernel,
        [counts],
        [sums, fast_first, slow_first, norm_fast_a, norm_slow_a, mask, edges, wfb, wb],
        [
            ((rows, lane), BF), ((rows, cm), BF), ((rows, lane), F32), ((rows, cm), F32),
            ((1, small), F32), ((devices, 1, small), F32),
        ],
        buffers + patches + [((9 * lane, lane), BF), tile],
    )

    if near_mesh:
        side_short = held(side_short, vec)
        pieces = near_short, side_short, swap_cores(near_short), swap_cores(side_short)
        ws, shortcut, short_vec = local_call(
            placed_short_kernel,
            [],
            [mask, flat(joined), *pieces],
            [((cu, co), BF), ((rows, co), BF), ((1, 2 * co), F32)],
            early=(0,),
        )
    else:
        shortcut, short_vec = local_call(
            short_kernel, [], [mask, flat(joined), ws], [((rows, co), BF), ((1, 2 * co), F32)]
        )
    sums = held(exchange(vec), short_vec)
    hidden_b, hidden_d, fast_third, slow_third, total_2, vec = local_call(
        expand_kernel,
        [counts],
        [sums, short_vec, fast_second, slow_second, norm_fast_b, norm_slow_b, mask, w_fast_c, wc],
        [
            ((rows, lane), BF), ((rows, cm), BF), ((rows, fw), F32), ((rows, co), BF),
            ((1, small), F32), ((dp, 1, 2 * cf + 4 * co), F32),
        ],
        [((rows, fw), F32), ((rows, co), F32), ((lane, fw), BF), tile],
    )
    slow_cots = held(cot_slow, vec).transpose(1, 0, 2, 3).reshape(frames, cells, co)
    slow_cots = flat(slow_cots)
    sums = lax.all_to_all(vec, "dp", 0, 0, tiled=True)
    (vec,) = quick_call(sum_kernel, [sums], [((mp, 1, vec.shape[2]), F32)])
    sums = lax.all_to_all(vec, "mp", 0, 0, tiled=True)

    fast_out, slow_out, fast_cot, slow_cot, total_3, vec = local_call(
        output_kernel,
        [counts],
        [
            sums, fast_third, slow_third, shortcut, fast, flat(by_pixel(cot_fast)),
            slow_cots, norm_fast_c, norm_slow_c, norm_short, mask,
        ],
        [
            ((rows * ALPHA, cf), BF), ((rows, co), BF), ((rows, fw), F32), ((rows, co), BF),
            ((1, 2 * cf + 4 * co), F32), ((devices, 1, 2 * cf + 3 * co), F32),
        ],
        [((rows * ALPHA, cf), F32)] * 2,
        late=(2, 3, 6),
        early=(0, 1, 2, 3),
    )
    slow_out = framed(slow_out).reshape(frames, batch, pixels, co).transpose(1, 0, 2, 3)
    sums = held(exchange(vec), slow_out)

    d_fast_third, d_slow_third, d_short, grad_fb, grad_sb, total_4, vec = local_call(
        narrow_kernel,
        [counts],
        [
            sums, total_3, total_2, fast_cot, slow_cot, fast_third, slow_third, shortcut,
            fast_second, slow_second, norm_fast_c, norm_slow_c, norm_short, norm_fast_b, norm_slow_b,
            mask, w_fast_c, wc,
        ],
        [
            ((rows, fw), BF), ((rows, co), BF), ((rows, co), BF), ((rows, lane), F32),
            ((rows, cm), F32), ((1, 2 * cf + 3 * co), F32), ((devices, 1, small), F32),
        ],
        [((lane, fw), BF), tile],
        late=(4, 6, 7, 8, 9, 17),
        early=(0, 1, 2),
    )

    def weight_grad(kernel, arrays, size, length, total, scratch=()):
        halves = ((mp, size, length), BF)
        return local_call(kernel, [], arrays, [halves, halves], [((total, length), BF), *scratch])

    if near_mesh:
        raw_cs = weight_grad(
            grad_cs_kernel, [d_short, d_slow_third, flat(joined), hidden_d], wide // 2, cu + cm, co
        )
        sums, raw_cs = lax.optimization_barrier((exchange(vec), raw_cs))
        sent_cs = swap_cores(raw_cs[0])
    else:
        raw_cs = jnp.concatenate(
            [rows_dot(framed(d_short), joined), rows_dot(framed(d_slow_third), framed(hidden_d))], -1
        )
        sum_cs = reduce_whole(raw_cs.reshape(mp, 2, wide // 2, cu + cm)).reshape(wide, cu + cm)
        sums = exchange(vec)

    d_fast_second, d_slow_second, grad_fa, grad_sa, total_5, vec = local_call(
        conv_back_kernel,
        [counts],
        [
            sums, total_2, total_1, grad_fb, grad_sb, fast_second, slow_second, fast_first,
            slow_first, norm_fast_b, norm_slow_b, norm_fast_a, norm_slow_a, mask, edges, wfb, wb_back,
        ],
        [
            ((rows, lane), BF), ((rows, cm), BF), ((rows, lane), F32), ((rows, cm), F32),
            ((1, small), F32), ((devices, 1, small), F32),
        ],
        buffers + patches + [((9 * lane, lane), BF), tile],
    )
    grad_b_scratch = [buffers[1], patches[1]]
    if near_mesh:
        raw_b = weight_grad(
            grad_b_kernel, [d_slow_second, hidden_c, edges], part // 2, 9 * cm, cm, grad_b_scratch
        )
        sums, raw_b = lax.optimization_barrier((exchange(vec), raw_b))
        sent_b = swap_cores(raw_b[0])
    else:
        (raw_b,) = local_call(
            grad_b_whole_kernel,
            [],
            [d_slow_second, hidden_c, edges],
            [((cm, 9 * cm), F32)],
            grad_b_scratch,
        )
        sum_b = reduce_whole(raw_b.reshape(mp, 2, part // 2, 9 * cm)).reshape(part, 9, cm)
        sums = exchange(vec)
    d_fast_0, d_fast_1, d_slow_0, d_slow_1, total_6 = local_call(
        first_kernel,
        [counts],
        [sums, total_1, grad_fa, grad_sa, fast_first, slow_first, norm_fast_a, norm_slow_a, mask],
        [((cells, lane), BF)] * 2 + [((cells, cm), BF)] * 2 + [((1, small), F32)],
        [tile],
    )
    slow_parts = [
        d_slow_0, d_slow_1, shift_permute(d_slow_1, "mp", 1), shift_permute(d_slow_0, "mp", -1)
    ]
    (fast_inner,) = local_call(
        fast_inner_kernel,
        [],
        [held(hidden_a, d_slow_0), d_fast_second, hidden_b, d_fast_third, edges],
        [((9 * ci // ALPHA + 8 + ci, 128), BF)],
        [buffers[0], patches[0]],
    )
    if near_mesh:
        far_1, near_1 = merge((raw_cs[1], held(raw_b[1], d_slow_0)), (sent_cs, sent_b))
        raw_a = weight_grad(
            grad_a_kernel, held(slow_parts, (far_1, fast_inner)) + [joined], 3 * part // 2, cu, 3 * cm
        )
        sent_a = swap_cores(raw_a[0])
        slow_parts = held(slow_parts, raw_a)
    else:
        three = jnp.stack(
            [
                jnp.concatenate([d_slow_1, slow_parts[3]]),
                jnp.concatenate([d_slow_0, d_slow_1]),
                jnp.concatenate([slow_parts[2][:, :cm], d_slow_0]),
            ]
        )
        raw_a = jnp.einsum("kro,rc->koc", three, flat(joined), preferred_element_type=F32)
        raw_a = raw_a.reshape(3, mp, 2, part // 2, cu).transpose(1, 2, 0, 3, 4)
        sum_a = reduce_whole(raw_a.reshape(mp, 2, 3 * part // 2, cu))
        sum_a = sum_a.reshape(2, 3, part // 2, cu).transpose(1, 0, 2, 3).reshape(3, part, cu)
    d_lateral, lateral_edge = lateral_back(
        [mask, *slow_parts, d_fast_0, framed(d_short), wa, ws],
        [((frames, cells, cl), BF), ((cells, cl + lane), BF)],
    )
    lateral_after = shift_permute(lateral_edge, "mp", -1)
    fast_before = shift_permute(held(d_fast_1, d_lateral), "mp", 1)
    fast_outer = [fast_stack, d_fast_0, d_fast_1, lateral_stack, d_lateral, fast_inner]
    if near_mesh:
        half_fast = ((8, 16, FAST_ROWS // 2), BF)
        fast_send, fast_keep = local_call(
            fast_outer_kernel, [], fast_outer, [half_fast] * 2, [((FAST_ROWS, 128), BF)]
        )
        turned_1 = turn(far_1, near_1)
        keeps = raw_a[1], held(fast_keep, turned_1)
        far_2, near_2 = merge(keeps, (sent_a, swap_cores(fast_send)))
        slow_parts = held(slow_parts, far_2)
    else:
        (raw_fast,) = local_call(outer_rows, [], fast_outer, [((FAST_ROWS, 128), F32)])
        raw_fast = lax.psum(raw_fast, ("dp", "mp"))
    (grad_slow_in,) = local_call(
        joined_back_kernel,
        [],
        [mask, *slow_parts, framed(d_short), wa, ws],
        [((cells, frames, cs), BF)],
    )
    norms = local_call(
        norms_kernel,
        [],
        [total_4, total_5, total_6],
        [((2, width), F32) for width in (ci, ci, cf, cm, cm, co, co)],
        limit=SMALL,
    )
    if near_mesh:
        pieces_1 = cut_lines(turned_1[0], held(turned_1[1], grad_slow_in))
        sent_1 = over_z(pieces_1)
        pieces_2 = cut_lines(*turn(far_2, held(near_2, pieces_1)))
        sent_2 = over_z(pieces_2)
        (total_1,) = along_line(held(pieces_1[0], pieces_2), sent_1, pieces_1[0].shape[1])
        sum_c, sum_s, sum_b = cross_clips(
            clips_kernel,
            total_1,
            [(cm, wide), (cu, wide), (9, part, cm)],
            [((wide, cu + cm), F32)],
            norms,
        )
        mine = held(pieces_2[0], (lateral_after, fast_before, sum_c))
        total, raw_fast = along_line(mine, sent_2, mine.shape[1] - FAST_ROWS // 4)
        raw_fast = lax.all_to_all(raw_fast, ("dp", "mp"), 0, 0, tiled=True)
        d_lateral = held(d_lateral, total)
    (grad_fast_in,) = local_call(
        fast_back_kernel,
        [],
        [
            mask, d_fast_0, d_fast_1, fast_before, lateral_after, d_lateral, fast_cot,
            w_lateral.reshape(-1, cl), w_fast_a.reshape(-1, ci),
        ],
        [((rows * ALPHA, cf), BF)],
        [((rows * ALPHA, cf), F32), ((3 * lane, fw), BF)],
    )
    if near_mesh:
        (sum_a,) = cross_clips(clips_a_kernel, total, [(3, part, cu)], [], grad_fast_in)
    else:
        sum_c, sum_s = sum_cs[:, cu:].T, sum_cs[:, :cu].T
        sum_b = sum_b.transpose(1, 0, 2)
    if near_mesh:
        raw_fast = held(raw_fast, sum_a)
    fast_a, fast_b, fast_c, grad_lateral = local_call(
        fast_results_kernel,
        [],
        [raw_fast],
        [((3, cf, ci), F32), ((9, ci, ci), F32), ((ci, cf), F32), ((5, cf, cl), F32)],
        [((FAST_ROWS, 128), BF), ((3 * cf, 128), F32)],
        limit=SMALL,
    )
    return (
        by_frame(fast_out.reshape(cells, fast_frames, cf)),
        slow_out,
        by_frame(grad_fast_in.reshape(cells, fast_frames, cf)),
        by_frame(grad_slow_in),
        fast_a,
        fast_b,
        fast_c,
        grad_lateral,
        jnp.swapaxes(sum_a, 1, 2),
        jnp.swapaxes(sum_b, 1, 2),
        sum_c,
        sum_s,
        *norms,
    )


def solution(mesh):
    frames = P("dp", "mp", None, None)
    last = P(None, None, "mp")
    wide = P(None, "mp")
    return jax.shard_map(
        per_device,
        mesh=mesh,
        in_specs=(frames, frames, P(), P(), P(), P(), P(), last, last, wide, wide)
        + (P(),) * 7
        + (frames, frames),
        out_specs=(frames,) * 4 + (P(),) * 4 + (last, last, wide, wide) + (P(),) * 7,
        check_vma=False,
    )
```

```python
import functools

import jax
import jax.numpy as jnp
import numpy as np
from jax import lax
from jax.experimental import pallas as pl
from jax.experimental.pallas import tpu as pltpu
from jax.sharding import PartitionSpec as P

H = 14
W = 14
ALPHA = 4
NORM_EPSILON = 1e-05
BF = jnp.bfloat16
F32 = jnp.float32


def xor_permute(values, axis, bits):
    count = lax.axis_size(axis)
    return lax.ppermute(values, axis, [(i, i ^ bits) for i in range(count)])


def cross_permute(values, turn):
    members = lax.axis_size("mp")
    pairs = []
    for clip in range(lax.axis_size("dp")):
        for place in range(members):
            over_x = (clip % 2 == 0) == (turn == 0)
            other = (clip ^ 2, place) if over_x else (clip, place ^ 1)
            pairs.append((clip * members + place, other[0] * members + other[1]))
    return lax.ppermute(values, ("dp", "mp"), pairs)


def shift_permute(values, axis, step):
    count = lax.axis_size(axis)
    return lax.ppermute(
        values, axis, [(i, i + step) for i in range(count) if 0 <= i + step < count]
    )


def small_mesh():
    return lax.axis_size("dp") == 4 and lax.axis_size("mp") == 8


def pick(values, index, axis):
    return lax.dynamic_index_in_dim(values, index, axis, keepdims=False)


FREE = pl.CostEstimate(flops=0, bytes_accessed=1, transcendentals=0)
VMEM = pl.BlockSpec(memory_space=pltpu.VMEM)
SMEM = pl.BlockSpec(memory_space=pltpu.SMEM)
LARGE = 56 * 2**20
SMALL = 16 * 2**20


class Sync:
    def __init__(self, copies_in, copies_out):
        self.copies_in, self.copies_out = copies_in, copies_out

    def arrive(self, *places):
        for place in places:
            self.copies_in[place].wait()

    def send(self, *places):
        for place in places:
            self.copies_out[place].start()


def local_call(
    kernel, scalars, arrays, outs, scratch=(), limit=LARGE, out_specs=None, late=(), early=()
):
    count, total = len(scalars), len(arrays)
    anywhere = pl.BlockSpec(memory_space=pl.ANY)
    in_specs = [SMEM] * count + [anywhere if k in late else VMEM for k in range(total)]
    out_specs = out_specs or [anywhere if k in early else VMEM for k in range(len(outs))]
    own = [pltpu.VMEM(s, d) for s, d in scratch]
    buffers = [pltpu.VMEM(arrays[k].shape, arrays[k].dtype) for k in late]
    buffers += [pltpu.VMEM(*outs[k]) for k in early]

    def body(*refs):
        refs = list(refs)
        first_out = count + total
        sems = refs.pop()
        spare = refs[len(refs) - len(buffers) :]
        refs = refs[: len(refs) - len(buffers)]
        copies_in, copies_out = {}, {}
        for i, k in enumerate(late):
            copies_in[k] = pltpu.make_async_copy(refs[count + k], spare[i], sems.at[i])
            copies_in[k].start()
            refs[count + k] = spare[i]
        for i, k in enumerate(early, len(late)):
            copies_out[k] = pltpu.make_async_copy(spare[i], refs[first_out + k], sems.at[i])
            refs[first_out + k] = spare[i]
        kernel(*refs, sync=Sync(copies_in, copies_out))
        for copy in copies_out.values():
            copy.wait()

    moved = len(late) + len(early)
    return pl.pallas_call(
        body if moved else kernel,
        out_shape=[jax.ShapeDtypeStruct(s, d) for s, d in outs],
        in_specs=in_specs,
        out_specs=out_specs,
        scratch_shapes=own + buffers + ([pltpu.SemaphoreType.DMA((moved,))] if moved else []),
        compiler_params=pltpu.CompilerParams(vmem_limit_bytes=limit),
        cost_estimate=FREE,
    )(*scalars, *arrays)


def quick_call(kernel, arrays, outs):
    return local_call(kernel, [], arrays, outs, limit=SMALL)


def this_core():
    return lax.rem(lax.axis_index("dp"), 2)


def place_pieces(kernel, pieces, outs):
    me, core = lax.axis_index("mp"), this_core()
    side = lax.rem(me, 2)
    for k in range(4):
        owner_side = side if k % 2 == 0 else 1 - side
        half = core if k < 2 else 1 - core
        for far in range(4):
            line = jnp.bitwise_xor(me - side, 2 * far)
            kernel(line + owner_side, half, pieces[k].at[far], *outs)


def place_call(kernel, pieces, outs):
    def body(*refs):
        place_pieces(kernel, refs[:4], refs[4:])

    return local_call(body, [], pieces, [(shape, BF) for shape in outs], limit=32 * 2**20)


def stack_kernel(*refs):
    for k, ref in enumerate(refs[:-1]):
        refs[-1][k] = ref[...]


def line_pieces(mine):
    return [mine] + [xor_permute(mine, "mp", 2 * step) for step in (1, 2, 3)]


def stacked(pieces):
    return quick_call(stack_kernel, pieces, [((4,) + pieces[0].shape, BF)])[0]


def both_sides(near):
    side = xor_permute(near, "mp", 1)
    return near, side, xor_permute(near, "dp", 1), xor_permute(side, "dp", 1)


def place_a(block, half, piece, out):
    part = piece.shape[0] // 3
    width = out.shape[0] // 3
    for tap in range(3):
        start = pl.multiple_of(tap * width + block * (2 * part) + half * part, part)
        out[pl.ds(start, part), :] = piece[tap * part : (tap + 1) * part, :]


def place_bc(block, half, piece, out_f, out_b, out_c):
    width = out_f.shape[0]
    part = width // 16
    for tap in range(9):
        values = piece[tap * part : (tap + 1) * part, :]
        start = pl.multiple_of(block * (2 * part) + half * part, part)
        out_f[pl.ds(start, part), tap * width : (tap + 1) * width] = values
        start = pl.multiple_of((8 - tap) * width + block * (2 * part) + half * part, part)
        out_b[pl.ds(start, part), :] = values
    rest = piece.shape[0] - 9 * part
    columns = pl.ds(pl.multiple_of(block * 128, 128), 128)
    for k in range(2):
        start = pl.multiple_of(half * (2 * rest) + k * rest, rest)
        out_c[pl.ds(start, rest), columns] = piece[9 * part :, k * 128 : (k + 1) * 128]


def place_short(block, half, piece, out):
    part = piece.shape[0]
    columns = pl.ds(pl.multiple_of(block * 128, 128), 128)
    out[pl.ds(pl.multiple_of(half * part, part), part), columns] = piece[...]


def held(values, other):
    return lax.optimization_barrier((values, other))[0]


def shards_kernel(a_ref, b_ref, c_ref, s_ref, a_out, bc_out, s_out):
    core = this_core()
    half = a_ref.shape[1] // 2
    mine = pl.ds(pl.multiple_of(core * half, half), half)
    for tap in range(3):
        a_out[tap * half : (tap + 1) * half, :] = a_ref[tap, mine, :]
    for tap in range(9):
        bc_out[tap * half : (tap + 1) * half, :] = b_ref[tap, mine, :]
    rest = c_ref.shape[0] // 4
    for k in range(2):
        rows = pl.ds(pl.multiple_of(core * (2 * rest) + k * rest, rest), rest)
        bc_out[9 * half :, k * 128 : (k + 1) * 128] = c_ref[rows, :]
    size = s_out.shape[0]
    s_out[...] = s_ref[pl.ds(pl.multiple_of(core * size, size), size), :]


def own_halves(a_t, b_t, w_slow_c, w_short):
    half, cu = a_t.shape[1] // 2, a_t.shape[2]
    cm = b_t.shape[2]
    outs = [((3 * half, cu), BF), ((9 * half + cm // 4, cm), BF), ((cu // 2, 128), BF)]
    return quick_call(shards_kernel, [a_t, b_t, w_slow_c, w_short], outs)


def gather_whole(a_t, b_t, w_slow_c, w_short):
    wa = lax.all_gather(a_t, "mp", axis=1, tiled=True)
    wb = lax.all_gather(b_t, "mp", axis=1, tiled=True)
    wc = lax.all_gather(w_slow_c, "mp", axis=1, tiled=True)
    ws = lax.all_gather(w_short, "mp", axis=1, tiled=True)
    cm = wb.shape[1]
    wb_back = wb[::-1].reshape(9 * cm, cm)
    return wa.reshape(-1, wa.shape[2]), wb.transpose(1, 0, 2).reshape(cm, 9 * cm), wb_back, wc, ws


def plus(*values):
    total = values[0].astype(F32)
    for value in values[1:]:
        total = total + value.astype(F32)
    return total.astype(BF)


def columns_of(index, width):
    return pl.ds(pl.multiple_of(index * width, 128), width)


def swap_cores(send):
    return xor_permute(send, "dp", 1)


def row_groups(rows, width):
    return [(row, row // 16 * width) for row in range(0, rows, 16)]


def merge_kernel(*refs):
    count = len(refs) // 2 - 1
    keeps, sents, (far_ref, near_ref) = refs[:count], refs[count:-2], refs[-2:]
    core = this_core()
    x, side = lax.axis_index("dp") // 2, lax.rem(lax.axis_index("mp"), 2)
    total = near_ref.shape[2] // 2
    for q in range(2):
        for other, out_ref in ((0, near_ref), (1, far_ref)):
            own_x = x if other == 0 else 1 - x
            own_side = side if other == 0 else 1 - side
            column = jnp.where(core == 0, own_x, q)
            place = jnp.where(core == 0, q, own_side)
            first = q * total
            for keep, sent in zip(keeps, sents):
                width = keep.shape[2] // 2
                columns = columns_of(column, width)
                for row, start in row_groups(keep.shape[1], width):
                    for line in range(4):
                        block = 2 * line + place
                        out_ref[line, :, first + start : first + start + width] = plus(
                            keep[block, row : row + 16, columns], sent[block, row : row + 16, columns]
                        )
                first += keep.shape[1] // 16 * width


def turn_kernel(near_ref, sent_ref, far_out, near_out):
    x, side = lax.axis_index("dp") // 2, lax.rem(lax.axis_index("mp"), 2)
    mine = jnp.where(this_core() == 0, side, x)
    width = near_out.shape[2]
    for index, out_ref in ((mine, near_out), (1 - mine, far_out)):
        columns = columns_of(index, width)
        out_ref[...] = plus(near_ref[:, :, columns], sent_ref[:, :, columns])


def lines_kernel(near_ref, sent_ref, *out_refs):
    mine = lax.axis_index("mp") // 2
    for step, out_ref in enumerate(out_refs):
        place = jnp.bitwise_xor(mine, step)
        out_ref[...] = plus(near_ref[place], sent_ref[place])


def along_kernel(*refs):
    count = 4
    main_ref = refs[count]
    width = main_ref.shape[1]
    main_ref[...] = plus(*[ref[:, :width] for ref in refs[:count]])
    for fast_ref in refs[count + 1 :]:
        fast = plus(*[ref[:, width:] for ref in refs[:count]])
        fast_ref[...] = jnp.broadcast_to(fast[None], fast_ref.shape)


def merge(keeps, sents):
    columns = sum(keep.shape[1] // 16 * keep.shape[2] for keep in keeps)
    return quick_call(merge_kernel, [*keeps, *sents], [((4, 16, columns), BF)] * 2)


def turn(far, near):
    outs = [((4, 16, near.shape[2] // 2), BF)] * 2
    return quick_call(turn_kernel, [near, cross_permute(far, 0)], outs)


def cut_lines(far, near):
    arrays = [near, cross_permute(far, 1)]
    return quick_call(lines_kernel, arrays, [((16, near.shape[2]), BF)] * 4)


def along_line(mine, sent, width):
    outs = [((16, width), BF)]
    if mine.shape[1] > width:
        outs.append(((32, 16, mine.shape[1] - width), BF))
    return quick_call(along_kernel, [mine, *sent], outs)


def over_z(pieces):
    return [xor_permute(piece, "mp", 2 * step) for step, piece in enumerate(pieces) if step]


def clip_values(refs):
    core, x = this_core(), lax.axis_index("dp") // 2
    places = ((core, x), (core, 1 - x), (1 - core, x), (1 - core, 1 - x))
    return [(half, side, ref) for (half, side), ref in zip(places, refs)]


def clips_kernel(
    mine_ref, far_ref, other_ref, far_other_ref, c_ref, s_ref, b_ref, block_ref
):
    cu = s_ref.shape[0]
    wide = block_ref.shape[1] // 2
    half_rows = block_ref.shape[0] // 2
    for half, side, ref in clip_values((mine_ref, far_ref, other_ref, far_other_ref)):
        for group in range(half_rows // 16):
            rows = pl.ds(pl.multiple_of(half * half_rows + group * 16, 16), 16)
            values = ref[:, group * wide : (group + 1) * wide].astype(F32)
            block_ref[rows, columns_of(side, wide)] = values
        start = half_rows // 16 * wide
        count = b_ref.shape[0] * b_ref.shape[2] // 256
        rows = pl.ds(pl.multiple_of(half * 16, 16), 16)
        for k in range(count):
            unit = side * count + k
            columns = pl.ds(pl.multiple_of(lax.rem(unit, 2) * 128, 128), 128)
            values = ref[:, start + k * 128 : start + (k + 1) * 128].astype(F32)
            b_ref[unit // 2, rows, columns] = values
    for column in range(0, cu, 128):
        s_ref[column : column + 128, :] = block_ref[:, column : column + 128].T
    for column in range(cu, block_ref.shape[1], 128):
        c_ref[column - cu : column - cu + 128, :] = block_ref[:, column : column + 128].T


def clips_a_kernel(mine_ref, far_ref, other_ref, far_other_ref, a_ref):
    part = a_ref.shape[2] // 2
    for half, side, ref in clip_values((mine_ref, far_ref, other_ref, far_other_ref)):
        rows = pl.ds(pl.multiple_of(half * 16, 16), 16)
        for tap in range(3):
            values = ref[:, tap * part : (tap + 1) * part].astype(F32)
            a_ref[tap, rows, columns_of(side, part)] = values


def cross_clips(kernel, total, outs, scratch, other):
    sent = [xor_permute(total, "dp", bits) for bits in (2, 1, 3)]
    arrays = [held(total, other), *sent]
    return local_call(kernel, [], arrays, [(shape, F32) for shape in outs], scratch, SMALL)


def reduce_whole(blocks):
    whole = lax.psum(blocks.astype(BF), "dp")
    return lax.psum_scatter(whole, "mp", scatter_dimension=0, tiled=True)[0].astype(F32)


def tn(left, right):
    return lax.dot_general(left, right, (((0,), (0,)), ((), ())), preferred_element_type=F32)


def cut_halves(core, whole_ref, send_ref, keep_ref, groups=1):
    blocks, size = keep_ref.shape[0], keep_ref.shape[1] // groups
    for group in range(groups):
        for block in range(blocks):
            start = (group * blocks + block) * 2 * size
            place = slice(group * size, (group + 1) * size)
            send_ref[block, place, :] = whole_ref[pl.ds(pl.multiple_of(start + (1 - core) * size, size), size), :]
            keep_ref[block, place, :] = whole_ref[pl.ds(pl.multiple_of(start + core * size, size), size), :]


def grad_cs_kernel(dh_ref, ds_ref, joined_ref, hidden_ref, send_ref, keep_ref, whole_ref):
    wide, cu = dh_ref.shape[1], joined_ref.shape[1]
    for start in range(0, wide, 256):
        part = slice(start, start + 256)
        whole_ref[part, 0:cu] = tn(dh_ref[:, part], joined_ref[...]).astype(BF)
    whole_ref[:, cu:] = tn(ds_ref[...], hidden_ref[...]).astype(BF)
    cut_halves(this_core(), whole_ref, send_ref, keep_ref)


def fill_buffer(buffer, values_ref):
    clear_margins(buffer)
    for start in range(0, values_ref.shape[0], ROWS_STEP):
        rows = values_ref[start : start + ROWS_STEP, :].astype(F32)
        buffer[MARGIN + start : MARGIN + start + ROWS_STEP, :] = rows


def grad_b_kernel(
    ds_ref, hidden_ref, edge_ref, send_ref, keep_ref, whole_ref, buffer_ref, patches_ref
):
    fill_buffer(buffer_ref, hidden_ref)
    write_patches(buffer_ref, patches_ref, edge_ref)
    whole_ref[...] = tn(ds_ref[...], patches_ref[...]).astype(BF)
    cut_halves(this_core(), whole_ref, send_ref, keep_ref)


def grad_b_whole_kernel(
    ds_ref, hidden_ref, edge_ref, out_ref, buffer_ref, patches_ref
):
    fill_buffer(buffer_ref, hidden_ref)
    write_patches(buffer_ref, patches_ref, edge_ref)
    out_ref[...] = tn(ds_ref[...], patches_ref[...])


def grad_a_kernel(
    one_ref, two_ref, before_ref, after_ref, joined_ref, send_ref, keep_ref, whole_ref
):
    cm = whole_ref.shape[0] // 3
    pairs = ((two_ref, after_ref), (one_ref, two_ref), (before_ref, one_ref))
    for tap, (left_ref, right_ref) in enumerate(pairs):
        total = tn(left_ref[:, :cm], joined_ref[0]) + tn(right_ref[...], joined_ref[1])
        whole_ref[tap * cm : (tap + 1) * cm, :] = total.astype(BF)
    cut_halves(this_core(), whole_ref, send_ref, keep_ref, 3)


def leftward(values, j):
    return pltpu.roll(values, 128 - j * (128 // ALPHA), 1) if j else values


def packed(values, groups):
    size, width = values.shape[0] // groups, 128 // groups
    mask = lane_mask(size, 0)
    total = values[:size, :] * mask
    for k in range(1, groups):
        total = total + pltpu.roll(values[k * size : (k + 1) * size, :] * mask, k * width, 1)
    return total


def unpacked(values, groups):
    return [leftward(values, k) for k in range(groups)]


def fast_inner_kernel(
    hidden_a_ref, second_ref, hidden_ref, third_ref, edge_ref, out_ref, buffer_ref, patches_ref
):
    ci, cf = 128 // ALPHA, 128
    fill_buffer(buffer_ref, hidden_a_ref)
    write_patches(buffer_ref, patches_ref, edge_ref)
    raw = tn(patches_ref[...], second_ref[...])
    taps = [
        sum(leftward(raw[tap * 128 + j * ci : tap * 128 + (j + 1) * ci, :], j) for j in range(ALPHA))
        for tap in range(9)
    ]
    both = packed(jnp.concatenate(taps, axis=0), ALPHA)
    start = out_ref.shape[0] - ci
    rest = jnp.zeros((start - both.shape[0], 128), F32)
    out_ref[:start, :] = jnp.concatenate([both, rest], axis=0).astype(BF)
    raw = tn(hidden_ref[...], third_ref[...])
    out_ref[start:, :] = sum(
        raw[j * ci : (j + 1) * ci, j * cf : (j + 1) * cf] for j in range(ALPHA)
    ).astype(BF)


FAST_ROWS = 1536


def outer_rows(stack_ref, one_ref, two_ref, lateral_ref, dl_ref, inner_ref, out_ref):
    cf, kind = 128, out_ref.dtype
    raw = tn(stack_ref[0], one_ref[...]) + tn(stack_ref[1], two_ref[...])
    total = sum(leftward(raw[j * cf : (j + 3) * cf, :], j) for j in range(ALPHA))
    start = 3 * cf // ALPHA
    out_ref[:start, :] = packed(total, ALPHA).astype(kind)
    count = inner_ref.shape[0]
    out_ref[start : start + count, :] = inner_ref[...].astype(kind)
    start += count
    raw = tn(lateral_ref[0], dl_ref[0]) + tn(lateral_ref[1], dl_ref[1])
    size = raw.shape[0]
    out_ref[start : start + size, :] = raw[:, :128].astype(kind)
    out_ref[start + size : start + 2 * size, :] = raw[:, 128:].astype(kind)
    start += 2 * size
    out_ref[start:, :] = jnp.zeros((out_ref.shape[0] - start, 128), kind)


def fast_outer_kernel(
    stack_ref, one_ref, two_ref, lateral_ref, dl_ref, inner_ref, send_ref, keep_ref, whole_ref
):
    outer_rows(stack_ref, one_ref, two_ref, lateral_ref, dl_ref, inner_ref, whole_ref)
    core = this_core()
    groups = FAST_ROWS // 256
    for half, out_ref in ((core, keep_ref), (1 - core, send_ref)):
        for block in range(8):
            for group in range(groups):
                row = half * (FAST_ROWS // 2) + (block * groups + group) * 16
                rows = pl.ds(pl.multiple_of(row, 16), 16)
                out_ref[block, :, group * 128 : (group + 1) * 128] = whole_ref[rows, :]


def first_kernel(
    count_ref, sums_ref, first_ref, gf_ref, gs_ref, vf_ref, vs_ref, afa_ref, asa_ref, mask_ref,
    f0_ref, f1_ref, s0_ref, s1_ref, total_ref, tile_ref,
):
    fast_count, slow_count = count_ref[0], count_ref[1]
    total = jnp.sum(sums_ref[...], axis=0)
    total_ref[...] = total
    cells = f0_ref.shape[0]
    fast_beta, fast_gamma, beta, gamma = split(total, (128, 128, 256, 256))
    ft, fq, st, sq = split(first_ref[...], (128, 128, 256, 256))
    mean, inverse = mean_inverse(fold_lanes(ft, ALPHA), fold_lanes(fq, ALPHA), fast_count)
    fast_lines = back_line(
        mean, inverse, tiled_affine(afa_ref, tile_ref)[0:1], fold_lanes(fast_beta, ALPHA), fold_lanes(fast_gamma, ALPHA), fast_count
    )
    slow_lines = back_line(*mean_inverse(st, sq, slow_count), asa_ref[0:1, :], beta, gamma, slow_count)
    for grad_ref, value_ref, outs, (one, two, three) in (
        (gf_ref, vf_ref, (f0_ref, f1_ref), fast_lines),
        (gs_ref, vs_ref, (s0_ref, s1_ref), slow_lines),
    ):
        for frame, out_ref in enumerate(outs):
            now = slice(frame * cells, (frame + 1) * cells)
            mask = wide_mask(mask_ref[now, :], grad_ref.shape[1])
            grad = mask * (grad_ref[now, :] * one - two - value_ref[now, :] * three)
            out_ref[...] = grad.astype(BF)


def joined_back_kernel(
    mask_ref, one_ref, two_ref, before_ref, after_ref, dh_ref, wa_ref, ws_ref, out_ref
):
    cells = one_ref.shape[0]
    cs = out_ref.shape[2]
    cm = wa_ref.shape[0] // 3
    for frame, pieces in enumerate(
        ((two_ref, one_ref, before_ref), (after_ref, two_ref, one_ref))
    ):
        mask = mask_ref[frame * cells : (frame + 1) * cells, :]
        taps = jnp.concatenate([piece[:, :cm] for piece in pieces], axis=1)
        for start in range(0, cs, 256):
            part = slice(start, start + 256)
            grad = mm(taps, wa_ref[:, part]) + mm_t(dh_ref[frame], ws_ref[part, :])
            out_ref[:, frame, part] = (grad * wide_mask(mask, 256)).astype(BF)


def lateral_back_kernel(
    mask_ref, one_ref, two_ref, before_ref, after_ref, fast_ref, dh_ref, wa_ref, ws_ref,
    lat_ref, edge_ref, a_ref, s_ref, sems,
):
    cells, cl = one_ref.shape[0], lat_ref.shape[2]
    cm = wa_ref.shape[0] // 3
    cs = ws_ref.shape[0] - cl
    copies = [
        pltpu.make_async_copy(wa_ref.at[:, pl.ds(cs, cl)], a_ref, sems.at[0]),
        pltpu.make_async_copy(ws_ref.at[pl.ds(cs, cl), :], s_ref, sems.at[1]),
    ]
    for copy in copies:
        copy.start()
    for copy in copies:
        copy.wait()
    for frame, pieces in enumerate(
        ((two_ref, one_ref, before_ref), (after_ref, two_ref, one_ref))
    ):
        mask = mask_ref[frame * cells : (frame + 1) * cells, :]
        taps = jnp.concatenate([piece[:, :cm] for piece in pieces], axis=1)
        grad = mm(taps, a_ref[...]) + mm_t(dh_ref[frame], s_ref[...])
        grad = (grad * wide_mask(mask, cl)).astype(BF)
        lat_ref[frame] = grad
        if frame == 0:
            edge_ref[:, :cl] = grad
            edge_ref[:, cl:] = fast_ref[...]


def lateral_back(arrays, outs):
    wa, ws = arrays[-2:]
    cl = outs[0][0][2]
    anywhere = pl.BlockSpec(memory_space=pl.ANY)
    return pl.pallas_call(
        lateral_back_kernel,
        out_shape=[jax.ShapeDtypeStruct(s, d) for s, d in outs],
        in_specs=[VMEM] * (len(arrays) - 2) + [anywhere] * 2,
        out_specs=[VMEM] * len(outs),
        scratch_shapes=[
            pltpu.VMEM((wa.shape[0], cl), BF),
            pltpu.VMEM((cl, ws.shape[1]), BF),
            pltpu.SemaphoreType.DMA((2,)),
        ],
        compiler_params=pltpu.CompilerParams(vmem_limit_bytes=LARGE),
        cost_estimate=FREE,
    )(*arrays)


def unpack_kernel(
    clip_ref, in_ref, mask_ref, out_ref, tail_ref, last_ref, head_ref, count_ref, rows_ref
):
    frames, cells = out_ref.shape[:2]
    step = frames * ALPHA
    pixels = H * W
    batch = cells // pixels
    total = sum(clip_ref[i, 0] for i in range(clip_ref.shape[0]))
    count_ref[1] = (total * pixels).astype(F32)
    count_ref[0] = (total * (pixels * ALPHA)).astype(F32)
    rows_ref[...] = in_ref[...].astype(F32)
    spot = lax.broadcasted_iota(jnp.int32, (cells, 128), 0)
    for frame in range(frames):
        place = lax.axis_index("mp") * frames + frame
        mask = jnp.zeros((cells, 128), F32)
        for b in range(batch):
            length = clip_ref[lax.axis_index("dp") * batch + b, 0]
            valid = (place < length).astype(F32)
            inside = (spot >= b * pixels) & (spot < (b + 1) * pixels)
            mask = jnp.where(inside, valid, mask)
        mask_ref[frame * cells : (frame + 1) * cells, :] = mask
        for j in range(ALPHA):
            values = rows_ref[pl.ds(frame * ALPHA + j, cells, step), :] * mask
            values = values.astype(BF)
            out_ref[frame, :, j * 128 : (j + 1) * 128] = values
            if frame == frames - 1 and j >= 2:
                (tail_ref, last_ref)[j - 2][...] = values
            if frame == 0 and j == 0:
                head_ref[...] = values


def copies():
    width = 128 // ALPHA
    lanes = jnp.bitwise_and(lax.broadcasted_iota(jnp.int32, (width, 128), 1), width - 1)
    rows = lax.broadcasted_iota(jnp.int32, (width, 128), 0)
    return jnp.where(lanes == rows, 1.0, 0.0).astype(BF)


def lane_mask(rows, j):
    group = lax.broadcasted_iota(jnp.int32, (rows, 128), 1) // (128 // ALPHA)
    return jnp.where(group == j, 1.0, 0.0)


def tiled_affine(ref, tile_ref):
    if ref.shape[1] == 128:
        return jnp.concatenate([ref[...]] * ALPHA, axis=1)
    tile_ref[...] = jnp.zeros_like(tile_ref)
    tile_ref[0:2, 0 : ref.shape[1]] = ref[...]
    return fold_lanes(tile_ref[0:2, :], ALPHA)


def build_a(w_ref, out_ref):
    tiles = mm(w_ref[...], copies())
    size = w_ref.shape[0] // 3
    masks = [lane_mask(size, j) for j in range(ALPHA)]
    for i in range(ALPHA + 2):
        total = sum(
            tiles[(i - j) * size : (i - j + 1) * size, :] * masks[j]
            for j in range(ALPHA)
            if 0 <= i - j < 3
        )
        out_ref[i * size : (i + 1) * size, :] = total.astype(BF)


def build_b(w_ref, out_ref, back):
    ci = w_ref.shape[1]
    for tap in range(9):
        block = w_ref[tap * ci : (tap + 1) * ci, :]
        tile = tn(block, copies()) if back else mm(block, copies())
        place = 8 - tap if back else tap
        for j in range(ALPHA):
            start = place * 128 + j * ci
            out_ref[start : start + ci, :] = (tile * lane_mask(ci, j)).astype(BF)


def build_c(w_ref, out_ref):
    ci, cf = w_ref.shape
    out_ref[...] = jnp.zeros_like(out_ref)
    for j in range(ALPHA):
        out_ref[j * ci : (j + 1) * ci, j * cf : (j + 1) * cf] = w_ref[...]


def build_back(w_ref, out_ref):
    ci = w_ref.shape[1]
    size = w_ref.shape[0] // 3
    one = jnp.where(
        lax.broadcasted_iota(jnp.int32, (ci, ci), 0) == lax.broadcasted_iota(jnp.int32, (ci, ci), 1),
        1.0,
        0.0,
    ).astype(BF)
    out_ref[...] = jnp.zeros_like(out_ref)
    for tap in range(3):
        block = mm_t(one, w_ref[tap * size : (tap + 1) * size, :]).astype(BF)
        for j in range(ALPHA):
            start = 128 + (j + 1 - tap) * ci
            out_ref[start : start + ci, j * size : (j + 1) * size] = block


def entry_kernel(
    mask_ref, fast_ref, before_ref, last_ref, after_ref, slow_ref, wa_ref, wl_ref,
    stack_ref, lateral_ref, first_ref, sums_ref, joined_ref, big_ref, rows_ref,
):
    cells = before_ref.shape[0]
    cs, cf = slow_ref.shape[2], 128
    build_a(wa_ref, big_ref)
    for column in range(0, cs, 128):
        values = slow_ref[:, :, column : column + 128].reshape(2 * cells, 128)
        rows_ref[column // 128] = values.astype(F32)
    tots, squares = [], []
    for frame in range(2):
        mask = mask_ref[frame * cells : (frame + 1) * cells, :]
        own = fast_ref[frame]
        past = (before_ref[...], last_ref[...])
        if frame:
            past = (fast_ref[0][:, 2 * cf : 3 * cf], fast_ref[0][:, 3 * cf :])
        following = fast_ref[1][:, :cf] if frame == 0 else after_ref[...]
        stack_ref[frame, :, 0:cf] = past[1]
        stack_ref[frame, :, cf : 5 * cf] = own
        stack_ref[frame, :, 5 * cf :] = following
        lateral_ref[frame, :, 0:cf] = past[0]
        lateral_ref[frame, :, cf : 2 * cf] = past[1]
        lateral_ref[frame, :, 2 * cf :] = own[:, : 3 * cf]
        value = mm(stack_ref[frame], big_ref[...])
        first_ref[frame * cells : (frame + 1) * cells, :] = value
        tots.append(total_row(value * mask))
        squares.append(total_row(value * mask * value))
        lateral = mm(lateral_ref[frame], wl_ref[...]).astype(BF)
        joined_ref[frame, :, cs:] = lateral * wide_mask(mask.astype(BF), 256)
        for column in range(0, cs, 128):
            values = rows_ref[column // 128, pl.ds(frame, cells, 2), :] * mask
            joined_ref[frame, :, column : column + 128] = values.astype(BF)
    sums_ref[:, :128] = tots[0] + tots[1]
    sums_ref[:, 128:] = squares[0] + squares[1]


def taps_kernel(joined_ref, wa_ref, base_ref, right_ref, left_ref, one_ref, two_ref):
    cells, cm = right_ref.shape
    one_ref[...] = mm_t(joined_ref[0], wa_ref[...])
    two_ref[...] = mm_t(joined_ref[1], wa_ref[...])
    base_ref[:cells, :] = one_ref[:, cm : 2 * cm] + two_ref[:, 2 * cm :]
    base_ref[cells:, :] = two_ref[:, cm : 2 * cm] + one_ref[:, :cm]
    right_ref[...] = two_ref[:, :cm].astype(BF)
    left_ref[...] = one_ref[:, 2 * cm :].astype(BF)


def placed_taps_kernel(
    joined_ref, own_ref, side_ref, core_ref, both_ref,
    wa_ref, base_ref, right_ref, left_ref, one_ref, two_ref, *, sync,
):
    place_pieces(place_a, (own_ref, side_ref, core_ref, both_ref), (wa_ref,))
    sync.send(0)
    taps_kernel(joined_ref, wa_ref, base_ref, right_ref, left_ref, one_ref, two_ref)


def first_sums_kernel(mask_ref, base_ref, left_ref, right_ref, fast_ref, first_ref, vec_ref):
    cells, cm = left_ref.shape
    tot = square = jnp.zeros((1, cm), F32)
    for frame, halo_ref in enumerate((left_ref, right_ref)):
        now = slice(frame * cells, (frame + 1) * cells)
        value = base_ref[now, :] + halo_ref[...].astype(F32)
        first_ref[now, :] = value
        masked = value * wide_mask(mask_ref[now, :], cm)
        tot = tot + total_row(masked)
        square = square + total_row(masked * value)
    send_all(vec_ref, [fast_ref[...], tot, square])


def sum_kernel(sums_ref, vec_ref):
    total = jnp.sum(sums_ref[...], axis=0)
    vec_ref[...] = jnp.broadcast_to(total[None], vec_ref.shape)


def fast_back_kernel(
    mask_ref, one_ref, two_ref, before_ref, after_ref, dl_ref, cot_ref, wl_ref, wa_ref,
    out_ref, rows_ref, big_ref,
):
    cells = one_ref.shape[0]
    cf = 128
    build_back(wa_ref, big_ref)
    for frame in range(2):
        now = slice(frame * cells, (frame + 1) * cells)
        mask = mask_ref[now, :]
        cl = dl_ref.shape[2]
        pieces = (before_ref[...], one_ref[...], two_ref[...])
        if frame:
            pieces = pieces[1:] + (after_ref[:, cl:],)
        taps = jnp.concatenate(pieces, axis=1)
        now_dl, next_dl = dl_ref[frame], after_ref[:, :cl] if frame else dl_ref[1]
        for j in range(ALPHA):
            part = slice(j * 128, (j + 1) * 128)
            grad = mm(taps, big_ref[:, part]) + cot_ref[now, part]
            if j < 3:
                grad = grad + mm_t(now_dl, wl_ref[(j + 2) * cf : (j + 3) * cf, :])
            if j >= 2:
                grad = grad + mm_t(next_dl, wl_ref[(j - 2) * cf : (j - 1) * cf, :])
            rows_ref[pl.ds(frame * ALPHA + j, cells, 2 * ALPHA), :] = grad * mask
    out_ref[...] = rows_ref[...].astype(BF)


def dot(left, right, left_dim, right_dim):
    return lax.dot_general(
        left, right, (((left_dim,), (right_dim,)), ((), ())), preferred_element_type=F32
    )


def rows_dot(left, right):
    return lax.dot_general(
        left, right, (((0, 1), (0, 1)), ((), ())), preferred_element_type=F32
    )


def folded(vector, groups):
    return jnp.sum(vector.reshape(groups, -1), axis=0)


def norm_terms(totals, squares, count, groups=1):
    average = totals / count
    inverse = lax.rsqrt(squares / count - average * average + NORM_EPSILON)
    return jnp.tile(average, groups), jnp.tile(inverse, groups)


ROWS_STEP = 112
TAPS = [(dh, dw) for dh in (-1, 0, 1) for dw in (-1, 0, 1)]


def row_chunks(rows, step):
    return [pl.ds(start, step) for start in range(0, rows, step)]


def loop_rows(rows, step, body, init):
    def turn(i, carry):
        return body(pl.ds(pl.multiple_of(i * step, step), step), carry)

    return lax.fori_loop(0, rows // step, turn, init)


def collapse(values):
    return jnp.sum(values.reshape(-1, 8, values.shape[-1]), axis=0)


def gate_of(values):
    return 0.5 * jnp.tanh(0.5 * values) + 0.5


def fold_lanes(vector, groups):
    width = vector.shape[-1] // groups
    total = vector
    for j in range(1, groups):
        total = total + pltpu.roll(vector, j * width, 1)
    return total


def mean_inverse(totals, squares, count):
    average = totals / count
    return average, lax.rsqrt(squares / count - average * average + NORM_EPSILON)


def line(average, inverse, affine):
    scale = affine[0:1] * inverse
    return scale, affine[1:2] - average * scale


def send_all(vec_ref, pieces):
    start = 0
    for piece in pieces:
        width = piece.shape[-1]
        spread = jnp.broadcast_to(piece[None], (vec_ref.shape[0], 1, width))
        vec_ref[:, :, start : start + width] = spread
        start += width


def received(sums_ref, widths):
    total = jnp.sum(sums_ref[...], axis=0)
    return split(total, widths)


def split(total, widths):
    pieces = []
    start = 0
    for width in widths:
        pieces.append(total[:, start : start + width])
        start += width
    return pieces


def total_row(vector):
    return jnp.sum(vector, axis=0, keepdims=True)


MARGIN = 16


def clear_margins(buffer):
    rows = buffer.shape[0]
    zeros = jnp.zeros((MARGIN, buffer.shape[1]), F32)
    buffer[0:MARGIN, :] = zeros
    buffer[rows - MARGIN : rows, :] = zeros


def write_patches(buffer, patches, edges):
    rows, channels = patches.shape[0], buffer.shape[1]
    for start in range(0, rows, ROWS_STEP):
        top, bottom, left, right = (edges[k, start : start + ROWS_STEP, :] for k in range(4))
        for tap, (dh, dw) in enumerate(TAPS):
            mask = None
            if dh:
                mask = top if dh < 0 else bottom
            if dw:
                side = left if dw < 0 else right
                mask = side if mask is None else mask * side
            offset = MARGIN + start + W * dh + dw
            for column in range(0, channels, 128):
                piece = buffer[offset : offset + ROWS_STEP, column : column + 128]
                if mask is not None:
                    piece = piece * mask
                place = tap * channels + column
                patches[start : start + ROWS_STEP, place : place + 128] = piece.astype(BF)


def mm(left, right):
    return jnp.dot(left, right, preferred_element_type=F32)


def mm_t(left, right):
    return lax.dot_general(left, right, (((1,), (1,)), ((), ())), preferred_element_type=F32)


def wide_mask(mask, width):
    return jnp.concatenate([mask] * (width // 128), axis=1) if width > 128 else mask


def conv_kernel(
    count_ref, sums_ref, vf_ref, vs_ref, af_ref, as_ref, mask_ref, edge_ref, wf_ref, ws_ref,
    hf_ref, hs_ref, of_ref, os_ref, total_ref, vec_ref, bf_ref, bs_ref, pf_ref, ps_ref, big_ref, tile_ref,
):
    fast_count, slow_count = count_ref[0], count_ref[1]
    total = jnp.sum(sums_ref[...], axis=0)
    total_ref[...] = total
    ft, fq, st, sq = split(total, (128, 128, 256, 256))
    lines = []
    build_b(wf_ref, big_ref, False)
    for tot, square, count, affine in ((ft, fq, fast_count, af_ref), (st, sq, slow_count, as_ref)):
        if tot.shape[-1] == 128:
            tot, square = fold_lanes(tot, ALPHA), fold_lanes(square, ALPHA)
            affine = tiled_affine(affine, tile_ref)
        else:
            affine = affine[...]
        lines.append(line(*mean_inverse(tot, square, count), affine))
    rows = vf_ref.shape[0]
    for value_ref, hidden_ref, buffer, (scale, shift) in (
        (vf_ref, hf_ref, bf_ref, lines[0]),
        (vs_ref, hs_ref, bs_ref, lines[1]),
    ):
        width = value_ref.shape[1]
        clear_margins(buffer)
        for start in range(0, rows, ROWS_STEP):
            z = value_ref[start : start + ROWS_STEP, :] * scale + shift
            hidden = z * gate_of(z) * wide_mask(mask_ref[start : start + ROWS_STEP, :], width)
            buffer[MARGIN + start : MARGIN + start + ROWS_STEP, :] = hidden
            hidden_ref[start : start + ROWS_STEP, :] = hidden.astype(BF)
    write_patches(bf_ref, pf_ref, edge_ref)
    write_patches(bs_ref, ps_ref, edge_ref)
    of_ref[...] = mm(pf_ref[...], big_ref[...])
    os_ref[...] = mm_t(ps_ref[...], ws_ref[...])
    pieces = []
    for out_ref in (of_ref, os_ref):
        width = out_ref.shape[1]

        def body(rows_now, carry):
            value = out_ref[rows_now, :]
            masked = value * wide_mask(mask_ref[rows_now, :], width)
            return carry[0] + collapse(masked), carry[1] + collapse(masked * value)

        zero = jnp.zeros((8, width), F32)
        pieces += [total_row(v) for v in loop_rows(rows, ROWS_STEP, body, (zero, zero))]
    send_all(vec_ref, pieces)


def expand_kernel(
    count_ref, sums_ref, short_ref, vf_ref, vs_ref, af_ref, as_ref, mask_ref, wf_ref, ws_ref,
    hf_ref, hs_ref, yf_ref, ys_ref, total_ref, vec_ref, of_ref, os_ref, big_ref, tile_ref,
):
    fast_count, slow_count = count_ref[0], count_ref[1]
    total = jnp.sum(sums_ref[...], axis=0)
    total_ref[...] = total
    ft, fq, st, sq = split(total, (128, 128, 256, 256))
    ft, fq = fold_lanes(ft, ALPHA), fold_lanes(fq, ALPHA)
    build_c(wf_ref, big_ref)
    lines = (
        line(*mean_inverse(ft, fq, fast_count), tiled_affine(af_ref, tile_ref)),
        line(*mean_inverse(st, sq, slow_count), as_ref[...]),
    )
    rows = vf_ref.shape[0]
    for value_ref, hidden_ref, (scale, shift) in ((vf_ref, hf_ref, lines[0]), (vs_ref, hs_ref, lines[1])):
        width = value_ref.shape[1]

        def body(rows_now, carry):
            z = value_ref[rows_now, :] * scale + shift
            hidden = z * gate_of(z) * wide_mask(mask_ref[rows_now, :], width)
            hidden_ref[rows_now, :] = hidden.astype(BF)
            return carry

        loop_rows(rows, ROWS_STEP, body, 0)
    of_ref[...] = mm(hf_ref[...], big_ref[...])
    os_ref[...] = mm(hs_ref[...], ws_ref[...])
    pieces = []
    for out_ref, low_ref in ((of_ref, yf_ref), (os_ref, ys_ref)):
        width = out_ref.shape[1]
        tots, squares = [], []
        for column in range(0, width, 512):

            def body(rows_now, carry):
                value = out_ref[rows_now, column : column + 512]
                low_ref[rows_now, column : column + 512] = value.astype(low_ref.dtype)
                value = value.astype(low_ref.dtype).astype(F32)
                masked = value * wide_mask(mask_ref[rows_now, :], 512)
                return carry[0] + collapse(masked), carry[1] + collapse(masked * value)

            zero = jnp.zeros((8, 512), F32)
            one, two = loop_rows(rows, 16, body, (zero, zero))
            tots.append(total_row(one))
            squares.append(total_row(two))
        if width == 512:
            pieces += [sum(v[:, j * 128 : (j + 1) * 128] for j in range(ALPHA)) for v in (tots[0], squares[0])]
        else:
            pieces += [jnp.concatenate(tots, 1), jnp.concatenate(squares, 1)]
    send_all(vec_ref, pieces + [short_ref[...]])


def short_kernel(mask_ref, joined_ref, ws_ref, out_ref, vec_ref):
    rows, wide = out_ref.shape
    for column in range(0, wide, 256):
        part = slice(column, column + 256)
        one = jnp.zeros((8, 256), F32)
        two = one
        for start in range(0, rows, 2 * ROWS_STEP):
            now = slice(start, min(start + 2 * ROWS_STEP, rows))
            value = mm(joined_ref[now, :], ws_ref[:, part])
            out_ref[now, part] = value.astype(BF)
            value = value.astype(BF).astype(F32)
            masked = value * wide_mask(mask_ref[now, :], 256)
            one = one + collapse(masked)
            two = two + collapse(masked * value)
        vec_ref[:, part] = total_row(one)
        vec_ref[:, wide + column : wide + column + 256] = total_row(two)


def placed_short_kernel(
    mask_ref, joined_ref, own_ref, side_ref, core_ref, both_ref, ws_ref, out_ref, vec_ref, *, sync
):
    place_pieces(place_short, (own_ref, side_ref, core_ref, both_ref), (ws_ref,))
    sync.send(0)
    short_kernel(mask_ref, joined_ref, ws_ref, out_ref, vec_ref)


def output_kernel(
    count_ref, sums_ref, vf_ref, vs_ref, vh_ref, fast_ref, cf_ref, cs_ref,
    af_ref, as_ref, ah_ref, mask_ref,
    yf_ref, ys_ref, gf_ref, gs_ref, total_ref, vec_ref, rows_ref, cots_ref, *, sync,
):
    fast_count, slow_count = count_ref[0], count_ref[1]
    total = jnp.sum(sums_ref[...], axis=0)
    total_ref[...] = total
    wide = vs_ref.shape[1]
    ft, fq, st, sq, ht, hq = split(total, (128, 128, wide, wide, wide, wide))
    rows = vf_ref.shape[0]
    mean, inverse = mean_inverse(ft, fq, fast_count)
    mean, inverse = (jnp.concatenate([v] * ALPHA, 1) for v in (mean, inverse))
    scale, shift = line(mean, inverse, tiled_affine(af_ref, None))

    frames, cells = fast_ref.shape[:2]
    step = frames * ALPHA
    cots_ref[...] = cf_ref[...].astype(F32)
    zero = jnp.zeros((8, 512), F32)
    beta = gamma = jnp.zeros((1, 128), F32)
    for frame in range(frames):
        now = slice(frame * cells, (frame + 1) * cells)
        for j in range(ALPHA):
            part = slice(j * 128, (j + 1) * 128)
            place = pl.ds(frame * ALPHA + j, cells, step)
            mask = mask_ref[now, :]
            value = vf_ref[now, part]
            z = value * scale[:, part] + shift[:, part] + fast_ref[frame, :, part].astype(F32)
            gate = gate_of(z)
            rows_ref[place, :] = mask * z * gate
            grad = cots_ref[place, :] * mask * gate * (1.0 + z * (1.0 - gate))
            gf_ref[now, part] = grad
            beta = beta + total_row(grad)
            gamma = gamma + total_row(grad * value)
    yf_ref[...] = rows_ref[...].astype(BF)
    sync.send(0, 2)
    sync.arrive(2, 3, 6)
    pieces = [beta, (gamma - mean[:, :128] * beta) * inverse[:, :128]]
    mean_c, inverse_c = mean_inverse(st, sq, slow_count)
    mean_h, inverse_h = mean_inverse(ht, hq, slow_count)
    scale_c, shift_c = line(mean_c, inverse_c, as_ref[...])
    scale_h, shift_h = line(mean_h, inverse_h, ah_ref[...])
    betas, gammas, others = [], [], []
    for column in range(0, wide, 512):
        part = slice(column, column + 512)
        sc, sh, shift_both = scale_c[:, part], scale_h[:, part], shift_c[:, part] + shift_h[:, part]

        def body(rows_now, carry):
            third, short = vs_ref[rows_now, part].astype(F32), vh_ref[rows_now, part].astype(F32)
            mask = wide_mask(mask_ref[rows_now, :], 512)
            z = third * sc + short * sh + shift_both
            gate = gate_of(z)
            ys_ref[rows_now, part] = (mask * z * gate).astype(BF)
            grad = cs_ref[rows_now, part].astype(F32) * mask * gate * (1.0 + z * (1.0 - gate))
            gs_ref[rows_now, part] = grad.astype(BF)
            grad = grad.astype(BF).astype(F32)
            return (
                carry[0] + collapse(grad),
                carry[1] + collapse(grad * third),
                carry[2] + collapse(grad * short),
            )

        beta, gamma, other = (total_row(v) for v in loop_rows(rows, 16, body, (zero, zero, zero)))
        betas.append(beta)
        gammas.append((gamma - mean_c[:, part] * beta) * inverse_c[:, part])
        others.append((other - mean_h[:, part] * beta) * inverse_h[:, part])
    pieces += [jnp.concatenate(v, 1) for v in (betas, gammas, others)]
    sync.send(1, 3)
    send_all(vec_ref, pieces)


def back_line(mean, inverse, scale, beta, gamma, count):
    first = inverse * scale
    third = first * gamma * inverse / count
    return first, first * beta / count - mean * third, third


def narrow_kernel(
    count_ref, sums_ref, third_ref, second_ref,
    gf_ref, gs_ref, vf_ref, vs_ref, vh_ref, uf_ref, us_ref,
    afc_ref, asc_ref, ash_ref, afb_ref, asb_ref, mask_ref, wf_ref, ws_ref,
    df_ref, ds_ref, dh_ref, of_ref, os_ref, total_ref, vec_ref, big_ref, tile_ref, *, sync,
):
    fast_count, slow_count = count_ref[0], count_ref[1]
    total = jnp.sum(sums_ref[...], axis=0)
    total_ref[...] = total
    wide = vs_ref.shape[1]
    rows = vf_ref.shape[0]
    fast_beta, fast_gamma, beta, gamma_c, gamma_h = split(total, (128, 128, wide, wide, wide))
    ft, fq, st, sq, ht, hq = split(third_ref[...], (128, 128, wide, wide, wide, wide))
    mean, inverse = mean_inverse(ft, fq, fast_count)
    tiled = [jnp.concatenate([v] * ALPHA, 1) for v in (mean, inverse, fast_beta, fast_gamma)]
    build_c(wf_ref, big_ref)
    f1, f2, f3 = back_line(tiled[0], tiled[1], tiled_affine(afc_ref, None)[0:1], tiled[2], tiled[3], fast_count)

    def fast_body(rows_now, carry):
        mask = wide_mask(mask_ref[rows_now, :], 512)
        grad = mask * (gf_ref[rows_now, :].astype(F32) * f1 - f2 - vf_ref[rows_now, :].astype(F32) * f3)
        df_ref[rows_now, :] = grad.astype(BF)
        return carry

    loop_rows(rows, 16, fast_body, 0)
    sync.send(0)
    sync.arrive(4, 6, 7)
    mean_c, inverse_c = mean_inverse(st, sq, slow_count)
    mean_h, inverse_h = mean_inverse(ht, hq, slow_count)
    lines_c = back_line(mean_c, inverse_c, asc_ref[0:1, :], beta, gamma_c, slow_count)
    lines_h = back_line(mean_h, inverse_h, ash_ref[0:1, :], beta, gamma_h, slow_count)
    for column in range(0, wide, 512):
        part = slice(column, column + 512)
        c1, c2, c3 = (v[:, part] for v in lines_c)
        h1, h2, h3 = (v[:, part] for v in lines_h)

        def body(rows_now, carry):
            mask = wide_mask(mask_ref[rows_now, :], 512)
            grad = gs_ref[rows_now, part].astype(F32)
            third, short = vs_ref[rows_now, part].astype(F32), vh_ref[rows_now, part].astype(F32)
            ds_ref[rows_now, part] = (mask * (grad * c1 - c2 - third * c3)).astype(BF)
            dh_ref[rows_now, part] = (mask * (grad * h1 - h2 - short * h3)).astype(BF)
            return carry

        loop_rows(rows, 16, body, 0)
    sync.send(1, 2)
    sync.arrive(8, 9, 17)
    of_ref[...] = mm_t(df_ref[...], big_ref[...])
    os_ref[...] = mm_t(ds_ref[...], ws_ref[...])
    ft, fq, st, sq = split(second_ref[...], (128, 128, 256, 256))
    pieces = slope_sums(
        (of_ref, uf_ref, tiled_affine(afb_ref, tile_ref), fold_lanes(ft, ALPHA), fold_lanes(fq, ALPHA), fast_count),
        (os_ref, us_ref, asb_ref, st, sq, slow_count),
        mask_ref,
    )
    send_all(vec_ref, pieces)


def slope_sums(fast_parts, slow_parts, mask_ref):
    pieces = []
    for out_ref, value_ref, affine, tot, square, count in (fast_parts, slow_parts):
        width = out_ref.shape[1]
        mean, inverse = mean_inverse(tot, square, count)
        scale, shift = line(mean, inverse, affine[...])

        def body(rows_now, carry):
            value = value_ref[rows_now, :]
            z = value * scale + shift
            gate = gate_of(z)
            mask = wide_mask(mask_ref[rows_now, :], width)
            grad = out_ref[rows_now, :] * mask * gate * (1.0 + z * (1.0 - gate))
            out_ref[rows_now, :] = grad
            return carry[0] + collapse(grad), carry[1] + collapse(grad * value)

        zero = jnp.zeros((8, width), F32)
        rows = out_ref.shape[0]
        beta, gamma = (total_row(v) for v in loop_rows(rows, ROWS_STEP // 2, body, (zero, zero)))
        pieces += [beta, (gamma - mean * beta) * inverse]
    return pieces


def conv_back_kernel(
    count_ref, sums_ref, second_ref, first_ref,
    gf_ref, gs_ref, uf_ref, us_ref, vf_ref, vs_ref,
    afb_ref, asb_ref, afa_ref, asa_ref, mask_ref, edge_ref, wf_ref, ws_ref,
    df_ref, ds_ref, of_ref, os_ref, total_ref, vec_ref,
    bf_ref, bs_ref, pf_ref, ps_ref, big_ref, tile_ref,
):
    fast_count, slow_count = count_ref[0], count_ref[1]
    total = jnp.sum(sums_ref[...], axis=0)
    total_ref[...] = total
    rows = gf_ref.shape[0]
    build_b(wf_ref, big_ref, True)
    fast_beta, fast_gamma, beta, gamma = split(total, (128, 128, 256, 256))
    ft, fq, st, sq = split(second_ref[...], (128, 128, 256, 256))
    mean, inverse = mean_inverse(fold_lanes(ft, ALPHA), fold_lanes(fq, ALPHA), fast_count)
    fast_lines = back_line(
        mean, inverse, tiled_affine(afb_ref, tile_ref)[0:1], fold_lanes(fast_beta, ALPHA), fold_lanes(fast_gamma, ALPHA), fast_count
    )
    slow_lines = back_line(*mean_inverse(st, sq, slow_count), asb_ref[0:1, :], beta, gamma, slow_count)
    for grad_ref, value_ref, out_ref, buffer, lines in (
        (gf_ref, uf_ref, df_ref, bf_ref, fast_lines),
        (gs_ref, us_ref, ds_ref, bs_ref, slow_lines),
    ):
        width = grad_ref.shape[1]
        one, two, three = lines
        clear_margins(buffer)
        for start in range(0, rows, ROWS_STEP):
            now = slice(start, start + ROWS_STEP)
            grad = grad_ref[now, :] * one - two - value_ref[now, :] * three
            grad = grad * wide_mask(mask_ref[now, :], width)
            out_ref[now, :] = grad.astype(BF)
            buffer[MARGIN + start : MARGIN + start + ROWS_STEP, :] = grad
    write_patches(bf_ref, pf_ref, edge_ref)
    write_patches(bs_ref, ps_ref, edge_ref)
    of_ref[...] = mm(pf_ref[...], big_ref[...])
    os_ref[...] = mm(ps_ref[...], ws_ref[...])
    ft, fq, st, sq = split(first_ref[...], (128, 128, 256, 256))
    pieces = slope_sums(
        (of_ref, vf_ref, tiled_affine(afa_ref, tile_ref), fold_lanes(ft, ALPHA), fold_lanes(fq, ALPHA), fast_count),
        (os_ref, vs_ref, asa_ref, st, sq, slow_count),
        mask_ref,
    )
    send_all(vec_ref, pieces)


def exchange(vec):
    return lax.all_to_all(vec, ("dp", "mp"), 0, 0, tiled=True)


def fast_results_kernel(in_ref, a_ref, b_ref, c_ref, l_ref, rows_ref, taps_ref):
    if len(in_ref.shape) == 3:
        groups = FAST_ROWS // 512
        for device in range(in_ref.shape[0]):
            x, core, block = device // 16, device // 8 % 2, device % 8
            for k in range(groups):
                start = core * (FAST_ROWS // 2) + ((block * 2 + x) * groups + k) * 16
                rows_ref[start : start + 16, :] = in_ref[device, :, k * 128 : (k + 1) * 128]
        in_ref = rows_ref
    taps, cf, ci = a_ref.shape
    start = 0
    for out_ref, rest in ((a_ref, 0), (b_ref, 8)):
        count, rows = out_ref.shape[:2]
        size = count * rows // ALPHA
        values = in_ref[start : start + size + rest, :].astype(F32)[:size, :]
        for k, piece in enumerate(unpacked(values, ALPHA)):
            taps_ref[k * size : (k + 1) * size, :] = piece
        for tap in range(count):
            out_ref[tap] = taps_ref[tap * rows : (tap + 1) * rows, :][:, :ci]
        start += size + rest
    c_ref[...] = in_ref[start : start + ci, :].astype(F32)
    start += ci
    for side in range(2):
        for tap in range(5):
            rows = slice(start + (side * 5 + tap) * cf, start + (side * 5 + tap + 1) * cf)
            l_ref[tap, :, side * 128 : (side + 1) * 128] = in_ref[rows, :].astype(F32)


def norms_kernel(c_ref, b_ref, a_ref, fa_ref, fb_ref, fc_ref, sa_ref, sb_ref, sc_ref, sh_ref):
    wide = sc_ref.shape[1]
    beta, gamma, slow, gamma_c, gamma_h = split(c_ref[...], (128, 128, wide, wide, wide))
    for out_ref, scale, shift in (
        (fc_ref, gamma, beta), (sc_ref, gamma_c, slow), (sh_ref, gamma_h, slow)
    ):
        out_ref[0:1, :] = scale
        out_ref[1:2, :] = shift
    for in_ref, fast_ref, slow_ref in ((b_ref, fb_ref, sb_ref), (a_ref, fa_ref, sa_ref)):
        width, cm = fast_ref.shape[1], slow_ref.shape[1]
        beta, gamma, slow, slow_gamma = split(in_ref[...], (128, 128, cm, cm))
        fast_ref[0:1, :] = fold_lanes(gamma, ALPHA)[:, :width]
        fast_ref[1:2, :] = fold_lanes(beta, ALPHA)[:, :width]
        slow_ref[0:1, :] = slow_gamma
        slow_ref[1:2, :] = slow


def per_device(
    fast_in,
    slow_in,
    clip_len,
    w_fast_a,
    w_fast_b,
    w_fast_c,
    w_lateral,
    w_slow_a,
    w_slow_b,
    w_slow_c,
    w_short,
    norm_fast_a,
    norm_fast_b,
    norm_fast_c,
    norm_slow_a,
    norm_slow_b,
    norm_slow_c,
    norm_short,
    cot_fast,
    cot_slow,
):
    batch, fast_frames, pixels, cf = fast_in.shape
    frames, cs = slow_in.shape[1], slow_in.shape[3]
    cells = batch * pixels
    ci = w_fast_a.shape[2]
    cl = w_lateral.shape[2]
    co = norm_slow_c.shape[1]
    cm = norm_slow_a.shape[1]
    cu = cs + cl
    mp = lax.axis_size("mp")
    me = lax.axis_index("mp")

    part, wide = w_slow_a.shape[2], w_short.shape[1]
    rows = frames * cells
    lane, fw = ALPHA * ci, ALPHA * cf
    small = 2 * lane + 2 * cm
    dp = lax.axis_size("dp")
    devices = dp * mp
    near_mesh = small_mesh()
    spot = np.arange(rows) % pixels
    edges = np.stack([spot >= W, spot < pixels - W, spot % W > 0, spot % W < W - 1])
    edges = jnp.asarray(np.repeat(edges.astype(np.float32)[:, :, None], 128, axis=2))
    buffers = [((rows + 2 * MARGIN, lane), F32), ((rows + 2 * MARGIN, cm), F32)]
    patches = [((rows, 9 * lane), BF), ((rows, 9 * cm), BF)]
    tile = ((8, 128), F32)

    def flat(values):
        return values.reshape(-1, values.shape[-1])

    def framed(values):
        return values.reshape(frames, cells, values.shape[-1])

    def by_pixel(values):
        return values.transpose(0, 2, 1, 3).reshape(cells, -1, values.shape[-1])

    def by_frame(values):
        return values.reshape(batch, pixels, -1, values.shape[-1]).transpose(0, 2, 1, 3)

    shards = jnp.swapaxes(w_slow_a, 1, 2), jnp.swapaxes(w_slow_b, 1, 2), w_slow_c, w_short
    if near_mesh:
        mine_a, mine_bc, mine_short = own_halves(*shards)
        line_a = line_pieces(mine_a)
        fast_in = held(fast_in, mine_a)
    mask, fast, tail, last, head, counts = local_call(
        unpack_kernel,
        [clip_len],
        [flat(by_pixel(fast_in))],
        [
            ((rows, 128), F32), ((frames, cells, fw), BF), ((cells, cf), BF), ((cells, cf), BF),
            ((cells, cf), BF), ((2,), F32),
        ],
        [((rows * ALPHA, cf), F32)],
        out_specs=[VMEM] * 5 + [SMEM],
    )
    if near_mesh:
        tail, last, head = held((tail, last, head), line_a[1])
    before = [shift_permute(values, "mp", 1) for values in (tail, last)]
    following = shift_permute(head, "mp", -1)
    if near_mesh:
        near_a = stacked(held(line_a, (before, following)))
    fast_stack, lateral_stack, fast_first, fast_sums, joined = local_call(
        entry_kernel,
        [],
        [
            mask, fast, *before, following, by_pixel(slow_in), w_fast_a.reshape(-1, ci),
            w_lateral.reshape(-1, cl),
        ],
        [
            ((frames, cells, 6 * cf), BF), ((frames, cells, 5 * cf), BF), ((rows, lane), F32),
            ((1, 2 * lane), F32), ((frames, cells, cu), BF),
        ],
        [((6 * cf, lane), BF), ((cs // 128, rows, 128), F32)],
    )

    if near_mesh:
        near_bc = stacked(held(line_pieces(held(mine_bc, near_a)), joined))
        line_short = line_pieces(held(mine_short, near_a))
        side_a = held(xor_permute(near_a, "mp", 1), (joined, near_bc))
        pieces_a = near_a, side_a, swap_cores(near_a), swap_cores(side_a)
        arrays = [joined, *pieces_a]
        placed = [((3 * cm, cu), BF)]
    else:
        wa, wb, wb_back, wc, ws = gather_whole(*shards)
        arrays = [joined, wa]
        placed = []
    *placed, base, to_right, to_left = local_call(
        placed_taps_kernel if near_mesh else taps_kernel,
        [],
        arrays,
        placed + [((rows, cm), F32), ((cells, cm), BF), ((cells, cm), BF)],
        [((cells, 3 * cm), F32)] * 2,
        early=(0,) if near_mesh else (),
    )
    if near_mesh:
        (wa,) = placed
    left = shift_permute(to_right, "mp", 1)
    right = shift_permute(to_left, "mp", -1)
    if near_mesh:
        pieces_bc = both_sides(near_bc)
        near_short = stacked(held(line_short, (left, right)))
    slow_first, vec = local_call(
        first_sums_kernel,
        [],
        [mask, base, left, right, fast_sums],
        [((rows, cm), F32), ((devices, 1, small), F32)],
    )
    if near_mesh:
        wb, wb_back, wc = place_call(
            place_bc, pieces_bc, [(cm, 9 * cm), (9 * cm, cm), (cm, 8 * wide)]
        )
        side_short = xor_permute(near_short, "mp", 1)
        sums = held(exchange(vec), (wb, side_short))
    else:
        sums = exchange(vec)

    wfb = w_fast_b.reshape(-1, ci)
    hidden_a, hidden_c, fast_second, slow_second, total_1, vec = local_call(
        conv_kernel,
        [counts],
        [sums, fast_first, slow_first, norm_fast_a, norm_slow_a, mask, edges, wfb, wb],
        [
            ((rows, lane), BF), ((rows, cm), BF), ((rows, lane), F32), ((rows, cm), F32),
            ((1, small), F32), ((devices, 1, small), F32),
        ],
        buffers + patches + [((9 * lane, lane), BF), tile],
    )

    if near_mesh:
        side_short = held(side_short, vec)
        pieces = near_short, side_short, swap_cores(near_short), swap_cores(side_short)
        ws, shortcut, short_vec = local_call(
            placed_short_kernel,
            [],
            [mask, flat(joined), *pieces],
            [((cu, co), BF), ((rows, co), BF), ((1, 2 * co), F32)],
            early=(0,),
        )
    else:
        shortcut, short_vec = local_call(
            short_kernel, [], [mask, flat(joined), ws], [((rows, co), BF), ((1, 2 * co), F32)]
        )
    sums = held(exchange(vec), short_vec)
    hidden_b, hidden_d, fast_third, slow_third, total_2, vec = local_call(
        expand_kernel,
        [counts],
        [sums, short_vec, fast_second, slow_second, norm_fast_b, norm_slow_b, mask, w_fast_c, wc],
        [
            ((rows, lane), BF), ((rows, cm), BF), ((rows, fw), F32), ((rows, co), BF),
            ((1, small), F32), ((dp, 1, 2 * cf + 4 * co), F32),
        ],
        [((rows, fw), F32), ((rows, co), F32), ((lane, fw), BF), tile],
    )
    slow_cots = held(cot_slow, vec).transpose(1, 0, 2, 3).reshape(frames, cells, co)
    slow_cots = flat(slow_cots)
    sums = lax.all_to_all(vec, "dp", 0, 0, tiled=True)
    (vec,) = quick_call(sum_kernel, [sums], [((mp, 1, vec.shape[2]), F32)])
    sums = lax.all_to_all(vec, "mp", 0, 0, tiled=True)

    fast_out, slow_out, fast_cot, slow_cot, total_3, vec = local_call(
        output_kernel,
        [counts],
        [
            sums, fast_third, slow_third, shortcut, fast, flat(by_pixel(cot_fast)),
            slow_cots, norm_fast_c, norm_slow_c, norm_short, mask,
        ],
        [
            ((rows * ALPHA, cf), BF), ((rows, co), BF), ((rows, fw), F32), ((rows, co), BF),
            ((1, 2 * cf + 4 * co), F32), ((devices, 1, 2 * cf + 3 * co), F32),
        ],
        [((rows * ALPHA, cf), F32)] * 2,
        late=(2, 3, 6),
        early=(0, 1, 2, 3),
    )
    slow_out = framed(slow_out).reshape(frames, batch, pixels, co).transpose(1, 0, 2, 3)
    sums = held(exchange(vec), slow_out)

    d_fast_third, d_slow_third, d_short, grad_fb, grad_sb, total_4, vec = local_call(
        narrow_kernel,
        [counts],
        [
            sums, total_3, total_2, fast_cot, slow_cot, fast_third, slow_third, shortcut,
            fast_second, slow_second, norm_fast_c, norm_slow_c, norm_short, norm_fast_b, norm_slow_b,
            mask, w_fast_c, wc,
        ],
        [
            ((rows, fw), BF), ((rows, co), BF), ((rows, co), BF), ((rows, lane), F32),
            ((rows, cm), F32), ((1, 2 * cf + 3 * co), F32), ((devices, 1, small), F32),
        ],
        [((lane, fw), BF), tile],
        late=(4, 6, 7, 8, 9, 17),
        early=(0, 1, 2),
    )

    def weight_grad(kernel, arrays, size, length, total, scratch=()):
        halves = ((mp, size, length), BF)
        return local_call(kernel, [], arrays, [halves, halves], [((total, length), BF), *scratch])

    if near_mesh:
        raw_cs = weight_grad(
            grad_cs_kernel, [d_short, d_slow_third, flat(joined), hidden_d], wide // 2, cu + cm, co
        )
        sums, raw_cs = lax.optimization_barrier((exchange(vec), raw_cs))
        sent_cs = swap_cores(raw_cs[0])
    else:
        raw_cs = jnp.concatenate(
            [rows_dot(framed(d_short), joined), rows_dot(framed(d_slow_third), framed(hidden_d))], -1
        )
        sum_cs = reduce_whole(raw_cs.reshape(mp, 2, wide // 2, cu + cm)).reshape(wide, cu + cm)
        sums = exchange(vec)

    d_fast_second, d_slow_second, grad_fa, grad_sa, total_5, vec = local_call(
        conv_back_kernel,
        [counts],
        [
            sums, total_2, total_1, grad_fb, grad_sb, fast_second, slow_second, fast_first,
            slow_first, norm_fast_b, norm_slow_b, norm_fast_a, norm_slow_a, mask, edges, wfb, wb_back,
        ],
        [
            ((rows, lane), BF), ((rows, cm), BF), ((rows, lane), F32), ((rows, cm), F32),
            ((1, small), F32), ((devices, 1, small), F32),
        ],
        buffers + patches + [((9 * lane, lane), BF), tile],
    )
    grad_b_scratch = [buffers[1], patches[1]]
    if near_mesh:
        raw_b = weight_grad(
            grad_b_kernel, [d_slow_second, hidden_c, edges], part // 2, 9 * cm, cm, grad_b_scratch
        )
        sums, raw_b = lax.optimization_barrier((exchange(vec), raw_b))
        sent_b = swap_cores(raw_b[0])
    else:
        (raw_b,) = local_call(
            grad_b_whole_kernel,
            [],
            [d_slow_second, hidden_c, edges],
            [((cm, 9 * cm), F32)],
            grad_b_scratch,
        )
        sum_b = reduce_whole(raw_b.reshape(mp, 2, part // 2, 9 * cm)).reshape(part, 9, cm)
        sums = exchange(vec)
    d_fast_0, d_fast_1, d_slow_0, d_slow_1, total_6 = local_call(
        first_kernel,
        [counts],
        [sums, total_1, grad_fa, grad_sa, fast_first, slow_first, norm_fast_a, norm_slow_a, mask],
        [((cells, lane), BF)] * 2 + [((cells, cm), BF)] * 2 + [((1, small), F32)],
        [tile],
    )
    slow_parts = [
        d_slow_0, d_slow_1, shift_permute(d_slow_1, "mp", 1), shift_permute(d_slow_0, "mp", -1)
    ]
    (fast_inner,) = local_call(
        fast_inner_kernel,
        [],
        [held(hidden_a, d_slow_0), d_fast_second, hidden_b, d_fast_third, edges],
        [((9 * ci // ALPHA + 8 + ci, 128), BF)],
        [buffers[0], patches[0]],
    )
    if near_mesh:
        far_1, near_1 = merge((raw_cs[1], held(raw_b[1], d_slow_0)), (sent_cs, sent_b))
        raw_a = weight_grad(
            grad_a_kernel, held(slow_parts, (far_1, fast_inner)) + [joined], 3 * part // 2, cu, 3 * cm
        )
        sent_a = swap_cores(raw_a[0])
        slow_parts = held(slow_parts, raw_a)
    else:
        three = jnp.stack(
            [
                jnp.concatenate([d_slow_1, slow_parts[3]]),
                jnp.concatenate([d_slow_0, d_slow_1]),
                jnp.concatenate([slow_parts[2][:, :cm], d_slow_0]),
            ]
        )
        raw_a = jnp.einsum("kro,rc->koc", three, flat(joined), preferred_element_type=F32)
        raw_a = raw_a.reshape(3, mp, 2, part // 2, cu).transpose(1, 2, 0, 3, 4)
        sum_a = reduce_whole(raw_a.reshape(mp, 2, 3 * part // 2, cu))
        sum_a = sum_a.reshape(2, 3, part // 2, cu).transpose(1, 0, 2, 3).reshape(3, part, cu)
    d_lateral, lateral_edge = lateral_back(
        [mask, *slow_parts, d_fast_0, framed(d_short), wa, ws],
        [((frames, cells, cl), BF), ((cells, cl + lane), BF)],
    )
    lateral_after = shift_permute(lateral_edge, "mp", -1)
    fast_before = shift_permute(held(d_fast_1, d_lateral), "mp", 1)
    fast_outer = [fast_stack, d_fast_0, d_fast_1, lateral_stack, d_lateral, fast_inner]
    if near_mesh:
        half_fast = ((8, 16, FAST_ROWS // 2), BF)
        fast_send, fast_keep = local_call(
            fast_outer_kernel, [], fast_outer, [half_fast] * 2, [((FAST_ROWS, 128), BF)]
        )
        turned_1 = turn(far_1, near_1)
        keeps = raw_a[1], held(fast_keep, turned_1)
        far_2, near_2 = merge(keeps, (sent_a, swap_cores(fast_send)))
        slow_parts = held(slow_parts, far_2)
    else:
        (raw_fast,) = local_call(outer_rows, [], fast_outer, [((FAST_ROWS, 128), F32)])
        raw_fast = lax.psum(raw_fast, ("dp", "mp"))
    (grad_slow_in,) = local_call(
        joined_back_kernel,
        [],
        [mask, *slow_parts, framed(d_short), wa, ws],
        [((cells, frames, cs), BF)],
    )
    norms = local_call(
        norms_kernel,
        [],
        [total_4, total_5, total_6],
        [((2, width), F32) for width in (ci, ci, cf, cm, cm, co, co)],
        limit=SMALL,
    )
    if near_mesh:
        pieces_1 = cut_lines(turned_1[0], held(turned_1[1], grad_slow_in))
        sent_1 = over_z(pieces_1)
        pieces_2 = cut_lines(*turn(far_2, held(near_2, pieces_1)))
        sent_2 = over_z(pieces_2)
        (total_1,) = along_line(held(pieces_1[0], pieces_2), sent_1, pieces_1[0].shape[1])
        sum_c, sum_s, sum_b = cross_clips(
            clips_kernel,
            total_1,
            [(cm, wide), (cu, wide), (9, part, cm)],
            [((wide, cu + cm), F32)],
            norms,
        )
        mine = held(pieces_2[0], (lateral_after, fast_before, sum_c))
        total, raw_fast = along_line(mine, sent_2, mine.shape[1] - FAST_ROWS // 4)
        raw_fast = lax.all_to_all(raw_fast, ("dp", "mp"), 0, 0, tiled=True)
        d_lateral = held(d_lateral, total)
    (grad_fast_in,) = local_call(
        fast_back_kernel,
        [],
        [
            mask, d_fast_0, d_fast_1, fast_before, lateral_after, d_lateral, fast_cot,
            w_lateral.reshape(-1, cl), w_fast_a.reshape(-1, ci),
        ],
        [((rows * ALPHA, cf), BF)],
        [((rows * ALPHA, cf), F32), ((3 * lane, fw), BF)],
    )
    if near_mesh:
        (sum_a,) = cross_clips(clips_a_kernel, total, [(3, part, cu)], [], grad_fast_in)
    else:
        sum_c, sum_s = sum_cs[:, cu:].T, sum_cs[:, :cu].T
        sum_b = sum_b.transpose(1, 0, 2)
    if near_mesh:
        raw_fast = held(raw_fast, sum_a)
    fast_a, fast_b, fast_c, grad_lateral = local_call(
        fast_results_kernel,
        [],
        [raw_fast],
        [((3, cf, ci), F32), ((9, ci, ci), F32), ((ci, cf), F32), ((5, cf, cl), F32)],
        [((FAST_ROWS, 128), BF), ((3 * cf, 128), F32)],
        limit=SMALL,
    )
    return (
        by_frame(fast_out.reshape(cells, fast_frames, cf)),
        slow_out,
        by_frame(grad_fast_in.reshape(cells, fast_frames, cf)),
        by_frame(grad_slow_in),
        fast_a,
        fast_b,
        fast_c,
        grad_lateral,
        jnp.swapaxes(sum_a, 1, 2),
        jnp.swapaxes(sum_b, 1, 2),
        sum_c,
        sum_s,
        *norms,
    )


def solution(mesh):
    frames = P("dp", "mp", None, None)
    last = P(None, None, "mp")
    wide = P(None, "mp")
    return jax.shard_map(
        per_device,
        mesh=mesh,
        in_specs=(frames, frames, P(), P(), P(), P(), P(), last, last, wide, wide)
        + (P(),) * 7
        + (frames, frames),
        out_specs=(frames,) * 4 + (P(),) * 4 + (last, last, wide, wide) + (P(),) * 7,
        check_vma=False,
    )
```
